256 devices in a mesh: ctx: 32 (over z, x_lo, core), head: 8 (over x_hi, y).
Axes of the slice: x: 4 (x_hi: 2, x_lo: 2; x = x_hi * 2 + x_lo), y: 4, z: 8, core: 2. Of those that a mesh axis runs over, the one named last changes fastest.
Arguments:
- queries: bfloat16 [128, 128, 192], P('ctx', 'head'), may hold values from -200 to 200
- out_grad: bfloat16 [128, 128, 128], P('ctx', 'head'), may hold values from -6 to 6
- kv_up: bfloat16 [128, 512, 256], P('head'), may hold values from -0.25 to 0.25
- latent_cache: bfloat16 [32768, 576], P('ctx'), may hold values from -12 to 12
- token_ratio: float32 [128], P('ctx'), may hold values from -4 to 4
- pair_lens: int32 [4], replicated, may hold values from 1 to 64, 128 in all
- prompt_len: int32 [1], replicated, may hold values from 16384 to 32768
Outputs:
- query_grad: bfloat16 [128, 128, 192], P('ctx', 'head')
- cache_grad: bfloat16 [32768, 576], P(('ctx', 'head'))
The draws below stay inside these ranges and needn't reach their ends.
All inputs are finite; a program needn't handle non-finite values.
Results may differ from the reference program's by a relative error of at most 0.029.
Values may be sent and summed in bfloat16 or wider, within the bound.
No kernel may reach another device: no remote copies, remote signals or barrier semaphores. Data moves between devices by JAX's collectives and lax.ppermute only.
A program may use at most 128 MiB of HBM per device.

```python
import math
import jax
import jax.numpy as jnp
import numpy as np
from jax import lax

D_LAT = 512
D_ROPE = 64
D_NOPE = 128
D_V = 128
CD = 576
QD = 192
HEADS = 128
PROMPT = 32768
QTOT = 128
NSEG = 4
MOST = 64


def draw_latent_cache(key, part):
    key = jax.random.fold_in(key, 1)
    base = jax.random.normal(key, (PROMPT, CD), jnp.float32)
    result = base
    return jnp.clip(result, -12.0, 12.0).astype(jnp.bfloat16)


def draw_queries(key, part):
    key = jax.random.fold_in(key, 2)
    base = jax.random.normal(key, (QTOT, HEADS, QD), jnp.float32)
    result = base
    return jnp.clip(result, -200.0, 200.0).astype(jnp.bfloat16)


def draw_token_ratio(key, part):
    key = jax.random.fold_in(key, 3)
    rising = 1.0 + 2.0 * jnp.arange(QTOT, dtype=jnp.float32) / max(QTOT - 1, 1)
    values = 0.4 * jax.random.normal(key, (QTOT,), jnp.float32) * rising
    return jnp.clip(values, -4.0, 4.0)


def steps_of(stream_key, shape, shards, smallest, high):
    def one(axis_at, parts):
        steps = jax.random.uniform(jax.random.fold_in(jax.random.fold_in(stream_key, 6), axis_at), (parts,), jnp.float32, smallest / len(shards), high / len(shards))
        return jnp.repeat(jnp.exp(steps), shape[axis_at] // parts).reshape((-1,) + (1,) * (len(shape) - axis_at - 1))

    loudness = one(*shards[0])
    for cut in shards[1:]:
        loudness = loudness * one(*cut)
    return loudness


def split_up(amount, total, bound, slope):
    portions = [(1 << 20) // math.isqrt(rank ** slope) + 1 for rank in range(2, amount + 1)]
    spare, given = total - bound - (amount - 1), [1] * (amount - 1)
    while spare > 0:
        movable = [i for i in range(amount - 1) if given[i] < bound]
        whole, left = sum([portions[i] for i in movable]), spare
        for i in movable:
            more = min(bound - given[i], max(1, left * portions[i] // whole), spare)
            given[i] = given[i] + more
            spare = spare - more
    return np.array([bound] + given)


def ragged(key, amount, total, reach, slope):
    if amount == 2:
        one = jax.random.randint(key, (), max(1, total - reach), min(reach, total - 1) + 1)
        return jnp.stack([one, total - one])
    lengths = jnp.asarray(split_up(amount, total, reach, slope), jnp.int32)
    pairs = (amount - 1) // 2
    donor, taker = lengths[1:1 + 2 * pairs:2], lengths[2:2 + 2 * pairs:2]
    slack = jnp.minimum(donor - 1, reach - taker)
    moved = jax.random.randint(jax.random.fold_in(key, 1), (pairs,), 0, 1 << 20) % (slack + 1)
    lengths = lengths.at[1:1 + 2 * pairs:2].set(donor - moved).at[2:2 + 2 * pairs:2].set(taker + moved)
    return lengths[jax.random.permutation(jax.random.fold_in(key, 2), amount)]


def centred(stream_key, shape, scale, most, split=(), kind=jnp.bfloat16):
    array = jax.random.normal(stream_key, shape, jnp.float32) * scale
    if len(split) > 0:
        array = steps_of(stream_key, shape, split, -0.22, 0.18) * array
    return jnp.clip(array, min=-most, max=most).astype(kind)


def setup_inputs(seed: int = 0) -> dict:
    splits = jax.random.split(jax.random.key(seed), 8)
    return {
        "queries": draw_queries(jax.random.fold_in(splits[7], 71), 0),
        "out_grad": centred(splits[1], (QTOT, HEADS, D_V), 1.0, 6.0, ((0, 32), (1, 8))),
        "kv_up": centred(splits[2], (HEADS, D_LAT, D_NOPE + D_V), D_LAT ** -0.5, 0.25, ((0, 8),)),
        "latent_cache": draw_latent_cache(jax.random.fold_in(splits[7], 71), 0),
        "token_ratio": draw_token_ratio(jax.random.fold_in(splits[7], 71), 0),
        "pair_lens": ragged(splits[5], NSEG, QTOT, MOST, 1).astype(jnp.int32),
        "prompt_len": jax.random.randint(splits[6], (1,), PROMPT // 2, PROMPT + 1).astype(jnp.int32),
    }


BETA = 0.1
LOSS_SCALE = 2048.0


def segment_table(rows, pair_lens):
    bounds = jnp.cumsum(pair_lens)
    segment = jnp.sum((rows[:, None] >= bounds[None, :]).astype(jnp.int32), axis=1)
    labels = jnp.arange(pair_lens.shape[0], dtype=jnp.int32)
    return (segment[:, None] == labels[None, :]).astype(jnp.float32)


def pair_gains(ratios):
    margin = BETA * (ratios[0::2] - ratios[1::2])
    weight = LOSS_SCALE * BETA * jax.nn.sigmoid(-margin)
    return jnp.stack([-weight, weight], axis=1).reshape(-1)


def reference(queries, out_grad, kv_up, latent_cache, token_ratio, pair_lens, prompt_len):
    rows = jnp.arange(QTOT, dtype=jnp.int32)
    table = segment_table(rows, pair_lens)
    ratios = jnp.sum(table * token_ratio[:, None], axis=0)
    gains = jnp.sum(table * pair_gains(ratios)[None, :], axis=1)
    valid = jnp.arange(PROMPT, dtype=jnp.int32) < prompt_len[0]
    scale = QD ** -0.5
    latent = latent_cache[:, :D_LAT]

    def per_head(carry, inputs):
        query_h, grad_h, weight_h = inputs
        w_key = weight_h[:, :D_NOPE]
        w_val = weight_h[:, D_NOPE:]
        q_lat = jnp.dot(query_h[:, :D_NOPE], w_key.T, preferred_element_type=jnp.float32).astype(jnp.bfloat16)
        full_query = jnp.concatenate([q_lat, query_h[:, D_NOPE:]], axis=1)
        grad_lat = jnp.dot(grad_h, w_val.T, preferred_element_type=jnp.float32).astype(jnp.bfloat16)
        scores = scale * jnp.dot(full_query, latent_cache.T, preferred_element_type=jnp.float32)
        masked = jnp.where(valid[None, :], scores, -1e30)
        top = jnp.max(masked, axis=1, keepdims=True)
        mass = jnp.sum(jnp.where(valid[None, :], jnp.exp(scores - top), 0.0), axis=1, keepdims=True)
        lse = top + jnp.log(mass)
        prob = jnp.where(valid[None, :], jnp.exp(scores - lse), 0.0)
        dprod = gains[:, None] * jnp.dot(grad_lat, latent.T, preferred_element_type=jnp.float32)
        delta = jnp.sum(prob * dprod, axis=1, keepdims=True)
        dscore = (prob * (dprod - delta)).astype(jnp.bfloat16)
        gain_prob = (gains[:, None] * prob).astype(jnp.bfloat16)
        dq_full = scale * jnp.dot(dscore, latent_cache, preferred_element_type=jnp.float32)
        dq_nope = jnp.dot(dq_full[:, :D_LAT], w_key.astype(jnp.float32), precision=lax.Precision.HIGHEST)
        dq_head = jnp.concatenate([dq_nope, dq_full[:, D_LAT:]], axis=1)
        dkey = scale * jnp.dot(dscore.T, full_query, preferred_element_type=jnp.float32)
        dval = jnp.dot(gain_prob.T, grad_lat, preferred_element_type=jnp.float32)
        cache_head = dkey + jnp.pad(dval, ((0, 0), (0, D_ROPE)))
        return carry + cache_head, dq_head

    start = jnp.zeros((PROMPT, CD), jnp.float32)
    inputs = (jnp.swapaxes(queries, 0, 1), jnp.swapaxes(out_grad, 0, 1), kv_up)
    cache_sum, dq_stack = lax.scan(per_head, start, inputs)
    query_grad = jnp.swapaxes(dq_stack, 0, 1).astype(jnp.bfloat16)
    return query_grad, cache_sum.astype(jnp.bfloat16)
```

```python
import jax
import jax.numpy as jnp
from jax import lax
from jax.sharding import PartitionSpec as P

BETA = 0.1
LOSS_SCALE = 2048.0
LOG2E = 1.4426950408889634
NEVER = -1e30
FLOOR = -1e29
F32 = jnp.float32
BF16 = jnp.bfloat16


def segment_table(rows, pair_lens):
    bounds = jnp.cumsum(pair_lens)
    segment = jnp.sum((rows[:, None] >= bounds[None, :]).astype(jnp.int32), axis=1)
    labels = jnp.arange(pair_lens.shape[0], dtype=jnp.int32)
    return (segment[:, None] == labels[None, :]).astype(F32)


def pair_gains(ratios):
    margin = BETA * (ratios[0::2] - ratios[1::2])
    weight = LOSS_SCALE * BETA * jax.nn.sigmoid(-margin)
    return jnp.stack([-weight, weight], axis=1).reshape(-1)


def row_gains(token_ratio, pair_lens):
    table = segment_table(jnp.arange(token_ratio.shape[0], dtype=jnp.int32), pair_lens)
    ratios = jnp.sum(table * token_ratio[:, None], axis=0)
    return jnp.sum(table * pair_gains(ratios)[None, :], axis=1)


def permute(x, axis, to):
    return lax.ppermute(x, axis, [(i, to(i)) for i in range(lax.axis_size(axis))])


def in_order(mine, theirs, second, axis):
    return jnp.where(
        second,
        jnp.concatenate([theirs, mine], axis),
        jnp.concatenate([mine, theirs], axis),
    )


def pick(x, index, axis):
    return lax.dynamic_index_in_dim(x, index, axis, keepdims=False)


def join_stats(parts):
    top = jnp.max(parts[:, 0], axis=0)
    factor = jnp.exp2(parts[:, 0] - top[None])
    return jnp.stack(
        [top, jnp.sum(factor * parts[:, 1], axis=0), jnp.sum(factor * parts[:, 2], axis=0)]
    )


def per_device(queries, out_grad, kv_up, latent_cache, token_ratio, pair_lens, prompt_len):
    ctx_index = lax.axis_index("ctx")
    head_index = lax.axis_index("head")
    core = ctx_index % 2
    x_lo = (ctx_index // 2) % 2
    z = ctx_index // 4
    nz = lax.axis_size("ctx") // 4
    ny = 4
    y = head_index % ny
    x_hi = head_index // ny
    other_core = lambda i: i ^ 1
    other_x_lo = lambda i: i ^ 2
    z_groups = [[4 * k + j for k in range(nz)] for j in range(4)]

    q_dev, heads, q_width = queries.shape
    p_dev, c_width = latent_cache.shape
    d_lat = kv_up.shape[1]
    d_rope = c_width - d_lat
    d_nope = q_width - d_rope
    half = heads // 2
    rows = q_dev * 4 * nz
    scale = q_width ** (-0.5)

    other_cache = permute(latent_cache, "ctx", other_core)

    high = lax.reduce_precision(token_ratio, 8, 7)
    middle = lax.reduce_precision(token_ratio - high, 8, 7)
    low = token_ratio - high - middle
    terms = jnp.stack([high, middle, low], axis=1).astype(BF16)
    terms = jnp.broadcast_to(terms[:, None, :], (q_dev, heads, 3))
    own = jnp.concatenate([queries, out_grad, terms], axis=2)
    own = jnp.transpose(own, (1, 0, 2)).reshape(2, half, q_dev, -1)
    block = in_order(
        pick(own, core, 0), permute(pick(own, 1 - core, 0), "ctx", other_core), core == 1, 1
    )
    block = in_order(block, permute(block, "ctx", other_x_lo), x_lo == 1, 1)
    up = down = block
    ring = [block] + [None] * (nz - 1)
    for k in range(1, nz // 2 + 1):
        up = permute(up, "ctx", lambda i: (i + 4) % (4 * nz))
        ring[nz - k] = up
        if k < nz // 2:
            down = permute(down, "ctx", lambda i: (i - 4) % (4 * nz))
            ring[k] = down
    ring = jnp.stack(ring, axis=1)
    ring = jnp.concatenate([ring, ring], axis=1)
    everything = lax.dynamic_slice_in_dim(ring, (nz - z) % nz, nz, 1)
    everything = everything.reshape(half, rows, -1)
    raw_q = everything[:, :, :d_nope]
    rope_q = everything[:, :, d_nope:q_width]
    raw_g = everything[:, :, q_width : q_width + out_grad.shape[2]]
    ratio = jnp.sum(everything[0, :, -3:].astype(F32), axis=1)
    gains = row_gains(ratio, pair_lens)

    weights = lax.dynamic_slice_in_dim(kv_up, core * half, half, 0)
    w_key = weights[:, :, :d_nope]
    w_val = weights[:, :, d_nope:]
    q_lat = jnp.einsum("hin,hln->hil", raw_q, w_key, preferred_element_type=F32).astype(BF16)
    full_query = jnp.concatenate([q_lat, rope_q], axis=2).reshape(half * rows, c_width)
    grad_lat = jnp.einsum("hiv,hlv->hil", raw_g, w_val, preferred_element_type=F32).astype(BF16)
    grad_lat = grad_lat.reshape(half * rows, d_lat)

    cache = jnp.concatenate([latent_cache, other_cache], axis=0)
    key = jnp.arange(p_dev, dtype=jnp.int32)
    key = jnp.concatenate([ctx_index * p_dev + key, (ctx_index ^ 1) * p_dev + key])
    valid = (key < prompt_len[0])[:, None]
    scores = jnp.einsum("kc,rc->kr", cache, full_query, preferred_element_type=F32)
    scores = jnp.where(valid, scores * (scale * LOG2E), NEVER)
    dprod = jnp.einsum("kl,rl->kr", cache[:, :d_lat], grad_lat, preferred_element_type=F32)
    top = jnp.maximum(jnp.max(scores, axis=0), FLOOR)
    expo = jnp.exp2(scores - top[None])
    mass = jnp.sum(expo, axis=0)
    dsum = jnp.sum(expo * dprod, axis=0)
    centre = dsum / jnp.maximum(mass, 1e-30)
    spread = (expo * (dprod - centre[None])).astype(BF16)
    expo = expo.astype(BF16)

    stats = jnp.stack([top, mass, dsum])
    pair = permute(stats, "ctx", other_x_lo)

    def query_terms(x):
        full = jnp.einsum("kr,kc->rc", x, cache, preferred_element_type=F32)
        full = full.reshape(half, rows, c_width)
        nope = jnp.einsum(
            "hil,hln->hin", full[:, :, :d_lat].astype(BF16), w_key, preferred_element_type=F32
        )
        return jnp.concatenate([nope, full[:, :, d_lat:]], axis=2)

    query_spread = query_terms(spread)
    query_expo = query_terms(expo)

    joined = join_stats(jnp.stack([stats, pair]))
    joined = lax.all_to_all(
        jnp.broadcast_to(joined[None], (nz,) + joined.shape),
        "ctx",
        0,
        0,
        axis_index_groups=z_groups,
    )
    joined = join_stats(joined)
    factor = jnp.tile(gains, half) * jnp.exp2(top - joined[0]) / joined[1]
    shift = joined[2] / joined[1] - centre

    factor3 = factor.reshape(half, rows, 1)
    shift3 = shift.reshape(half, rows, 1)
    dq = ((scale * factor3) * (query_spread - shift3 * query_expo)).astype(BF16)
    dq = dq.reshape(half, nz, 2, 2 * q_dev, q_width)
    from_pair = permute(pick(dq, 1 - x_lo, 2), "ctx", other_x_lo)
    dq = (pick(dq, x_lo, 2).astype(F32) + from_pair.astype(F32)).astype(BF16)

    scaled_query = scale * factor[:, None] * full_query.astype(F32)
    with_spread = scaled_query.astype(BF16)
    with_expo = factor[:, None] * jnp.pad(grad_lat.astype(F32), ((0, 0), (0, d_rope)))
    with_expo = (with_expo - shift[:, None] * scaled_query).astype(BF16)

    def cache_terms(part):
        return jnp.dot(spread[part], with_spread, preferred_element_type=F32) + jnp.dot(
            expo[part], with_expo, preferred_element_type=F32
        )

    for_other = cache_terms(slice(p_dev, 2 * p_dev)).astype(BF16)
    from_other = permute(for_other, "ctx", other_core)
    cache_grad = (cache_terms(slice(0, p_dev)) + from_other.astype(F32)).astype(BF16)
    cache_grad = cache_grad.reshape(2, ny, p_dev // (2 * ny), c_width)
    arrived = [
        permute(
            pick(cache_grad, (y + k) % ny, 1),
            "head",
            lambda i, k=k: (i // ny) * ny + (i + k) % ny,
        )
        for k in range(1, ny)
    ]

    dq = lax.all_to_all(dq, "ctx", 1, 1, axis_index_groups=z_groups)
    dq = jnp.sum(dq.astype(F32), axis=1).reshape(half, 2, q_dev, q_width).astype(BF16)
    dq_mine = pick(dq, core, 1)
    dq_theirs = permute(pick(dq, 1 - core, 1), "ctx", other_core)
    query_grad = jnp.transpose(in_order(dq_mine, dq_theirs, core == 1, 0), (1, 0, 2))

    total = pick(cache_grad, y, 1).astype(F32)
    for part in arrived:
        total = total + part.astype(F32)
    across = permute(
        pick(total, 1 - x_hi, 0).astype(BF16), "head", lambda i: (i + ny) % (2 * ny)
    )
    cache_grad = (pick(total, x_hi, 0) + across.astype(F32)).astype(BF16)
    return (query_grad, cache_grad)


def solution(mesh):
    placed = (
        P("ctx", "head", None),
        P("ctx", "head", None),
        P("head", None, None),
        P("ctx", None),
        P("ctx"),
        P(),
        P(),
    )
    return jax.shard_map(
        per_device,
        mesh=mesh,
        in_specs=placed,
        out_specs=(P("ctx", "head", None), P(("ctx", "head"), None)),
        check_vma=False,
    )
```

```python
import functools

import jax
import jax.numpy as jnp
from jax import lax
from jax.experimental import pallas as pl
from jax.experimental.pallas import tpu as pltpu
from jax.sharding import PartitionSpec as P

BETA = 0.1
LOSS_SCALE = 2048.0
LOG2E = 1.4426950408889634
NEVER = -1e30
FLOOR = -1e29
F32 = jnp.float32
BF16 = jnp.bfloat16
CHUNK = 128
VMEM_BYTES = 40 * 1024 * 1024


def segment_table(rows, pair_lens):
    bounds = jnp.cumsum(pair_lens)
    segment = jnp.sum((rows[:, None] >= bounds[None, :]).astype(jnp.int32), axis=1)
    labels = jnp.arange(pair_lens.shape[0], dtype=jnp.int32)
    return (segment[:, None] == labels[None, :]).astype(F32)


def pair_gains(ratios):
    margin = BETA * (ratios[0::2] - ratios[1::2])
    weight = LOSS_SCALE * BETA * jax.nn.sigmoid(-margin)
    return jnp.stack([-weight, weight], axis=1).reshape(-1)


def row_gains(token_ratio, pair_lens):
    table = segment_table(jnp.arange(token_ratio.shape[0], dtype=jnp.int32), pair_lens)
    ratios = jnp.sum(table * token_ratio[:, None], axis=0)
    return jnp.sum(table * pair_gains(ratios)[None, :], axis=1)


def permute(x, axis, to):
    return lax.ppermute(x, axis, [(i, to(i)) for i in range(lax.axis_size(axis))])


def in_order(mine, theirs, second, axis):
    return jnp.where(
        second,
        jnp.concatenate([theirs, mine], axis),
        jnp.concatenate([mine, theirs], axis),
    )


def pick(x, index, axis):
    return lax.dynamic_index_in_dim(x, index, axis, keepdims=False)


def join_stats(first, second):
    top = jnp.maximum(first[0], second[0])
    one = jnp.exp2(first[0] - top)
    two = jnp.exp2(second[0] - top)
    return jnp.stack([top, one * first[1] + two * second[1], one * first[2] + two * second[2]])


def against(x, y):
    return lax.dot_general(x, y, (((1,), (1,)), ((), ())), preferred_element_type=F32)


def attend_kernel(
    score_scale,
    where_ref,
    rows_ref,
    kv_ref,
    own_ref,
    other_ref,
    query_ref,
    grad_ref,
    expo_ref,
    spread_ref,
    stats_ref,
    scores,
    dprod,
):
    rows, d_nope = rows_ref.shape[1], kv_ref.shape[2] // 2
    d_lat = kv_ref.shape[1]
    d_rope = query_ref.shape[1] - d_lat
    keys = own_ref.shape[0]
    width = query_ref.shape[0]
    for j in range(rows_ref.shape[0]):
        at = slice(j * rows, (j + 1) * rows)
        lat = against(rows_ref[j, :, :d_nope], kv_ref[j, :, :d_nope])
        query_ref[at, :d_lat] = lat.astype(BF16)
        query_ref[at, d_lat:] = rows_ref[j, :, 2 * d_nope : 2 * d_nope + d_rope]
        lat = against(rows_ref[j, :, d_nope : 2 * d_nope], kv_ref[j, :, d_nope:])
        grad_ref[at, :] = lat.astype(BF16)
    scores[:keys] = against(own_ref[...], query_ref[...])
    scores[keys:] = against(other_ref[...], query_ref[...])
    dprod[:keys] = against(own_ref[:, :d_lat], grad_ref[...])
    dprod[keys:] = against(other_ref[:, :d_lat], grad_ref[...])
    steps = 2 * keys // CHUNK

    def fold(x, join):
        return join(x.reshape(CHUNK // 8, 8, width), axis=0)

    def highest(i, top):
        at = pl.ds(pl.multiple_of(i * CHUNK, CHUNK), CHUNK)
        first = jnp.where(i * CHUNK < keys, where_ref[1], where_ref[2] - keys) + i * CHUNK
        key = first + lax.broadcasted_iota(jnp.int32, (CHUNK, width), 0)
        value = jnp.where(key < where_ref[3], scores[at, :] * score_scale, NEVER)
        scores[at, :] = value
        return jnp.maximum(top, fold(value, jnp.max))

    top = lax.fori_loop(0, steps, highest, jnp.full((8, width), FLOOR, F32), unroll=2)
    top = jnp.max(top, axis=0, keepdims=True)

    def sums(i, so_far):
        at = pl.ds(pl.multiple_of(i * CHUNK, CHUNK), CHUNK)
        value = jnp.exp2(scores[at, :] - top)
        scores[at, :] = value
        expo_ref[at, :] = value.astype(BF16)
        return (
            so_far[0] + fold(value, jnp.sum),
            so_far[1] + fold(value * dprod[at, :], jnp.sum),
        )

    zero = jnp.zeros((8, width), F32)
    mass, dsum = lax.fori_loop(0, steps, sums, (zero, zero), unroll=2)
    mass = jnp.sum(mass, axis=0, keepdims=True)
    dsum = jnp.sum(dsum, axis=0, keepdims=True)
    centre = dsum / jnp.maximum(mass, 1e-30)

    def spreads(i, carry):
        at = pl.ds(pl.multiple_of(i * CHUNK, CHUNK), CHUNK)
        spread_ref[at, :] = (scores[at, :] * (dprod[at, :] - centre)).astype(BF16)
        return carry

    lax.fori_loop(0, steps, spreads, 0, unroll=2)
    stats_ref[0:1] = top
    stats_ref[1:2] = mass
    stats_ref[2:3] = dsum


def attend(where, everything, kv_up, own, other, score_scale):
    half, rows, packed = everything.shape
    d_lat = kv_up.shape[1]
    keys, c_width = own.shape
    total = half * rows
    width = 2 * rows
    whole = lambda p, w: (0, 0)
    column = lambda p, w: (0, p)
    return pl.pallas_call(
        functools.partial(attend_kernel, score_scale),
        out_shape=(
            jax.ShapeDtypeStruct((total, c_width), BF16),
            jax.ShapeDtypeStruct((total, d_lat), BF16),
            jax.ShapeDtypeStruct((2 * keys, total), BF16),
            jax.ShapeDtypeStruct((2 * keys, total), BF16),
            jax.ShapeDtypeStruct((3, total), F32),
        ),
        grid_spec=pltpu.PrefetchScalarGridSpec(
            num_scalar_prefetch=1,
            grid=(half // 2,),
            in_specs=[
                pl.BlockSpec((2, rows, packed), lambda p, w: (p, 0, 0)),
                pl.BlockSpec((2,) + kv_up.shape[1:], lambda p, w: (w[0] * (half // 2) + p, 0, 0)),
                pl.BlockSpec((keys, c_width), whole),
                pl.BlockSpec((keys, c_width), whole),
            ],
            out_specs=[
                pl.BlockSpec((width, c_width), lambda p, w: (p, 0)),
                pl.BlockSpec((width, d_lat), lambda p, w: (p, 0)),
                pl.BlockSpec((2 * keys, width), column),
                pl.BlockSpec((2 * keys, width), column),
                pl.BlockSpec((3, width), column),
            ],
            scratch_shapes=[
                pltpu.VMEM((2 * keys, width), F32),
                pltpu.VMEM((2 * keys, width), F32),
            ],
        ),
        compiler_params=pltpu.CompilerParams(vmem_limit_bytes=VMEM_BYTES),
        cost_estimate=pl.CostEstimate(
            flops=2 * 2 * keys * total * (c_width + d_lat),
            bytes_accessed=8 * keys * total,
            transcendentals=2 * keys * total,
        ),
    )(where, everything, kv_up, own, other)


def project_kernel(where_ref, cache_ref, spread_ref, expo_ref, kv_ref, by_spread_ref, by_expo_ref):
    d_lat = kv_ref.shape[1]
    d_nope = kv_ref.shape[2] // 2
    rows = spread_ref.shape[1] // kv_ref.shape[0]
    for terms_ref, out_ref in ((spread_ref, by_spread_ref), (expo_ref, by_expo_ref)):
        full = jnp.dot(cache_ref[...], terms_ref[...], preferred_element_type=F32)
        for j in range(kv_ref.shape[0]):
            at = slice(j * rows, (j + 1) * rows)
            lat = full[:d_lat, at].astype(BF16)
            out_ref[at, :d_nope] = lax.dot_general(
                lat,
                kv_ref[j, :, :d_nope],
                (((0,), (0,)), ((), ())),
                preferred_element_type=F32,
            )
            out_ref[at, d_nope:] = full[d_lat:, at].T


def project(where, cache_t, spread, expo, kv_up, half, q_width):
    c_width, keys = cache_t.shape
    total = spread.shape[1]
    width = 2 * total // half
    column = pl.BlockSpec((keys, width), lambda p, w: (0, p))
    result = pl.BlockSpec((width, q_width), lambda p, w: (p, 0))
    return pl.pallas_call(
        project_kernel,
        out_shape=(jax.ShapeDtypeStruct((total, q_width), F32),) * 2,
        grid_spec=pltpu.PrefetchScalarGridSpec(
            num_scalar_prefetch=1,
            grid=(half // 2,),
            in_specs=[
                pl.BlockSpec((c_width, keys), lambda p, w: (0, 0)),
                column,
                column,
                pl.BlockSpec((2,) + kv_up.shape[1:], lambda p, w: (w[0] * (half // 2) + p, 0, 0)),
            ],
            out_specs=[result, result],
        ),
        compiler_params=pltpu.CompilerParams(vmem_limit_bytes=VMEM_BYTES),
        cost_estimate=pl.CostEstimate(
            flops=4 * keys * total * c_width, bytes_accessed=4 * keys * total, transcendentals=0
        ),
    )(where, cache_t, spread, expo, kv_up)


def weigh_kernel(
    scale,
    joined_ref,
    own_ref,
    gains_ref,
    query_ref,
    grad_ref,
    by_spread_ref,
    by_expo_ref,
    spread_ref,
    expo_ref,
    dq_ref,
    with_spread_ref,
    with_expo_ref,
    out_ref,
):
    total = query_ref.shape[0]
    d_lat = grad_ref.shape[1]

    @pl.when(pl.program_id(0) == 0)
    def _():
        tops = [joined_ref[k, 0:1] for k in range(joined_ref.shape[0])]
        top = functools.reduce(jnp.maximum, tops)
        mass = jnp.zeros_like(top)
        dsum = jnp.zeros_like(top)
        for k in range(joined_ref.shape[0]):
            part = jnp.exp2(tops[k] - top)
            mass = mass + part * joined_ref[k, 1:2]
            dsum = dsum + part * joined_ref[k, 2:3]
        centre = own_ref[2:3] / jnp.maximum(own_ref[1:2], 1e-30)
        factor = gains_ref[...] * jnp.exp2(own_ref[0:1] - top) / mass
        shift = dsum / mass - centre
        sublane = lax.broadcasted_iota(jnp.int32, (8, total), 0)
        both = jnp.where(sublane == 0, factor, shift).T
        factor = both[:, 0:1]
        shift = both[:, 1:2]
        scaled = scale * factor
        dq = (scaled * (by_spread_ref[...] - shift * by_expo_ref[...])).astype(BF16)
        blocks, half, size = dq_ref.shape[0], dq_ref.shape[1], dq_ref.shape[2]
        for h in range(half):
            for b in range(blocks):
                first = (h * blocks + b) * size
                dq_ref[b, h] = dq[first : first + size]
        query = scaled * query_ref[...].astype(F32)
        with_spread_ref[...] = query.astype(BF16)
        moved = shift * query
        with_expo_ref[:, :d_lat] = (
            factor * grad_ref[...].astype(F32) - moved[:, :d_lat]
        ).astype(BF16)
        with_expo_ref[:, d_lat:] = (-moved[:, d_lat:]).astype(BF16)

    out = jnp.dot(spread_ref[...], with_spread_ref[...], preferred_element_type=F32)
    out = out + jnp.dot(expo_ref[...], with_expo_ref[...], preferred_element_type=F32)
    out_ref[...] = out.astype(BF16)


def weigh(joined, stats, gains, query, grad, by_spread, by_expo, spread, expo, scale, blocks, half):
    keys, total = spread.shape[0] // 2, spread.shape[1]
    c_width = query.shape[1]
    q_width = by_spread.shape[1]
    size = total // (half * blocks)
    tile = keys // 2
    whole = lambda x: pl.BlockSpec(x.shape, lambda i: (0,) * len(x.shape))
    dq = jax.ShapeDtypeStruct((blocks, half, size, q_width), BF16)
    weight = jax.ShapeDtypeStruct((total, c_width), BF16)
    second = pl.BlockSpec((tile, total), lambda i: (i + 2, 0))
    return pl.pallas_call(
        functools.partial(weigh_kernel, scale),
        out_shape=(dq, weight, weight, jax.ShapeDtypeStruct((keys, c_width), BF16)),
        grid=(2,),
        in_specs=[whole(x) for x in (joined, stats, gains, query, grad, by_spread, by_expo)]
        + [second, second],
        out_specs=[
            whole(dq),
            whole(weight),
            whole(weight),
            pl.BlockSpec((tile, c_width), lambda i: (i, 0)),
        ],
        compiler_params=pltpu.CompilerParams(vmem_limit_bytes=VMEM_BYTES),
        cost_estimate=pl.CostEstimate(
            flops=4 * keys * total * c_width, bytes_accessed=4 * keys * total, transcendentals=0
        ),
    )(joined, stats, gains, query, grad, by_spread, by_expo, spread, expo)


def cache_kernel(spread_ref, expo_ref, with_spread_ref, with_expo_ref, out_ref):
    out = jnp.dot(spread_ref[...], with_spread_ref[...], preferred_element_type=F32)
    out_ref[...] = out + jnp.dot(expo_ref[...], with_expo_ref[...], preferred_element_type=F32)


def cache_terms(spread, expo, with_spread, with_expo):
    keys, total = spread.shape[0] // 2, spread.shape[1]
    c_width = with_spread.shape[1]
    tile = keys // 2
    first = pl.BlockSpec((tile, total), lambda i: (i, 0))
    weight = pl.BlockSpec((total, c_width), lambda i: (0, 0))
    return pl.pallas_call(
        cache_kernel,
        out_shape=jax.ShapeDtypeStruct((keys, c_width), F32),
        grid=(2,),
        in_specs=[first, first, weight, weight],
        out_specs=pl.BlockSpec((tile, c_width), lambda i: (i, 0)),
        compiler_params=pltpu.CompilerParams(vmem_limit_bytes=VMEM_BYTES),
        cost_estimate=pl.CostEstimate(
            flops=4 * keys * total * c_width, bytes_accessed=4 * keys * total, transcendentals=0
        ),
    )(spread, expo, with_spread, with_expo)


def per_device(queries, out_grad, kv_up, latent_cache, token_ratio, pair_lens, prompt_len):
    ctx_index = lax.axis_index("ctx")
    head_index = lax.axis_index("head")
    core = ctx_index % 2
    x_lo = (ctx_index // 2) % 2
    z = ctx_index // 4
    nz = lax.axis_size("ctx") // 4
    ny = lax.axis_size("head") // 2
    y = head_index % ny
    x_hi = head_index // ny
    other_core = lambda i: i ^ 1
    other_x_lo = lambda i: i ^ 2
    z_groups = [[4 * k + j for k in range(nz)] for j in range(4)]

    q_dev, heads, q_width = queries.shape
    p_dev, c_width = latent_cache.shape
    d_lat = kv_up.shape[1]
    d_rope = c_width - d_lat
    d_nope = q_width - d_rope
    half = heads // 2
    rows = q_dev * 4 * nz
    scale = q_width ** (-0.5)

    other_cache = permute(latent_cache, "ctx", other_core)

    high = lax.reduce_precision(token_ratio, 8, 7)
    middle = lax.reduce_precision(token_ratio - high, 8, 7)
    low = token_ratio - high - middle
    terms = jnp.stack([high, middle, low], axis=1).astype(BF16)
    terms = jnp.broadcast_to(terms[:, None, :], (q_dev, heads, 3))
    own = jnp.concatenate(
        [queries[:, :, :d_nope], out_grad, queries[:, :, d_nope:], terms], axis=2
    )
    own = jnp.transpose(own, (1, 0, 2)).reshape(2, half, q_dev, -1)
    block = jnp.concatenate(
        [pick(own, core, 0), permute(pick(own, 1 - core, 0), "ctx", other_core)], 1
    )
    block = in_order(block, permute(block, "ctx", other_x_lo), x_lo == 1, 1)
    up = down = block
    ring = [block] + [None] * (nz - 1)
    for k in range(1, nz // 2 + 1):
        up = permute(up, "ctx", lambda i: (i + 4) % (4 * nz))
        ring[nz - k] = up
        if k < nz // 2:
            down = permute(down, "ctx", lambda i: (i - 4) % (4 * nz))
            ring[k] = down
    ring = jnp.stack(ring, axis=1)
    ring = jnp.concatenate([ring, ring], axis=1)
    everything = lax.dynamic_slice_in_dim(ring, (nz - z) % nz, nz, 1)
    everything = everything.reshape(half, rows, -1)

    ratio = jnp.sum(everything[0, :, -3:].astype(F32), axis=1).reshape(nz, 2, 2, q_dev)
    ratio = jnp.where(core == 1, ratio[:, :, ::-1], ratio).reshape(rows)
    gains = row_gains(ratio, pair_lens).reshape(nz, 2, 2, q_dev)
    gains = jnp.where(core == 1, gains[:, :, ::-1], gains).reshape(1, rows)
    gains = jnp.tile(gains, (1, half))

    where = jnp.stack(
        [core, ctx_index * p_dev, (ctx_index ^ 1) * p_dev, prompt_len[0]]
    ).astype(jnp.int32)
    query, grad, expo, spread, stats = attend(
        where, everything, kv_up, latent_cache, other_cache, scale * LOG2E
    )
    cache_t = jnp.concatenate([latent_cache, other_cache], axis=0).T
    pair = permute(stats, "ctx", other_x_lo)
    by_spread, by_expo = project(where, cache_t, spread, expo, kv_up, half, q_width)
    pair, by_spread, by_expo = lax.optimization_barrier((pair, by_spread, by_expo))
    joined = join_stats(stats, pair)
    joined = lax.all_to_all(
        jnp.broadcast_to(joined[None], (nz,) + joined.shape),
        "ctx",
        0,
        0,
        axis_index_groups=z_groups,
    )
    dq, with_spread, with_expo, for_other = weigh(
        joined, stats, gains, query, grad, by_spread, by_expo, spread, expo, scale, nz, half
    )
    from_other = permute(for_other, "ctx", other_core)
    partial = cache_terms(spread, expo, with_spread, with_expo)

    partial = partial.reshape(2, ny, p_dev // (2 * ny), c_width)
    from_other = from_other.reshape(partial.shape)

    def for_y(k):
        at = (y + k) % ny
        return pick(partial, at, 1) + pick(from_other, at, 1).astype(F32)

    blocks = [for_y(k).astype(BF16) for k in range(1, ny)]
    blocks, dq = lax.optimization_barrier((blocks, dq))
    arrived = [
        permute(blocks[k - 1], "head", lambda i, k=k: (i // ny) * ny + (i + k) % ny)
        for k in range(1, ny)
    ]

    dq = lax.all_to_all(dq, "ctx", 0, 0, axis_index_groups=z_groups)
    dq = jnp.sum(dq.astype(F32), axis=0).reshape(half, 2, 2 * q_dev, q_width)
    from_pair = permute(pick(dq, 1 - x_lo, 1).astype(BF16), "ctx", other_x_lo)
    dq = (pick(dq, x_lo, 1) + from_pair.astype(F32)).astype(BF16)
    theirs = permute(dq[:, q_dev:], "ctx", other_core)
    query_grad = jnp.transpose(in_order(dq[:, :q_dev], theirs, core == 1, 0), (1, 0, 2))

    total = for_y(0)
    for part in arrived:
        total = total + part.astype(F32)
    across = permute(
        pick(total, 1 - x_hi, 0).astype(BF16), "head", lambda i: (i + ny) % (2 * ny)
    )
    cache_grad = (pick(total, x_hi, 0) + across.astype(F32)).astype(BF16)
    return (query_grad, cache_grad)


def solution(mesh):
    placed = (
        P("ctx", "head", None),
        P("ctx", "head", None),
        P("head", None, None),
        P("ctx", None),
        P("ctx"),
        P(),
        P(),
    )
    return jax.shard_map(
        per_device,
        mesh=mesh,
        in_specs=placed,
        out_specs=(P("ctx", "head", None), P(("ctx", "head"), None)),
        check_vma=False,
    )
```

```python
import functools

import jax
import jax.numpy as jnp
from jax import lax
from jax.experimental import pallas as pl
from jax.experimental.pallas import tpu as pltpu
from jax.sharding import PartitionSpec as P

BETA = 0.1
LOSS_SCALE = 2048.0
LOG2E = 1.4426950408889634
NEVER = -1e30
FLOOR = -1e29
F32 = jnp.float32
BF16 = jnp.bfloat16
CHUNK = 128
PACKED = 384
MIB = 1024 * 1024
ATTEND_MIB = 18
PROJECT_MIB = 12
WEIGH_MIB = 16
CACHE_MIB = 20


def permute(x, axis, to):
    return lax.ppermute(x, axis, [(i, to(i)) for i in range(lax.axis_size(axis))])


def in_order(mine, theirs, second, axis):
    return jnp.where(
        second,
        jnp.concatenate([theirs, mine], axis),
        jnp.concatenate([mine, theirs], axis),
    )


def pick(x, index, axis):
    first = lax.index_in_dim(x, 0, axis, keepdims=False)
    second = lax.index_in_dim(x, 1, axis, keepdims=False)
    return jnp.where(index == 1, second, first)


def join_stats(first, second):
    top = jnp.maximum(first[0:1], second[0:1])
    both = jnp.exp2(first[0:1] - top) * first + jnp.exp2(second[0:1] - top) * second
    return jnp.where(lax.broadcasted_iota(jnp.int32, both.shape, 0) == 0, top, both)


def join_kernel(first_ref, second_ref, out_ref):
    out_ref[...] = join_stats(first_ref[...], second_ref[...])


def join(first, second):
    vmem = pl.BlockSpec(memory_space=pltpu.VMEM)
    return pl.pallas_call(
        join_kernel,
        out_shape=jax.ShapeDtypeStruct(first.shape, F32),
        in_specs=[vmem, vmem],
        out_specs=vmem,
        compiler_params=pltpu.CompilerParams(vmem_limit_bytes=MIB),
    )(first, second)


def against(x, y):
    return lax.dot_general(x, y, (((1,), (1,)), ((), ())), preferred_element_type=F32)


def stage_kernel(where_ref, *refs):
    cache_ref, out_ref = refs[0], refs[len(refs) // 2]
    out_ref[...] = cache_ref[...].T
    if len(refs) == 4:
        refs[3][...] = refs[1][...]


def stage(where, cache_t, kv_up=None, steps=4):
    c_width, keys = cache_t.shape
    width = keys // steps
    out_shape = [jax.ShapeDtypeStruct((keys, c_width), BF16)]
    in_specs = [pl.BlockSpec((c_width, width), lambda p, w: (0, p))]
    out_specs = [pl.BlockSpec((width, c_width), lambda p, w: (p, 0))]
    operands = [cache_t]
    if kv_up is not None:
        half = kv_up.shape[0] // 2
        block = (half // steps,) + kv_up.shape[1:]
        out_shape.append(jax.ShapeDtypeStruct((half,) + kv_up.shape[1:], BF16))
        in_specs.append(pl.BlockSpec(block, lambda p, w: (w[0] * steps + p, 0, 0)))
        out_specs.append(pl.BlockSpec(block, lambda p, w: (p, 0, 0)))
        operands.append(kv_up)
    return pl.pallas_call(
        stage_kernel,
        out_shape=out_shape,
        grid_spec=pltpu.PrefetchScalarGridSpec(
            num_scalar_prefetch=1, grid=(steps,), in_specs=in_specs, out_specs=out_specs
        ),
        compiler_params=pltpu.CompilerParams(vmem_limit_bytes=8 * MIB),
        cost_estimate=pl.CostEstimate(
            flops=keys * c_width, bytes_accessed=4 * keys * c_width, transcendentals=0
        ),
    )(where, *operands)


def attend_kernel(score_scale, blocks, where_ref, *refs):
    ring_refs, refs = refs[:blocks], refs[blocks:]
    kv_ref, own_ref, other_ref, query_ref, grad_ref, expo_ref, spread_ref, stats_ref = refs[:8]
    ratio_ref, raw, scores, dprod = refs[8:]
    size = ring_refs[0].shape[0]
    rows, d_nope = size * blocks, kv_ref.shape[2] // 2
    d_lat = kv_ref.shape[1]
    d_rope = query_ref.shape[1] - d_lat
    keys = own_ref.shape[0]
    width = query_ref.shape[0]
    for k in range(blocks):
        first = pl.multiple_of(where_ref[4 + k] * size, size)
        raw[pl.ds(first, size), :] = ring_refs[k][...]
    for j in range(kv_ref.shape[0]):
        at = slice(j * rows, (j + 1) * rows)
        lane = j * PACKED
        lat = against(raw[:, lane : lane + d_nope], kv_ref[j, :, :d_nope])
        query_ref[at, :d_lat] = lat.astype(BF16)
        query_ref[at, d_lat:] = raw[:, lane + 2 * d_nope : lane + 2 * d_nope + d_rope]
        lat = against(raw[:, lane + d_nope : lane + 2 * d_nope], kv_ref[j, :, d_nope:])
        grad_ref[at, :] = lat.astype(BF16)
    terms = raw[:, 2 * d_nope : 3 * d_nope].astype(F32)
    lane = lax.broadcasted_iota(jnp.int32, terms.shape, 1)
    terms = jnp.where((lane >= d_rope) & (lane < d_rope + 3), terms, 0.0)
    ratio_ref[...] = jnp.broadcast_to(jnp.sum(terms, axis=1, keepdims=True), ratio_ref.shape)
    scores[:keys] = against(own_ref[...], query_ref[...])
    scores[keys:] = against(other_ref[...], query_ref[...])
    dprod[:keys] = against(own_ref[:, :d_lat], grad_ref[...])
    dprod[keys:] = against(other_ref[:, :d_lat], grad_ref[...])
    steps = 2 * keys // CHUNK

    def fold(x, join):
        return join(x.reshape(CHUNK // 8, 8, width), axis=0)

    def highest(i, top):
        at = pl.ds(pl.multiple_of(i * CHUNK, CHUNK), CHUNK)
        first = jnp.where(i * CHUNK < keys, where_ref[1], where_ref[2] - keys) + i * CHUNK
        key = first + lax.broadcasted_iota(jnp.int32, (CHUNK, width), 0)
        value = jnp.where(key < where_ref[3], scores[at, :] * score_scale, NEVER)
        scores[at, :] = value
        return jnp.maximum(top, fold(value, jnp.max))

    top = lax.fori_loop(0, steps, highest, jnp.full((8, width), FLOOR, F32), unroll=2)
    top = jnp.max(top, axis=0, keepdims=True)

    def sums(i, so_far):
        at = pl.ds(pl.multiple_of(i * CHUNK, CHUNK), CHUNK)
        value = jnp.exp2(scores[at, :] - top)
        scores[at, :] = value
        expo_ref[at, :] = value.astype(BF16)
        return (
            so_far[0] + fold(value, jnp.sum),
            so_far[1] + fold(value * dprod[at, :], jnp.sum),
        )

    zero = jnp.zeros((8, width), F32)
    mass, dsum = lax.fori_loop(0, steps, sums, (zero, zero), unroll=2)
    mass = jnp.sum(mass, axis=0, keepdims=True)
    dsum = jnp.sum(dsum, axis=0, keepdims=True)
    centre = dsum / jnp.maximum(mass, 1e-30)

    def spreads(i, carry):
        at = pl.ds(pl.multiple_of(i * CHUNK, CHUNK), CHUNK)
        spread_ref[at, :] = (scores[at, :] * (dprod[at, :] - centre)).astype(BF16)
        return carry

    lax.fori_loop(0, steps, spreads, 0, unroll=2)
    stats_ref[0:1] = top
    stats_ref[1:2] = mass
    stats_ref[2:3] = dsum


def attend(where, ring, kv_up, own, other, score_scale):
    blocks, (size, packed) = len(ring), ring[0].shape
    half = packed // PACKED
    rows = blocks * size
    d_lat = kv_up.shape[1]
    keys, c_width = own.shape
    total = half * rows
    width = 2 * rows
    whole = lambda p, w: (0, 0)
    column = lambda p, w: (0, p)
    return pl.pallas_call(
        functools.partial(attend_kernel, score_scale, blocks),
        out_shape=(
            jax.ShapeDtypeStruct((total, c_width), BF16),
            jax.ShapeDtypeStruct((total, d_lat), BF16),
            jax.ShapeDtypeStruct((2 * keys, total), BF16),
            jax.ShapeDtypeStruct((2 * keys, total), BF16),
            jax.ShapeDtypeStruct((3, total), F32),
            jax.ShapeDtypeStruct((rows, 128), F32),
        ),
        grid_spec=pltpu.PrefetchScalarGridSpec(
            num_scalar_prefetch=1,
            grid=(half // 2,),
            in_specs=[pl.BlockSpec((size, 2 * PACKED), column)] * blocks
            + [
                pl.BlockSpec((2,) + kv_up.shape[1:], lambda p, w: (p, 0, 0)),
                pl.BlockSpec((keys, c_width), whole),
                pl.BlockSpec((keys, c_width), whole),
            ],
            out_specs=[
                pl.BlockSpec((width, c_width), lambda p, w: (p, 0)),
                pl.BlockSpec((width, d_lat), lambda p, w: (p, 0)),
                pl.BlockSpec((2 * keys, width), column),
                pl.BlockSpec((2 * keys, width), column),
                pl.BlockSpec((3, width), column),
                pl.BlockSpec((rows, 128), whole),
            ],
            scratch_shapes=[
                pltpu.VMEM((rows, 2 * PACKED), BF16),
                pltpu.VMEM((2 * keys, width), F32),
                pltpu.VMEM((2 * keys, width), F32),
            ],
        ),
        compiler_params=pltpu.CompilerParams(vmem_limit_bytes=ATTEND_MIB * MIB),
        cost_estimate=pl.CostEstimate(
            flops=2 * 2 * keys * total * (c_width + d_lat),
            bytes_accessed=8 * keys * total,
            transcendentals=2 * keys * total,
        ),
    )(where, *ring, kv_up, own, other)


def project_kernel(
    where_ref, own_ref, other_ref, spread_ref, expo_ref, kv_ref, by_spread_ref, by_expo_ref
):
    d_lat = kv_ref.shape[1]
    d_nope = kv_ref.shape[2] // 2
    rows = spread_ref.shape[1] // kv_ref.shape[0]
    for terms_ref, out_ref in ((spread_ref, by_spread_ref), (expo_ref, by_expo_ref)):
        keys = own_ref.shape[1]
        full = jnp.dot(own_ref[...], terms_ref[:keys], preferred_element_type=F32)
        full = full + jnp.dot(other_ref[...], terms_ref[keys:], preferred_element_type=F32)
        for j in range(kv_ref.shape[0]):
            at = slice(j * rows, (j + 1) * rows)
            lat = full[:d_lat, at].astype(BF16)
            out_ref[at, :d_nope] = lax.dot_general(
                lat,
                kv_ref[j, :, :d_nope],
                (((0,), (0,)), ((), ())),
                preferred_element_type=F32,
            )
            out_ref[at, d_nope:] = full[d_lat:, at].T


def project(p, where, own_t, other_t, spread, expo, kv_up, half, q_width):
    c_width, keys = own_t.shape
    width = 2 * spread.shape[1] // half
    column = pl.BlockSpec((2 * keys, width), lambda i, w: (0, p))
    result = pl.BlockSpec((width, q_width), lambda i, w: (0, 0))
    return pl.pallas_call(
        project_kernel,
        out_shape=(jax.ShapeDtypeStruct((width, q_width), F32),) * 2,
        grid_spec=pltpu.PrefetchScalarGridSpec(
            num_scalar_prefetch=1,
            grid=(1,),
            in_specs=[
                pl.BlockSpec((c_width, keys), lambda i, w: (0, 0)),
                pl.BlockSpec((c_width, keys), lambda i, w: (0, 0)),
                column,
                column,
                pl.BlockSpec((2,) + kv_up.shape[1:], lambda i, w: (p, 0, 0)),
            ],
            out_specs=[result, result],
        ),
        compiler_params=pltpu.CompilerParams(vmem_limit_bytes=PROJECT_MIB * MIB),
        cost_estimate=pl.CostEstimate(
            flops=8 * keys * width * c_width, bytes_accessed=8 * keys * width, transcendentals=0
        ),
    )(where, own_t, other_t, spread, expo, kv_up)


def row_gains(where_ref, lens_ref, ratio_ref, rows_of_core):
    rows = ratio_ref.shape[0]
    place = lax.broadcasted_iota(jnp.int32, (rows, 1), 0)
    turn = place % (2 * rows_of_core) >= rows_of_core
    swapped = jnp.where(turn, place - rows_of_core, place + rows_of_core)
    place = jnp.where(where_ref[0] == 1, swapped, place)
    ratio = ratio_ref[:, 0:1]
    segments = lens_ref.shape[0]
    members = []
    first = jnp.int32(0)
    for k in range(segments):
        last = first + lens_ref[k]
        members.append((place >= first) & (place < last))
        first = last
    sums = [jnp.sum(jnp.where(m, ratio, 0.0), axis=0, keepdims=True) for m in members]
    gains = jnp.zeros((rows, 1), F32)
    for p in range(segments // 2):
        margin = BETA * (sums[2 * p] - sums[2 * p + 1])
        weight = LOSS_SCALE * BETA / (1.0 + jnp.exp(margin))
        gains = jnp.where(members[2 * p], -weight, gains)
        gains = jnp.where(members[2 * p + 1], weight, gains)
    return gains


def weigh_kernel(scale, rows_of_core, where_ref, lens_ref, *refs):
    (joined_ref, last_ref, own_ref, ratio_ref, query_ref, grad_ref) = refs[:6]
    by_spread_refs, by_expo_refs = refs[6:-4:2], refs[7:-4:2]
    dq_keep_ref, dq_send_ref, with_spread_ref, with_expo_ref = refs[-4:]
    total = query_ref.shape[0]
    d_lat = grad_ref.shape[1]
    rows = ratio_ref.shape[0]
    half = total // rows
    gains = row_gains(where_ref, lens_ref, ratio_ref, rows_of_core)
    joined = join_stats(joined_ref[...], last_ref[...])
    centre = own_ref[2:3] / jnp.maximum(own_ref[1:2], 1e-30)
    factor = jnp.exp2(own_ref[0:1] - joined[0:1]) / joined[1:2]
    shift = joined[2:3] / joined[1:2] - centre
    sublane = lax.broadcasted_iota(jnp.int32, (8, total), 0)
    both = jnp.where(sublane == 0, factor, shift).T
    blocks, size = dq_keep_ref.shape[0], dq_keep_ref.shape[2] // 2
    second = where_ref[4 + blocks] == 1
    for h in range(half):
        at = slice(h * rows, (h + 1) * rows)
        part = slice((h % 2) * rows, (h % 2 + 1) * rows)
        factor = both[at, 0:1] * gains
        shift = both[at, 1:2]
        scaled = scale * factor
        dq = by_spread_refs[h // 2][part, :] - shift * by_expo_refs[h // 2][part, :]
        dq = scaled * dq
        if h % 2:
            for b in range(blocks):
                pieces = []
                for x in range(2):
                    first = (2 * b + x) * size
                    at_x = slice(first, first + size)
                    pieces.append(jnp.concatenate([before[at_x], dq[at_x]], axis=0))
                dq_keep_ref[b, h // 2] = jnp.where(second, pieces[1], pieces[0]).astype(BF16)
                dq_send_ref[b, h // 2] = jnp.where(second, pieces[0], pieces[1]).astype(BF16)
        before = dq
        query = scaled * query_ref[at, :].astype(F32)
        with_spread_ref[at, :] = query.astype(BF16)
        moved = shift * query
        with_expo_ref[at, :d_lat] = (
            factor * grad_ref[at, :].astype(F32) - moved[:, :d_lat]
        ).astype(BF16)
        with_expo_ref[at, d_lat:] = (-moved[:, d_lat:]).astype(BF16)


def weigh(where, lens, joined, last, stats, ratio, query, grad, projected, scale, blocks, q_dev):
    total, c_width = query.shape
    rows = ratio.shape[0]
    q_width = projected[0].shape[1]
    half = total // rows
    smem = pl.BlockSpec(memory_space=pltpu.SMEM)
    vmem = pl.BlockSpec(memory_space=pltpu.VMEM)
    dq = jax.ShapeDtypeStruct((blocks, half // 2, rows // blocks, q_width), BF16)
    weight = jax.ShapeDtypeStruct((total, c_width), BF16)
    inputs = (joined, last, stats, ratio, query, grad, *projected)
    return pl.pallas_call(
        functools.partial(weigh_kernel, scale, q_dev),
        out_shape=(dq, dq, weight, weight),
        in_specs=[smem, smem] + [vmem] * len(inputs),
        out_specs=[vmem] * 4,
        compiler_params=pltpu.CompilerParams(vmem_limit_bytes=WEIGH_MIB * MIB),
        cost_estimate=pl.CostEstimate(
            flops=10 * total * c_width, bytes_accessed=8 * total * c_width, transcendentals=0
        ),
    )(where, lens, *inputs)


def cache_kernel(part, d_lat, order_ref, spread_ref, expo_ref, with_spread_ref, with_expo_ref, *refs):
    adds, outs = refs[:-2], refs[-2:]
    keys = spread_ref.shape[3]

    def gather(ref):
        blocks = [ref[part, x, order_ref[i]] for i in range(2) for x in range(2)]
        return jnp.concatenate(blocks, axis=0)

    out = jnp.dot(gather(spread_ref), with_spread_ref[...], preferred_element_type=F32)
    out = out + jnp.dot(gather(expo_ref), with_expo_ref[...], preferred_element_type=F32)
    rope = out.shape[1] - d_lat
    for i in range(4):
        first = (i % 2) * d_lat
        lat = slice(first, first + d_lat)
        first = 2 * d_lat + (i % 2) * rope
        tail = slice(first, first + rope)
        at = slice(i * keys, (i + 1) * keys)
        for lanes, value in ((lat, out[at, :d_lat]), (tail, out[at, d_lat:])):
            if adds:
                value = value + adds[i // 2][:, lanes].astype(F32)
            outs[i // 2][:, lanes] = value.astype(outs[i // 2].dtype)


def cache_terms(part, order, d_lat, spread, expo, with_spread, with_expo, dtypes, adds=()):
    total, c_width = with_spread.shape
    keys = spread.shape[3]
    smem = pl.BlockSpec(memory_space=pltpu.SMEM)
    vmem = pl.BlockSpec(memory_space=pltpu.VMEM)
    return pl.pallas_call(
        functools.partial(cache_kernel, part, d_lat),
        out_shape=[jax.ShapeDtypeStruct((keys, 2 * c_width), dtype) for dtype in dtypes],
        in_specs=[smem] + [vmem] * (4 + len(adds)),
        out_specs=[vmem, vmem],
        compiler_params=pltpu.CompilerParams(vmem_limit_bytes=CACHE_MIB * MIB),
        cost_estimate=pl.CostEstimate(
            flops=16 * keys * total * c_width,
            bytes_accessed=16 * keys * total,
            transcendentals=0,
        ),
    )(order, spread, expo, with_spread, with_expo, *adds)


def per_device(queries, out_grad, kv_up, latent_cache, token_ratio, pair_lens, prompt_len):
    ctx_index = lax.axis_index("ctx")
    head_index = lax.axis_index("head")
    core = ctx_index & 1
    x_lo = (ctx_index >> 1) & 1
    z = ctx_index >> 2
    nz = lax.axis_size("ctx") // 4
    ny = lax.axis_size("head") // 2
    y = head_index & (ny - 1)
    x_hi = (head_index >= ny).astype(jnp.int32)
    other_core = lambda i: i ^ 1
    other_x_lo = lambda i: i ^ 2
    z_groups = [[4 * k + j for k in range(nz)] for j in range(4)]

    q_dev, heads, q_width = queries.shape
    p_dev, c_width = latent_cache.shape
    d_lat = kv_up.shape[1]
    d_rope = c_width - d_lat
    d_nope = q_width - d_rope
    half = heads // 2
    scale = q_width ** (-0.5)

    where = [core, ctx_index * p_dev, (ctx_index ^ 1) * p_dev, prompt_len[0]]
    where = where + [(z + k) & (nz - 1) for k in range(nz)] + [x_lo]
    where = jnp.stack(where).astype(jnp.int32)
    own_t = latent_cache.T
    other_t = permute(latent_cache, "ctx", other_core).T
    own_keys, kv_half = stage(where, own_t, kv_up)
    (other_keys,) = stage(where, other_t)

    high = lax.reduce_precision(token_ratio, 8, 7)
    middle = lax.reduce_precision(token_ratio - high, 8, 7)
    low = token_ratio - high - middle
    terms = jnp.stack([high, middle, low], axis=1).astype(BF16)
    terms = jnp.broadcast_to(terms[:, None, :], (q_dev, heads, 3))
    own = jnp.concatenate(
        [queries[:, :, :d_nope], out_grad, queries[:, :, d_nope:], terms], axis=2
    )
    own = jnp.pad(own, ((0, 0), (0, 0), (0, PACKED - own.shape[2])))
    own = own.reshape(q_dev, 2, half * PACKED)
    block = jnp.concatenate(
        [pick(own, core, 1), permute(pick(own, 1 - core, 1), "ctx", other_core)], 0
    )
    block = in_order(block, permute(block, "ctx", other_x_lo), x_lo == 1, 0)
    up = down = block
    ring = [block] + [None] * (nz - 1)
    for k in range(1, nz // 2 + 1):
        up = permute(up, "ctx", lambda i: (i + 4) % (4 * nz))
        ring[nz - k] = up
        if k < nz // 2:
            down = permute(down, "ctx", lambda i: (i - 4) % (4 * nz))
            ring[k] = down

    query, grad, expo, spread, stats, ratio = attend(
        where, ring, kv_half, own_keys, other_keys, scale * LOG2E
    )

    joined = stats
    projected = []
    pairings = [other_x_lo] + [lambda i, k=k: i ^ (4 << k) for k in range(nz.bit_length() - 1)]
    for p, pairing in enumerate(pairings):
        if p:
            joined = join(joined, last)
        last = permute(joined, "ctx", pairing)
        if p < half // 2:
            terms = project(p, where, own_t, other_t, spread, expo, kv_half, half, q_width)
            last, *terms = lax.optimization_barrier((last, *terms))
            projected += terms
    dq_keep, dq_send, with_spread, with_expo = weigh(
        where, pair_lens, joined, last, stats, ratio, query, grad, projected, scale, nz, q_dev
    )
    dq_pair = permute(dq_send, "ctx", other_x_lo)
    steps = (2, 1, 3, 0)
    order = jnp.stack([(y + k) & (ny - 1) for k in steps]).astype(jnp.int32)
    keys = p_dev // (2 * ny)
    shape = (2, 2, ny, keys, spread.shape[1])
    operands = (d_lat, spread.reshape(shape), expo.reshape(shape), with_spread, with_expo)
    sends = [cache_terms(1, order[k : k + 2], *operands, (BF16, BF16)) for k in (0, 2)]
    adds = [[permute(x, "ctx", other_core) for x in send] for send in sends]
    blocks = cache_terms(0, order[:2], *operands, (BF16, BF16), adds[0])
    last_block, total = cache_terms(0, order[2:], *operands, (BF16, F32), adds[1])
    blocks = [*blocks, last_block]
    dq = (dq_keep.astype(F32) + dq_pair.astype(F32)).astype(BF16)
    last_block, dq = lax.optimization_barrier((last_block, dq))
    blocks[-1] = last_block
    arrived = [
        permute(block, "head", lambda i, k=k: (i // ny) * ny + (i + k) % ny)
        for block, k in zip(blocks, steps)
    ]

    for part in arrived:
        total = total + part.astype(F32)
    total = jnp.stack(
        [
            jnp.concatenate(
                [
                    total[:, i * d_lat : (i + 1) * d_lat],
                    total[:, 2 * d_lat + i * d_rope : 2 * d_lat + (i + 1) * d_rope],
                ],
                axis=1,
            )
            for i in range(2)
        ]
    )
    across = permute(
        pick(total, 1 - x_hi, 0).astype(BF16), "head", lambda i: (i + ny) % (2 * ny)
    )

    dq = lax.all_to_all(dq, "ctx", 0, 0, axis_index_groups=z_groups)
    dq = jnp.sum(dq.astype(F32), axis=0).astype(BF16).reshape(half, 2, q_dev, q_width)
    theirs = permute(dq[:, 1], "ctx", other_core)
    query_grad = jnp.transpose(in_order(dq[:, 0], theirs, core == 1, 0), (1, 0, 2))

    cache_grad = (pick(total, x_hi, 0) + across.astype(F32)).astype(BF16)
    return (query_grad, cache_grad)


def solution(mesh):
    placed = (
        P("ctx", "head", None),
        P("ctx", "head", None),
        P("head", None, None),
        P("ctx", None),
        P("ctx"),
        P(),
        P(),
    )
    return jax.shard_map(
        per_device,
        mesh=mesh,
        in_specs=placed,
        out_specs=(P("ctx", "head", None), P(("ctx", "head"), None)),
        check_vma=False,
    )
```

```python
import functools

import jax
import jax.numpy as jnp
from jax import lax
from jax.experimental import pallas as pl
from jax.experimental.pallas import tpu as pltpu
from jax.sharding import PartitionSpec as P

BETA = 0.1
LOSS_SCALE = 2048.0
LOG2E = 1.4426950408889634
NEVER = -1e30
FLOOR = -1e29
F32 = jnp.float32
BF16 = jnp.bfloat16
CHUNK = 256
TOGETHER = 4
PACKED = 384
MIB = 1024 * 1024
ATTEND_MIB = 24
PROJECT_MIB = 8
WEIGH_MIB = 16
CACHE_MIB = 20


def permute(x, axis, to):
    return lax.ppermute(x, axis, [(i, to(i)) for i in range(lax.axis_size(axis))])


def in_order(mine, theirs, second, axis):
    return jnp.where(
        second,
        jnp.concatenate([theirs, mine], axis),
        jnp.concatenate([mine, theirs], axis),
    )


def pick(x, index, axis):
    first = lax.index_in_dim(x, 0, axis, keepdims=False)
    second = lax.index_in_dim(x, 1, axis, keepdims=False)
    return jnp.where(index == 1, second, first)


def join_stats(first, second):
    top = jnp.maximum(first[0:1], second[0:1])
    both = jnp.exp2(first[0:1] - top) * first + jnp.exp2(second[0:1] - top) * second
    return jnp.where(lax.broadcasted_iota(jnp.int32, both.shape, 0) == 0, top, both)


def join_kernel(first_ref, second_ref, out_ref):
    out_ref[...] = join_stats(first_ref[...], second_ref[...])


def join(first, second):
    vmem = pl.BlockSpec(memory_space=pltpu.VMEM)
    return pl.pallas_call(
        join_kernel,
        out_shape=jax.ShapeDtypeStruct(first.shape, F32),
        in_specs=[vmem, vmem],
        out_specs=vmem,
        compiler_params=pltpu.CompilerParams(vmem_limit_bytes=MIB),
    )(first, second)


def against(x, y):
    return lax.dot_general(x, y, (((1,), (1,)), ((), ())), preferred_element_type=F32)


def pack_kernel(where_ref, ratio_ref, queries_ref, out_grad_ref, mine_ref, theirs_ref):
    q_dev, heads, q_width = queries_ref.shape
    d_nope = out_grad_ref.shape[2]
    half = heads // 2
    d_rope = q_width - d_nope
    lane = lax.broadcasted_iota(jnp.int32, (heads, PACKED - 2 * d_nope - d_rope), 1)
    second = where_ref[0] == 1
    mine, theirs = [], []
    for j in range(q_dev):
        query = queries_ref[j].astype(F32)
        ratio = jnp.full(lane.shape, ratio_ref[j], F32)
        high = ratio.astype(BF16).astype(F32)
        middle = (ratio - high).astype(BF16).astype(F32)
        terms = jnp.where(lane == 0, high, jnp.where(lane == 1, middle, ratio - high - middle))
        terms = jnp.where(lane < 3, terms, 0.0)
        row = [query[:, :d_nope], out_grad_ref[j].astype(F32), query[:, d_nope:], terms]
        row = jnp.concatenate(row, axis=1)
        mine.append(jnp.where(second, row[half:], row[:half]))
        theirs.append(jnp.where(second, row[:half], row[half:]))
    mine_ref[...] = jnp.concatenate(mine, axis=0).astype(BF16)
    theirs_ref[...] = jnp.concatenate(theirs, axis=0).astype(BF16)


def pack(where, token_ratio, queries, out_grad):
    q_dev, heads = queries.shape[:2]
    smem = pl.BlockSpec(memory_space=pltpu.SMEM)
    vmem = pl.BlockSpec(memory_space=pltpu.VMEM)
    packed = jax.ShapeDtypeStruct((q_dev * heads // 2, PACKED), BF16)
    return pl.pallas_call(
        pack_kernel,
        out_shape=(packed, packed),
        in_specs=[smem, smem, vmem, vmem],
        out_specs=[vmem, vmem],
        compiler_params=pltpu.CompilerParams(vmem_limit_bytes=2 * MIB),
    )(where, token_ratio, queries, out_grad)


def stage_own_kernel(where_ref, cache_ref, kv_ref, out_ref, kv_out_ref, buffer, sems):
    half = kv_out_ref.shape[0]
    cache = pltpu.make_async_copy(cache_ref, buffer, sems.at[0])
    first = pl.multiple_of(where_ref[0] * half, half)
    heads = pltpu.make_async_copy(kv_ref.at[pl.ds(first, half)], kv_out_ref, sems.at[1])
    cache.start()
    heads.start()
    cache.wait()
    out_ref[...] = buffer[...].T
    heads.wait()


def stage_own(where, cache_t, kv_up):
    c_width, keys = cache_t.shape
    smem = pl.BlockSpec(memory_space=pltpu.SMEM)
    vmem = pl.BlockSpec(memory_space=pltpu.VMEM)
    hbm = pl.BlockSpec(memory_space=pltpu.HBM)
    return pl.pallas_call(
        stage_own_kernel,
        out_shape=(
            jax.ShapeDtypeStruct((keys, c_width), BF16),
            jax.ShapeDtypeStruct((kv_up.shape[0] // 2,) + kv_up.shape[1:], BF16),
        ),
        in_specs=[smem, hbm, hbm],
        out_specs=[vmem, vmem],
        scratch_shapes=[pltpu.VMEM((c_width, keys), BF16), pltpu.SemaphoreType.DMA((2,))],
        compiler_params=pltpu.CompilerParams(vmem_limit_bytes=50 * MIB),
        cost_estimate=pl.CostEstimate(
            flops=keys * c_width, bytes_accessed=8 * keys * c_width, transcendentals=0
        ),
    )(where, cache_t, kv_up)


def stage_kernel(cache_ref, out_ref):
    out_ref[...] = cache_ref[...].T


def stage(cache_t):
    c_width, keys = cache_t.shape
    vmem = pl.BlockSpec(memory_space=pltpu.VMEM)
    return pl.pallas_call(
        stage_kernel,
        out_shape=jax.ShapeDtypeStruct((keys, c_width), BF16),
        in_specs=[vmem],
        out_specs=vmem,
        compiler_params=pltpu.CompilerParams(vmem_limit_bytes=6 * MIB),
        cost_estimate=pl.CostEstimate(
            flops=keys * c_width, bytes_accessed=4 * keys * c_width, transcendentals=0
        ),
    )(cache_t)


def attend_kernel(score_scale, blocks, together, where_ref, *refs):
    ring_refs, refs = refs[:blocks], refs[blocks:]
    kv_ref, own_ref, other_ref, query_ref, grad_ref, expo_ref, spread_ref, stats_ref = refs[:8]
    ratio_ref, raw, expo, dprod = refs[8:]
    size = ring_refs[0].shape[0]
    half, d_lat, d_nope = kv_ref.shape[0], kv_ref.shape[1], kv_ref.shape[2] // 2
    rows = size * blocks // half
    d_rope = query_ref.shape[1] - d_lat
    keys = own_ref.shape[0]
    width = together * rows
    for k in range(blocks):
        first = pl.multiple_of(where_ref[4 + k] * size, size)
        for part in range(PACKED // 128):
            lanes = slice(part * 128, (part + 1) * 128)
            raw[part, pl.ds(first, size), :] = ring_refs[k][:, lanes].astype(F32)

    def of_head(h, part):
        return raw[part, pl.ds(h, rows, stride=half), :]

    terms = of_head(0, 2)
    lane = lax.broadcasted_iota(jnp.int32, terms.shape, 1)
    terms = jnp.where((lane >= d_rope) & (lane < d_rope + 3), terms, 0.0)
    ratio_ref[...] = jnp.broadcast_to(jnp.sum(terms, axis=1, keepdims=True), ratio_ref.shape)

    def fold(x, join):
        return join(join(x.reshape(CHUNK // 8, 8, width), axis=0), axis=0, keepdims=True)

    for p in range(half // together):
        for h in range(p * together, (p + 1) * together):
            at = slice(h * rows, (h + 1) * rows)
            lat = against(of_head(h, 0).astype(BF16), kv_ref[h, :, :d_nope])
            query_ref[at, :d_lat] = lat.astype(BF16)
            rope = of_head(h, 2)[:, :d_rope]
            query_ref[at, d_lat:] = rope.astype(BF16)
            lat = against(of_head(h, 1).astype(BF16), kv_ref[h, :, d_nope:])
            grad_ref[at, :] = lat.astype(BF16)
        columns = slice(p * width, (p + 1) * width)
        tops, masses, dsums = [], [], []
        for c in range(2 * keys // CHUNK):
            first = c * CHUNK % keys
            ref, base = (own_ref, where_ref[1]) if c * CHUNK < keys else (other_ref, where_ref[2])
            score = against(ref[first : first + CHUNK, :], query_ref[columns, :]) * score_scale
            dp = against(ref[first : first + CHUNK, :d_lat], grad_ref[columns, :])
            key = base + first + lax.broadcasted_iota(jnp.int32, (CHUNK, 1), 0)
            score = jnp.where(key < where_ref[3], score, NEVER)
            top = jnp.maximum(fold(score, jnp.max), FLOOR)
            value = jnp.exp2(score - top)
            at = slice(c * CHUNK, (c + 1) * CHUNK)
            expo[at] = value
            dprod[at] = dp
            tops.append(top)
            masses.append(fold(value, jnp.sum))
            dsums.append(fold(value * dp, jnp.sum))
        top = functools.reduce(jnp.maximum, tops)
        factors = [jnp.exp2(t - top) for t in tops]
        mass = sum(f * m for f, m in zip(factors, masses))
        dsum = sum(f * d for f, d in zip(factors, dsums))
        centre = dsum / jnp.maximum(mass, 1e-30)
        for c, f in enumerate(factors):
            at = slice(c * CHUNK, (c + 1) * CHUNK)
            value = expo[at] * f
            expo_ref[at, columns] = value.astype(BF16)
            spread_ref[at, columns] = (value * (dprod[at] - centre)).astype(BF16)
        stats_ref[0:1, columns] = top
        stats_ref[1:2, columns] = mass
        stats_ref[2:3, columns] = dsum


def attend(where, ring, kv_half, own, other, score_scale, together=TOGETHER):
    blocks, (size, packed) = len(ring), ring[0].shape
    half, d_lat = kv_half.shape[:2]
    total = blocks * size
    rows = total // half
    keys, c_width = own.shape
    smem = pl.BlockSpec(memory_space=pltpu.SMEM)
    vmem = pl.BlockSpec(memory_space=pltpu.VMEM)
    return pl.pallas_call(
        functools.partial(attend_kernel, score_scale, blocks, together),
        out_shape=(
            jax.ShapeDtypeStruct((total, c_width), BF16),
            jax.ShapeDtypeStruct((total, d_lat), BF16),
            jax.ShapeDtypeStruct((2 * keys, total), BF16),
            jax.ShapeDtypeStruct((2 * keys, total), BF16),
            jax.ShapeDtypeStruct((3, total), F32),
            jax.ShapeDtypeStruct((rows, 128), F32),
        ),
        in_specs=[smem] + [vmem] * (blocks + 3),
        out_specs=[vmem] * 6,
        scratch_shapes=[
            pltpu.VMEM((packed // 128, total, 128), F32),
            pltpu.VMEM((2 * keys, together * rows), F32),
            pltpu.VMEM((2 * keys, together * rows), F32),
        ],
        compiler_params=pltpu.CompilerParams(vmem_limit_bytes=ATTEND_MIB * MIB),
        cost_estimate=pl.CostEstimate(
            flops=2 * 2 * keys * total * (c_width + d_lat),
            bytes_accessed=8 * keys * total,
            transcendentals=2 * keys * total,
        ),
    )(where, *ring, kv_half, own, other)


def project_kernel(p, own_ref, other_ref, spread_ref, expo_ref, kv_ref, *out_refs):
    d_lat, d_nope = kv_ref.shape[1], kv_ref.shape[2] // 2
    keys = own_ref.shape[1]
    width = out_refs[0].shape[0]
    rows = spread_ref.shape[1] // kv_ref.shape[0]
    columns = slice(p * width, (p + 1) * width)
    for terms_ref, out_ref in zip((spread_ref, expo_ref), out_refs):
        full = jnp.dot(own_ref[...], terms_ref[:keys, columns], preferred_element_type=F32)
        full = full + jnp.dot(
            other_ref[...], terms_ref[keys:, columns], preferred_element_type=F32
        )
        for j in range(width // rows):
            at = slice(j * rows, (j + 1) * rows)
            out_ref[at, :d_nope] = lax.dot_general(
                full[:d_lat, at].astype(BF16),
                kv_ref[p * (width // rows) + j, :, :d_nope],
                (((0,), (0,)), ((), ())),
                preferred_element_type=F32,
            )
            out_ref[at, d_nope:] = full[d_lat:, at].T


def project(p, own_t, other_t, spread, expo, kv_half, q_width):
    c_width, keys = own_t.shape
    width = 2 * spread.shape[1] // kv_half.shape[0]
    vmem = pl.BlockSpec(memory_space=pltpu.VMEM)
    return pl.pallas_call(
        functools.partial(project_kernel, p),
        out_shape=(jax.ShapeDtypeStruct((width, q_width), F32),) * 2,
        in_specs=[vmem] * 5,
        out_specs=[vmem] * 2,
        compiler_params=pltpu.CompilerParams(vmem_limit_bytes=PROJECT_MIB * MIB),
        cost_estimate=pl.CostEstimate(
            flops=8 * keys * width * c_width, bytes_accessed=8 * keys * width, transcendentals=0
        ),
    )(own_t, other_t, spread, expo, kv_half)


def row_gains(where_ref, lens_ref, ratio_ref, rows_of_core):
    rows = ratio_ref.shape[0]
    place = lax.broadcasted_iota(jnp.int32, (rows, 1), 0)
    turn = place % (2 * rows_of_core) >= rows_of_core
    swapped = jnp.where(turn, place - rows_of_core, place + rows_of_core)
    place = jnp.where(where_ref[0] == 1, swapped, place)
    ratio = ratio_ref[:, 0:1]
    segments = lens_ref.shape[0]
    members = []
    first = jnp.int32(0)
    for k in range(segments):
        last = first + lens_ref[k]
        members.append((place >= first) & (place < last))
        first = last
    sums = [jnp.sum(jnp.where(m, ratio, 0.0), axis=0, keepdims=True) for m in members]
    gains = jnp.zeros((rows, 1), F32)
    for p in range(segments // 2):
        margin = BETA * (sums[2 * p] - sums[2 * p + 1])
        weight = LOSS_SCALE * BETA / (1.0 + jnp.exp(margin))
        gains = jnp.where(members[2 * p], -weight, gains)
        gains = jnp.where(members[2 * p + 1], weight, gains)
    return gains


def weigh_kernel(scale, rows_of_core, where_ref, lens_ref, *refs):
    (joined_ref, last_ref, own_ref, ratio_ref, query_ref, grad_ref) = refs[:6]
    by_spread_refs, by_expo_refs = refs[6:-4:2], refs[7:-4:2]
    dq_keep_ref, dq_send_ref, with_spread_ref, with_expo_ref = refs[-4:]
    total = query_ref.shape[0]
    d_lat = grad_ref.shape[1]
    rows = ratio_ref.shape[0]
    half = total // rows
    gains = row_gains(where_ref, lens_ref, ratio_ref, rows_of_core)
    joined = join_stats(joined_ref[...], last_ref[...])
    centre = own_ref[2:3] / jnp.maximum(own_ref[1:2], 1e-30)
    factor = jnp.exp2(own_ref[0:1] - joined[0:1]) / joined[1:2]
    shift = joined[2:3] / joined[1:2] - centre
    sublane = lax.broadcasted_iota(jnp.int32, (8, total), 0)
    both = jnp.where(sublane == 0, factor, shift).T
    blocks, size = dq_keep_ref.shape[0], dq_keep_ref.shape[2] // 2
    second = where_ref[4 + blocks] == 1
    for h in range(half):
        at = slice(h * rows, (h + 1) * rows)
        part = slice((h % 2) * rows, (h % 2 + 1) * rows)
        factor = both[at, 0:1] * gains
        shift = both[at, 1:2]
        scaled = scale * factor
        dq = by_spread_refs[h // 2][part, :] - shift * by_expo_refs[h // 2][part, :]
        dq = scaled * dq
        if h % 2:
            for b in range(blocks):
                pieces = []
                for x in range(2):
                    first = (2 * b + x) * size
                    at_x = slice(first, first + size)
                    pieces.append(jnp.concatenate([before[at_x], dq[at_x]], axis=0))
                dq_keep_ref[b, h // 2] = jnp.where(second, pieces[1], pieces[0]).astype(BF16)
                dq_send_ref[b, h // 2] = jnp.where(second, pieces[0], pieces[1]).astype(BF16)
        before = dq
        query = scaled * query_ref[at, :].astype(F32)
        with_spread_ref[at, :] = query.astype(BF16)
        moved = shift * query
        with_expo_ref[at, :d_lat] = (
            factor * grad_ref[at, :].astype(F32) - moved[:, :d_lat]
        ).astype(BF16)
        with_expo_ref[at, d_lat:] = (-moved[:, d_lat:]).astype(BF16)


def weigh(where, lens, joined, last, stats, ratio, query, grad, projected, scale, blocks, q_dev):
    total, c_width = query.shape
    rows = ratio.shape[0]
    q_width = projected[0].shape[1]
    half = total // rows
    smem = pl.BlockSpec(memory_space=pltpu.SMEM)
    vmem = pl.BlockSpec(memory_space=pltpu.VMEM)
    dq = jax.ShapeDtypeStruct((blocks, half // 2, rows // blocks, q_width), BF16)
    weight = jax.ShapeDtypeStruct((total, c_width), BF16)
    inputs = (joined, last, stats, ratio, query, grad, *projected)
    return pl.pallas_call(
        functools.partial(weigh_kernel, scale, q_dev),
        out_shape=(dq, dq, weight, weight),
        in_specs=[smem, smem] + [vmem] * len(inputs),
        out_specs=[vmem] * 4,
        compiler_params=pltpu.CompilerParams(vmem_limit_bytes=WEIGH_MIB * MIB),
        cost_estimate=pl.CostEstimate(
            flops=10 * total * c_width, bytes_accessed=8 * total * c_width, transcendentals=0
        ),
    )(where, lens, *inputs)


def cache_kernel(part, d_lat, order_ref, spread_ref, expo_ref, with_spread_ref, with_expo_ref, *refs):
    adds, outs = refs[:-2], refs[-2:]
    keys = spread_ref.shape[3]

    def gather(ref):
        blocks = [ref[part, x, order_ref[i]] for i in range(2) for x in range(2)]
        return jnp.concatenate(blocks, axis=0)

    out = jnp.dot(gather(spread_ref), with_spread_ref[...], preferred_element_type=F32)
    out = out + jnp.dot(gather(expo_ref), with_expo_ref[...], preferred_element_type=F32)
    rope = out.shape[1] - d_lat
    for i in range(4):
        first = (i % 2) * d_lat
        lat = slice(first, first + d_lat)
        first = 2 * d_lat + (i % 2) * rope
        tail = slice(first, first + rope)
        at = slice(i * keys, (i + 1) * keys)
        for lanes, value in ((lat, out[at, :d_lat]), (tail, out[at, d_lat:])):
            if adds:
                value = value + adds[i // 2][:, lanes].astype(F32)
            outs[i // 2][:, lanes] = value.astype(outs[i // 2].dtype)


def cache_terms(part, order, d_lat, spread, expo, with_spread, with_expo, dtypes, adds=()):
    total, c_width = with_spread.shape
    keys = spread.shape[3]
    smem = pl.BlockSpec(memory_space=pltpu.SMEM)
    vmem = pl.BlockSpec(memory_space=pltpu.VMEM)
    return pl.pallas_call(
        functools.partial(cache_kernel, part, d_lat),
        out_shape=[jax.ShapeDtypeStruct((keys, 2 * c_width), dtype) for dtype in dtypes],
        in_specs=[smem] + [vmem] * (4 + len(adds)),
        out_specs=[vmem, vmem],
        compiler_params=pltpu.CompilerParams(vmem_limit_bytes=CACHE_MIB * MIB),
        cost_estimate=pl.CostEstimate(
            flops=16 * keys * total * c_width,
            bytes_accessed=16 * keys * total,
            transcendentals=0,
        ),
    )(order, spread, expo, with_spread, with_expo, *adds)


def per_device(queries, out_grad, kv_up, latent_cache, token_ratio, pair_lens, prompt_len):
    ctx_index = lax.axis_index("ctx")
    head_index = lax.axis_index("head")
    core = ctx_index & 1
    x_lo = (ctx_index >> 1) & 1
    z = ctx_index >> 2
    nz = lax.axis_size("ctx") // 4
    ny = lax.axis_size("head") // 2
    y = head_index & (ny - 1)
    x_hi = (head_index >= ny).astype(jnp.int32)
    other_core = lambda i: i ^ 1
    other_x_lo = lambda i: i ^ 2
    z_groups = [[4 * k + j for k in range(nz)] for j in range(4)]

    q_dev, heads, q_width = queries.shape
    p_dev, c_width = latent_cache.shape
    d_lat = kv_up.shape[1]
    d_rope = c_width - d_lat
    d_nope = q_width - d_rope
    half = heads // 2
    scale = q_width ** (-0.5)

    where = [core, ctx_index * p_dev, (ctx_index ^ 1) * p_dev, prompt_len[0]]
    where = where + [(z + k) & (nz - 1) for k in range(nz)] + [x_lo]
    where = jnp.stack(where).astype(jnp.int32)
    own_t = latent_cache.T
    other_t = permute(latent_cache, "ctx", other_core).T
    mine, theirs = pack(where, token_ratio, queries, out_grad)
    own_keys, kv_half = stage_own(where, own_t, kv_up)
    other_keys = stage(other_t)
    block = jnp.concatenate([mine, permute(theirs, "ctx", other_core)], 0)
    block = in_order(block, permute(block, "ctx", other_x_lo), x_lo == 1, 0)
    up = down = block
    ring = [block] + [None] * (nz - 1)
    for k in range(1, nz // 2 + 1):
        up = permute(up, "ctx", lambda i: (i + 4) % (4 * nz))
        ring[nz - k] = up
        if k < nz // 2:
            down = permute(down, "ctx", lambda i: (i - 4) % (4 * nz))
            ring[k] = down

    query, grad, expo, spread, stats, ratio = attend(
        where, ring, kv_half, own_keys, other_keys, scale * LOG2E
    )

    joined = stats
    projected = []
    pairings = [other_x_lo] + [lambda i, k=k: i ^ (4 << k) for k in range(nz.bit_length() - 1)]
    for p, pairing in enumerate(pairings):
        if p:
            joined = join(joined, last)
        last = permute(joined, "ctx", pairing)
        if p < half // 2:
            terms = project(p, own_t, other_t, spread, expo, kv_half, q_width)
            last, *terms = lax.optimization_barrier((last, *terms))
            projected += terms
    dq_keep, dq_send, with_spread, with_expo = weigh(
        where, pair_lens, joined, last, stats, ratio, query, grad, projected, scale, nz, q_dev
    )
    dq_pair = permute(dq_send, "ctx", other_x_lo)
    steps = (2, 1, 3, 0)
    order = jnp.stack([(y + k) & (ny - 1) for k in steps]).astype(jnp.int32)
    keys = p_dev // (2 * ny)
    shape = (2, 2, ny, keys, spread.shape[1])
    operands = (d_lat, spread.reshape(shape), expo.reshape(shape), with_spread, with_expo)
    sends = [cache_terms(1, order[k : k + 2], *operands, (BF16, BF16)) for k in (0, 2)]
    adds = [[permute(x, "ctx", other_core) for x in send] for send in sends]
    blocks = cache_terms(0, order[:2], *operands, (BF16, BF16), adds[0])
    dq = (dq_keep.astype(F32) + dq_pair.astype(F32)).astype(BF16)
    *blocks, dq = lax.optimization_barrier((*blocks, dq))
    last_block, total = cache_terms(0, order[2:], *operands, (BF16, F32), adds[1])
    blocks = [*blocks, last_block]
    arrived = [
        permute(block, "head", lambda i, k=k: (i // ny) * ny + (i + k) % ny)
        for block, k in zip(blocks, steps)
    ]

    for part in arrived:
        total = total + part.astype(F32)
    total = jnp.stack(
        [
            jnp.concatenate(
                [
                    total[:, i * d_lat : (i + 1) * d_lat],
                    total[:, 2 * d_lat + i * d_rope : 2 * d_lat + (i + 1) * d_rope],
                ],
                axis=1,
            )
            for i in range(2)
        ]
    )
    across = permute(
        pick(total, 1 - x_hi, 0).astype(BF16), "head", lambda i: (i + ny) % (2 * ny)
    )

    dq = lax.all_to_all(dq, "ctx", 0, 0, axis_index_groups=z_groups)
    dq = jnp.sum(dq.astype(F32), axis=0).astype(BF16).reshape(half, 2, q_dev, q_width)
    theirs = permute(dq[:, 1], "ctx", other_core)
    query_grad = jnp.transpose(in_order(dq[:, 0], theirs, core == 1, 0), (1, 0, 2))

    cache_grad = (pick(total, x_hi, 0) + across.astype(F32)).astype(BF16)
    return (query_grad, cache_grad)


def solution(mesh):
    placed = (
        P("ctx", "head", None),
        P("ctx", "head", None),
        P("head", None, None),
        P("ctx", None),
        P("ctx"),
        P(),
        P(),
    )
    return jax.shard_map(
        per_device,
        mesh=mesh,
        in_specs=placed,
        out_specs=(P("ctx", "head", None), P(("ctx", "head"), None)),
        check_vma=False,
    )
```

```python
import functools

import jax
import jax.numpy as jnp
from jax import lax
from jax.experimental import pallas as pl
from jax.experimental.pallas import tpu as pltpu
from jax.sharding import PartitionSpec as P

BETA = 0.1
LOSS_SCALE = 2048.0
LOG2E = 1.4426950408889634
NEVER = -1e30
FLOOR = -1e29
F32 = jnp.float32
BF16 = jnp.bfloat16
CHUNK = 256
TOGETHER = 4
PACKED = 384
MIB = 1024 * 1024
ATTEND_MIB = 24
PROJECT_MIB = 8
WEIGH_MIB = 16
CACHE_MIB = 20


def permute(x, axis, to):
    return lax.ppermute(x, axis, [(i, to(i)) for i in range(lax.axis_size(axis))])


def in_order(mine, theirs, second, axis):
    return jnp.where(
        second,
        jnp.concatenate([theirs, mine], axis),
        jnp.concatenate([mine, theirs], axis),
    )


def join_stats(first, second):
    top = jnp.maximum(first[0:1], second[0:1])
    both = jnp.exp2(first[0:1] - top) * first + jnp.exp2(second[0:1] - top) * second
    return jnp.where(lax.broadcasted_iota(jnp.int32, both.shape, 0) == 0, top, both)


def join_kernel(first_ref, second_ref, out_ref):
    out_ref[...] = join_stats(first_ref[...], second_ref[...])


def join(first, second):
    vmem = pl.BlockSpec(memory_space=pltpu.VMEM)
    return pl.pallas_call(
        join_kernel,
        out_shape=jax.ShapeDtypeStruct(first.shape, F32),
        in_specs=[vmem, vmem],
        out_specs=vmem,
        compiler_params=pltpu.CompilerParams(vmem_limit_bytes=MIB),
    )(first, second)


def against(x, y):
    return lax.dot_general(x, y, (((1,), (1,)), ((), ())), preferred_element_type=F32)


def pack_kernel(where_ref, ratio_ref, queries_ref, out_grad_ref, mine_ref, theirs_ref):
    q_dev, heads, q_width = queries_ref.shape
    d_nope = out_grad_ref.shape[2]
    half = heads // 2
    d_rope = q_width - d_nope
    lane = lax.broadcasted_iota(jnp.int32, (heads, PACKED - 2 * d_nope - d_rope), 1)
    second = where_ref[0] == 1
    mine, theirs = [], []
    for j in range(q_dev):
        query = queries_ref[j].astype(F32)
        ratio = jnp.full(lane.shape, ratio_ref[j], F32)
        high = ratio.astype(BF16).astype(F32)
        middle = (ratio - high).astype(BF16).astype(F32)
        terms = jnp.where(lane == 0, high, jnp.where(lane == 1, middle, ratio - high - middle))
        terms = jnp.where(lane < 3, terms, 0.0)
        row = [query[:, :d_nope], out_grad_ref[j].astype(F32), query[:, d_nope:], terms]
        row = jnp.concatenate(row, axis=1)
        mine.append(jnp.where(second, row[half:], row[:half]))
        theirs.append(jnp.where(second, row[:half], row[half:]))
    mine_ref[...] = jnp.concatenate(mine, axis=0).astype(BF16)
    theirs_ref[...] = jnp.concatenate(theirs, axis=0).astype(BF16)


def pack(where, token_ratio, queries, out_grad):
    q_dev, heads = queries.shape[:2]
    smem = pl.BlockSpec(memory_space=pltpu.SMEM)
    vmem = pl.BlockSpec(memory_space=pltpu.VMEM)
    packed = jax.ShapeDtypeStruct((q_dev * heads // 2, PACKED), BF16)
    return pl.pallas_call(
        pack_kernel,
        out_shape=(packed, packed),
        in_specs=[smem, smem, vmem, vmem],
        out_specs=[vmem, vmem],
        compiler_params=pltpu.CompilerParams(vmem_limit_bytes=2 * MIB),
        cost_estimate=pl.CostEstimate(flops=0, bytes_accessed=32 * MIB, transcendentals=0),
    )(where, token_ratio, queries, out_grad)


def stage_kernel(cache_ref, out_ref):
    out_ref[...] = cache_ref[...].T


def stage(cache_t):
    c_width, keys = cache_t.shape
    vmem = pl.BlockSpec(memory_space=pltpu.VMEM)
    return pl.pallas_call(
        stage_kernel,
        out_shape=jax.ShapeDtypeStruct((keys, c_width), BF16),
        in_specs=[vmem],
        out_specs=vmem,
        compiler_params=pltpu.CompilerParams(vmem_limit_bytes=6 * MIB),
        cost_estimate=pl.CostEstimate(
            flops=keys * c_width, bytes_accessed=4 * keys * c_width, transcendentals=0
        ),
    )(cache_t)


def attend_kernel(score_scale, blocks, together, where_ref, *refs):
    ring_refs, refs = refs[:blocks], refs[blocks:]
    kv_ref, own_ref, other_ref, query_ref, grad_ref, expo_ref, spread_ref, stats_ref = refs[:8]
    ratio_ref, raw, expo, dprod = refs[8:]
    size = ring_refs[0].shape[0]
    half, d_lat, d_nope = kv_ref.shape[0] // 2, kv_ref.shape[1], kv_ref.shape[2] // 2
    rows = size * blocks // half
    first_head = where_ref[0] * half
    d_rope = query_ref.shape[1] - d_lat
    keys = own_ref.shape[0]
    width = together * rows
    for k in range(blocks):
        first = pl.multiple_of(where_ref[4 + k] * size, size)
        for part in range(PACKED // 128):
            lanes = slice(part * 128, (part + 1) * 128)
            raw[part, pl.ds(first, size), :] = ring_refs[k][:, lanes].astype(F32)

    def of_head(h, part):
        return raw[part, pl.ds(h, rows, stride=half), :]

    terms = of_head(0, 2)
    lane = lax.broadcasted_iota(jnp.int32, terms.shape, 1)
    terms = jnp.where((lane >= d_rope) & (lane < d_rope + 3), terms, 0.0)
    ratio_ref[...] = jnp.broadcast_to(jnp.sum(terms, axis=1, keepdims=True), ratio_ref.shape)

    def fold(x, join):
        return join(join(x.reshape(CHUNK // 8, 8, width), axis=0), axis=0, keepdims=True)

    for p in range(half // together):
        for h in range(p * together, (p + 1) * together):
            at = slice(h * rows, (h + 1) * rows)
            lat = against(of_head(h, 0).astype(BF16), kv_ref[first_head + h, :, :d_nope])
            query_ref[at, :d_lat] = lat.astype(BF16)
            rope = of_head(h, 2)[:, :d_rope]
            query_ref[at, d_lat:] = rope.astype(BF16)
            lat = against(of_head(h, 1).astype(BF16), kv_ref[first_head + h, :, d_nope:])
            grad_ref[at, :] = lat.astype(BF16)
        columns = slice(p * width, (p + 1) * width)
        tops, masses, dsums = [], [], []
        for c in range(2 * keys // CHUNK):
            first = c * CHUNK % keys
            ref, base = (own_ref, where_ref[1]) if c * CHUNK < keys else (other_ref, where_ref[2])
            score = against(ref[first : first + CHUNK, :], query_ref[columns, :]) * score_scale
            dp = against(ref[first : first + CHUNK, :d_lat], grad_ref[columns, :])
            key = base + first + lax.broadcasted_iota(jnp.int32, (CHUNK, 1), 0)
            score = jnp.where(key < where_ref[3], score, NEVER)
            top = jnp.maximum(fold(score, jnp.max), FLOOR)
            value = jnp.exp2(score - top)
            at = slice(c * CHUNK, (c + 1) * CHUNK)
            expo[at] = value
            dprod[at] = dp
            tops.append(top)
            masses.append(fold(value, jnp.sum))
            dsums.append(fold(value * dp, jnp.sum))
        top = functools.reduce(jnp.maximum, tops)
        factors = [jnp.exp2(t - top) for t in tops]
        mass = sum(f * m for f, m in zip(factors, masses))
        dsum = sum(f * d for f, d in zip(factors, dsums))
        centre = dsum / jnp.maximum(mass, 1e-30)
        for c, f in enumerate(factors):
            at = slice(c * CHUNK, (c + 1) * CHUNK)
            value = expo[at] * f
            expo_ref[at, columns] = value.astype(BF16)
            spread_ref[at, columns] = (value * (dprod[at] - centre)).astype(BF16)
        stats_ref[0:1, columns] = top
        stats_ref[1:2, columns] = mass
        stats_ref[2:3, columns] = dsum


def attend(where, ring, kv_up, own, other, score_scale, together=TOGETHER):
    blocks, (size, packed) = len(ring), ring[0].shape
    half, d_lat = kv_up.shape[0] // 2, kv_up.shape[1]
    total = blocks * size
    rows = total // half
    keys, c_width = own.shape
    smem = pl.BlockSpec(memory_space=pltpu.SMEM)
    vmem = pl.BlockSpec(memory_space=pltpu.VMEM)
    return pl.pallas_call(
        functools.partial(attend_kernel, score_scale, blocks, together),
        out_shape=(
            jax.ShapeDtypeStruct((total, c_width), BF16),
            jax.ShapeDtypeStruct((total, d_lat), BF16),
            jax.ShapeDtypeStruct((2 * keys, total), BF16),
            jax.ShapeDtypeStruct((2 * keys, total), BF16),
            jax.ShapeDtypeStruct((3, total), F32),
            jax.ShapeDtypeStruct((rows, 128), F32),
        ),
        in_specs=[smem] + [vmem] * (blocks + 3),
        out_specs=[vmem] * 6,
        scratch_shapes=[
            pltpu.VMEM((packed // 128, total, 128), F32),
            pltpu.VMEM((2 * keys, together * rows), F32),
            pltpu.VMEM((2 * keys, together * rows), F32),
        ],
        compiler_params=pltpu.CompilerParams(vmem_limit_bytes=ATTEND_MIB * MIB),
        cost_estimate=pl.CostEstimate(
            flops=2 * 2 * keys * total * (c_width + d_lat),
            bytes_accessed=8 * keys * total,
            transcendentals=2 * keys * total,
        ),
    )(where, *ring, kv_up, own, other)


def project_kernel(p, where_ref, own_ref, other_ref, spread_ref, expo_ref, kv_ref, *out_refs):
    d_lat, d_nope = kv_ref.shape[1], kv_ref.shape[2] // 2
    keys = own_ref.shape[1]
    width = out_refs[0].shape[0]
    half = kv_ref.shape[0] // 2
    rows = spread_ref.shape[1] // half
    first_head = where_ref[0] * half + p * (width // rows)
    columns = slice(p * width, (p + 1) * width)
    for terms_ref, out_ref in zip((spread_ref, expo_ref), out_refs):
        full = jnp.dot(own_ref[...], terms_ref[:keys, columns], preferred_element_type=F32)
        full = full + jnp.dot(
            other_ref[...], terms_ref[keys:, columns], preferred_element_type=F32
        )
        for j in range(width // rows):
            at = slice(j * rows, (j + 1) * rows)
            out_ref[at, :d_nope] = lax.dot_general(
                full[:d_lat, at].astype(BF16),
                kv_ref[first_head + j, :, :d_nope],
                (((0,), (0,)), ((), ())),
                preferred_element_type=F32,
            )
            out_ref[at, d_nope:] = full[d_lat:, at].T


def project(p, where, own_t, other_t, spread, expo, kv_up, q_width):
    c_width, keys = own_t.shape
    width = 4 * spread.shape[1] // kv_up.shape[0]
    smem = pl.BlockSpec(memory_space=pltpu.SMEM)
    vmem = pl.BlockSpec(memory_space=pltpu.VMEM)
    return pl.pallas_call(
        functools.partial(project_kernel, p),
        out_shape=(jax.ShapeDtypeStruct((width, q_width), F32),) * 2,
        in_specs=[smem] + [vmem] * 5,
        out_specs=[vmem] * 2,
        compiler_params=pltpu.CompilerParams(vmem_limit_bytes=PROJECT_MIB * MIB),
        cost_estimate=pl.CostEstimate(
            flops=8 * keys * width * c_width, bytes_accessed=8 * keys * width, transcendentals=0
        ),
    )(where, own_t, other_t, spread, expo, kv_up)


def row_gains(where_ref, lens_ref, ratio_ref, rows_of_core):
    rows = ratio_ref.shape[0]
    place = lax.broadcasted_iota(jnp.int32, (rows, 1), 0)
    turn = place % (2 * rows_of_core) >= rows_of_core
    swapped = jnp.where(turn, place - rows_of_core, place + rows_of_core)
    place = jnp.where(where_ref[0] == 1, swapped, place)
    ratio = ratio_ref[:, 0:1]
    segments = lens_ref.shape[0]
    members = []
    first = jnp.int32(0)
    for k in range(segments):
        last = first + lens_ref[k]
        members.append((place >= first) & (place < last))
        first = last
    sums = [jnp.sum(jnp.where(m, ratio, 0.0), axis=0, keepdims=True) for m in members]
    gains = jnp.zeros((rows, 1), F32)
    for p in range(segments // 2):
        margin = BETA * (sums[2 * p] - sums[2 * p + 1])
        weight = LOSS_SCALE * BETA / (1.0 + jnp.exp(margin))
        gains = jnp.where(members[2 * p], -weight, gains)
        gains = jnp.where(members[2 * p + 1], weight, gains)
    return gains


def weigh_kernel(scale, rows_of_core, where_ref, lens_ref, *refs):
    (joined_ref, last_ref, own_ref, ratio_ref, query_ref, grad_ref) = refs[:6]
    by_spread_refs, by_expo_refs = refs[6:-4:2], refs[7:-4:2]
    dq_keep_ref, dq_send_ref, with_spread_ref, with_expo_ref = refs[-4:]
    total = query_ref.shape[0]
    d_lat = grad_ref.shape[1]
    rows = ratio_ref.shape[0]
    half = total // rows
    gains = row_gains(where_ref, lens_ref, ratio_ref, rows_of_core)
    joined = join_stats(joined_ref[...], last_ref[...])
    centre = own_ref[2:3] / jnp.maximum(own_ref[1:2], 1e-30)
    factor = jnp.exp2(own_ref[0:1] - joined[0:1]) / joined[1:2]
    shift = joined[2:3] / joined[1:2] - centre
    sublane = lax.broadcasted_iota(jnp.int32, (8, total), 0)
    both = jnp.where(sublane == 0, factor, shift).T
    blocks, size = dq_keep_ref.shape[0], dq_keep_ref.shape[2] // 2
    second = where_ref[4 + blocks] == 1
    for h in range(half):
        at = slice(h * rows, (h + 1) * rows)
        part = slice((h % 2) * rows, (h % 2 + 1) * rows)
        factor = both[at, 0:1] * gains
        shift = both[at, 1:2]
        scaled = scale * factor
        dq = by_spread_refs[h // 2][part, :] - shift * by_expo_refs[h // 2][part, :]
        dq = scaled * dq
        if h % 2:
            for b in range(blocks):
                pieces = []
                for x in range(2):
                    first = (2 * b + x) * size
                    at_x = slice(first, first + size)
                    pieces.append(jnp.concatenate([before[at_x], dq[at_x]], axis=0))
                dq_keep_ref[b, h // 2] = jnp.where(second, pieces[1], pieces[0]).astype(BF16)
                dq_send_ref[b, h // 2] = jnp.where(second, pieces[0], pieces[1]).astype(BF16)
        before = dq
        query = scaled * query_ref[at, :].astype(F32)
        with_spread_ref[at, :] = query.astype(BF16)
        moved = shift * query
        with_expo_ref[at, :d_lat] = (
            factor * grad_ref[at, :].astype(F32) - moved[:, :d_lat]
        ).astype(BF16)
        with_expo_ref[at, d_lat:] = (-moved[:, d_lat:]).astype(BF16)


def weigh(where, lens, joined, last, stats, ratio, query, grad, projected, scale, blocks, q_dev):
    total, c_width = query.shape
    rows = ratio.shape[0]
    q_width = projected[0].shape[1]
    half = total // rows
    smem = pl.BlockSpec(memory_space=pltpu.SMEM)
    vmem = pl.BlockSpec(memory_space=pltpu.VMEM)
    dq = jax.ShapeDtypeStruct((blocks, half // 2, rows // blocks, q_width), BF16)
    weight = jax.ShapeDtypeStruct((total, c_width), BF16)
    inputs = (joined, last, stats, ratio, query, grad, *projected)
    return pl.pallas_call(
        functools.partial(weigh_kernel, scale, q_dev),
        out_shape=(dq, dq, weight, weight),
        in_specs=[smem, smem] + [vmem] * len(inputs),
        out_specs=[vmem] * 4,
        compiler_params=pltpu.CompilerParams(vmem_limit_bytes=WEIGH_MIB * MIB),
        cost_estimate=pl.CostEstimate(
            flops=10 * total * c_width, bytes_accessed=8 * total * c_width, transcendentals=0
        ),
    )(where, lens, *inputs)


def cache_kernel(part, d_lat, order_ref, spread_ref, expo_ref, with_spread_ref, with_expo_ref, *refs):
    adds, outs = refs[:-2], refs[-2:]
    keys = spread_ref.shape[3]

    def gather(ref):
        blocks = [ref[part, order_ref[i], order_ref[4 + i]] for i in range(4)]
        return jnp.concatenate(blocks, axis=0)

    out = jnp.dot(gather(spread_ref), with_spread_ref[...], preferred_element_type=F32)
    out = out + jnp.dot(gather(expo_ref), with_expo_ref[...], preferred_element_type=F32)
    rope = out.shape[1] - d_lat
    for i in range(4):
        first = (i % 2) * d_lat
        lat = slice(first, first + d_lat)
        first = 2 * d_lat + (i % 2) * rope
        tail = slice(first, first + rope)
        at = slice(i * keys, (i + 1) * keys)
        for lanes, value in ((lat, out[at, :d_lat]), (tail, out[at, d_lat:])):
            if adds:
                value = value + adds[i // 2][:, lanes].astype(F32)
            outs[i // 2][:, lanes] = value.astype(outs[i // 2].dtype)


def cache_terms(part, order, d_lat, spread, expo, with_spread, with_expo, dtypes, adds=()):
    total, c_width = with_spread.shape
    keys = spread.shape[3]
    smem = pl.BlockSpec(memory_space=pltpu.SMEM)
    vmem = pl.BlockSpec(memory_space=pltpu.VMEM)
    return pl.pallas_call(
        functools.partial(cache_kernel, part, d_lat),
        out_shape=[jax.ShapeDtypeStruct((keys, 2 * c_width), dtype) for dtype in dtypes],
        in_specs=[smem] + [vmem] * (4 + len(adds)),
        out_specs=[vmem, vmem],
        compiler_params=pltpu.CompilerParams(vmem_limit_bytes=CACHE_MIB * MIB),
        cost_estimate=pl.CostEstimate(
            flops=16 * keys * total * c_width,
            bytes_accessed=16 * keys * total,
            transcendentals=0,
        ),
    )(order, spread, expo, with_spread, with_expo, *adds)


def unfold(x, d_lat):
    rope = x.shape[1] // 2 - d_lat
    return [
        jnp.concatenate(
            [
                x[:, i * d_lat : (i + 1) * d_lat],
                x[:, 2 * d_lat + i * rope : 2 * d_lat + (i + 1) * rope],
            ],
            axis=1,
        )
        for i in range(2)
    ]


def fold_rows(x, d_lat, out_ref):
    size = x.shape[0] // 2
    rope = x.shape[1] - d_lat
    for i in range(2):
        part = x[i * size : (i + 1) * size].astype(BF16)
        out_ref[:, i * d_lat : (i + 1) * d_lat] = part[:, :d_lat]
        out_ref[:, 2 * d_lat + i * rope : 2 * d_lat + (i + 1) * rope] = part[:, d_lat:]


def forward_kernel(d_lat, keep_ref, arrived_ref, *out_refs):
    total = keep_ref[...].astype(F32) + arrived_ref[...].astype(F32)
    for block, out_ref in zip(unfold(total, d_lat), out_refs):
        fold_rows(block, d_lat, out_ref)


def turn_kernel(d_lat, own_ref, arrived_ref, send_ref, keep_ref):
    send, keep = unfold(own_ref[...] + arrived_ref[...].astype(F32), d_lat)
    fold_rows(send, d_lat, send_ref)
    keep_ref[...] = keep


def finish_kernel(d_lat, keep_ref, *refs):
    total = keep_ref[...]
    for arrived_ref in refs[:-1]:
        total = total + jnp.concatenate(unfold(arrived_ref[...].astype(F32), d_lat), axis=0)
    refs[-1][...] = total.T.astype(BF16)


def small(kernel, out_shape, *operands):
    vmem = pl.BlockSpec(memory_space=pltpu.VMEM)
    return pl.pallas_call(
        kernel,
        out_shape=out_shape,
        in_specs=[vmem] * len(operands),
        out_specs=jax.tree.map(lambda _: vmem, out_shape),
        compiler_params=pltpu.CompilerParams(vmem_limit_bytes=6 * MIB),
    )(*operands)


def per_device(queries, out_grad, kv_up, latent_cache, token_ratio, pair_lens, prompt_len):
    ctx_index = lax.axis_index("ctx")
    head_index = lax.axis_index("head")
    core = ctx_index & 1
    x_lo = (ctx_index >> 1) & 1
    z = ctx_index >> 2
    nz = lax.axis_size("ctx") // 4
    ny = lax.axis_size("head") // 2
    y = head_index & (ny - 1)
    x_hi = (head_index >= ny).astype(jnp.int32)
    other_core = lambda i: i ^ 1
    other_x_lo = lambda i: i ^ 2
    z_groups = [[4 * k + j for k in range(nz)] for j in range(4)]

    q_dev, heads, q_width = queries.shape
    p_dev, c_width = latent_cache.shape
    d_lat = kv_up.shape[1]
    d_rope = c_width - d_lat
    d_nope = q_width - d_rope
    half = heads // 2
    scale = q_width ** (-0.5)

    where = [core, ctx_index * p_dev, (ctx_index ^ 1) * p_dev, prompt_len[0]]
    where = where + [(z + k) & (nz - 1) for k in range(nz)] + [x_lo]
    where = jnp.stack(where).astype(jnp.int32)
    own_t = latent_cache.T
    other_t = permute(latent_cache, "ctx", other_core).T
    mine, theirs = pack(where, token_ratio, queries, out_grad)
    own_keys = stage(own_t)
    other_keys = stage(other_t)
    block = jnp.concatenate([mine, permute(theirs, "ctx", other_core)], 0)
    block = in_order(block, permute(block, "ctx", other_x_lo), x_lo == 1, 0)
    up = down = block
    ring = [block] + [None] * (nz - 1)
    for k in range(1, nz // 2 + 1):
        up = permute(up, "ctx", lambda i: (i + 4) % (4 * nz))
        ring[nz - k] = up
        if k < nz // 2:
            down = permute(down, "ctx", lambda i: (i - 4) % (4 * nz))
            ring[k] = down

    query, grad, expo, spread, stats, ratio = attend(
        where, ring, kv_up, own_keys, other_keys, scale * LOG2E
    )

    joined = stats
    projected = []
    pairings = [other_x_lo] + [lambda i, k=k: i ^ (4 << k) for k in range(nz.bit_length() - 1)]
    for p, pairing in enumerate(pairings):
        if p:
            joined = join(joined, last)
        last = permute(joined, "ctx", pairing)
        if p < half // 2:
            terms = project(p, where, own_t, other_t, spread, expo, kv_up, q_width)
            last, *terms = lax.optimization_barrier((last, *terms))
            projected += terms
    dq_keep, dq_send, with_spread, with_expo = weigh(
        where, pair_lens, joined, last, stats, ratio, query, grad, projected, scale, nz, q_dev
    )
    dq_pair = permute(dq_send, "ctx", other_x_lo)
    keys = p_dev // (2 * ny)
    there, here = 1 - x_hi, x_hi
    along = [(y + k) & (ny - 1) for k in (0, 1, 2, 3)]
    orders = [
        [there, there, here, here, along[2], along[1], along[2], along[1]],
        [there, here, there, here, along[3], along[3], along[0], along[0]],
    ]
    orders = [jnp.stack(order).astype(jnp.int32) for order in orders]
    shape = (2, 2, ny, keys, spread.shape[1])
    operands = (d_lat, spread.reshape(shape), expo.reshape(shape), with_spread, with_expo)
    adds = []
    sends = cache_terms(1, orders[0], *operands, (BF16, BF16))
    later, *sends = lax.optimization_barrier((orders[1], *sends))
    adds.append([permute(x, "ctx", other_core) for x in sends])
    sends = cache_terms(1, later, *operands, (BF16, BF16))
    adds.append([permute(x, "ctx", other_core) for x in sends])
    to_x_hi = lambda x: permute(x, "head", lambda i: (i + ny) % (2 * ny))
    to_y = lambda x, k: permute(x, "head", lambda i: (i // ny) * ny + (i + k) % ny)
    send, keep = cache_terms(0, orders[0], *operands, (BF16, F32), adds[0])
    later, send = lax.optimization_barrier((orders[1], send))
    from_x_hi = to_x_hi(send)
    send, own = cache_terms(0, later, *operands, (BF16, F32), adds[1])
    dq = (dq_keep.astype(F32) + dq_pair.astype(F32)).astype(BF16)
    send, dq = lax.optimization_barrier((send, dq))
    from_y = to_y(send, 3)

    half_rows = jax.ShapeDtypeStruct((keys // 2, 2 * c_width), BF16)
    block = jax.ShapeDtypeStruct((keys, c_width), F32)
    sends = small(
        functools.partial(forward_kernel, d_lat), (half_rows, half_rows), keep, from_x_hi
    )
    arrived = [to_y(sends[0], 2), to_y(sends[1], 1)]
    send, keep = small(functools.partial(turn_kernel, d_lat), (half_rows, block), own, from_y)
    arrived.append(to_x_hi(send))
    cache_grad = small(
        functools.partial(finish_kernel, d_lat),
        jax.ShapeDtypeStruct((c_width, keys), BF16),
        keep,
        *arrived,
    ).T

    dq = lax.all_to_all(dq, "ctx", 0, 0, axis_index_groups=z_groups)
    dq = jnp.sum(dq.astype(F32), axis=0).astype(BF16).reshape(half, 2, q_dev, q_width)
    theirs = permute(dq[:, 1], "ctx", other_core)
    query_grad = jnp.transpose(in_order(dq[:, 0], theirs, core == 1, 0), (1, 0, 2))

    return (query_grad, cache_grad)


def solution(mesh):
    placed = (
        P("ctx", "head", None),
        P("ctx", "head", None),
        P("head", None, None),
        P("ctx", None),
        P("ctx"),
        P(),
        P(),
    )
    return jax.shard_map(
        per_device,
        mesh=mesh,
        in_specs=placed,
        out_specs=(P("ctx", "head", None), P(("ctx", "head"), None)),
        check_vma=False,
    )
```

```python
import functools

import jax
import jax.numpy as jnp
from jax import lax
from jax.experimental import pallas as pl
from jax.experimental.pallas import tpu as pltpu
from jax.sharding import PartitionSpec as P

BETA = 0.1
LOSS_SCALE = 2048.0
LOG2E = 1.4426950408889634
NEVER = -1e30
FLOOR = -1e29
F32 = jnp.float32
BF16 = jnp.bfloat16
CHUNK = 256
TOGETHER = 4
PACKED = 384
MIB = 1024 * 1024
ATTEND_MIB = 24
PROJECT_MIB = 8
WEIGH_MIB = 16
CACHE_MIB = 20


def permute(x, axis, to):
    return lax.ppermute(x, axis, [(i, to(i)) for i in range(lax.axis_size(axis))])


def in_order(mine, theirs, second, axis):
    return jnp.where(
        second,
        jnp.concatenate([theirs, mine], axis),
        jnp.concatenate([mine, theirs], axis),
    )


def join_stats(first, second):
    top = jnp.maximum(first[0:1], second[0:1])
    both = jnp.exp2(first[0:1] - top) * first + jnp.exp2(second[0:1] - top) * second
    return jnp.where(lax.broadcasted_iota(jnp.int32, both.shape, 0) == 0, top, both)


def join_kernel(first_ref, second_ref, out_ref):
    out_ref[...] = join_stats(first_ref[...], second_ref[...])


def join(first, second):
    vmem = pl.BlockSpec(memory_space=pltpu.VMEM)
    return pl.pallas_call(
        join_kernel,
        out_shape=jax.ShapeDtypeStruct(first.shape, F32),
        in_specs=[vmem, vmem],
        out_specs=vmem,
        compiler_params=pltpu.CompilerParams(vmem_limit_bytes=MIB),
    )(first, second)


def against(x, y):
    return lax.dot_general(x, y, (((1,), (1,)), ((), ())), preferred_element_type=F32)


def pack_kernel(where_ref, ratio_ref, queries_ref, out_grad_ref, mine_ref, theirs_ref):
    q_dev, heads, q_width = queries_ref.shape
    d_nope = out_grad_ref.shape[2]
    half = heads // 2
    d_rope = q_width - d_nope
    lane = lax.broadcasted_iota(jnp.int32, (heads, PACKED - 2 * d_nope - d_rope), 1)
    second = where_ref[0] == 1
    mine, theirs = [], []
    for j in range(q_dev):
        query = queries_ref[j].astype(F32)
        ratio = jnp.full(lane.shape, ratio_ref[j], F32)
        high = ratio.astype(BF16).astype(F32)
        middle = (ratio - high).astype(BF16).astype(F32)
        terms = jnp.where(lane == 0, high, jnp.where(lane == 1, middle, ratio - high - middle))
        terms = jnp.where(lane < 3, terms, 0.0)
        row = [query[:, :d_nope], out_grad_ref[j].astype(F32), query[:, d_nope:], terms]
        row = jnp.concatenate(row, axis=1)
        mine.append(jnp.where(second, row[half:], row[:half]))
        theirs.append(jnp.where(second, row[:half], row[half:]))
    mine_ref[...] = jnp.concatenate(mine, axis=0).astype(BF16)
    theirs_ref[...] = jnp.concatenate(theirs, axis=0).astype(BF16)


def pack(where, token_ratio, queries, out_grad):
    q_dev, heads = queries.shape[:2]
    smem = pl.BlockSpec(memory_space=pltpu.SMEM)
    vmem = pl.BlockSpec(memory_space=pltpu.VMEM)
    packed = jax.ShapeDtypeStruct((q_dev * heads // 2, PACKED), BF16)
    return pl.pallas_call(
        pack_kernel,
        out_shape=(packed, packed),
        in_specs=[smem, smem, vmem, vmem],
        out_specs=[vmem, vmem],
        compiler_params=pltpu.CompilerParams(vmem_limit_bytes=63 * MIB),
        cost_estimate=pl.CostEstimate(flops=0, bytes_accessed=32 * MIB, transcendentals=0),
    )(where, token_ratio, queries, out_grad)


def stage_kernel(cache_ref, out_ref):
    out_ref[...] = cache_ref[...].T


def stage(cache_t):
    c_width, keys = cache_t.shape
    vmem = pl.BlockSpec(memory_space=pltpu.VMEM)
    return pl.pallas_call(
        stage_kernel,
        out_shape=jax.ShapeDtypeStruct((keys, c_width), BF16),
        in_specs=[vmem],
        out_specs=vmem,
        compiler_params=pltpu.CompilerParams(vmem_limit_bytes=6 * MIB),
        cost_estimate=pl.CostEstimate(
            flops=keys * c_width, bytes_accessed=4 * keys * c_width, transcendentals=0
        ),
    )(cache_t)


def attend_kernel(score_scale, blocks, together, where_ref, *refs):
    ring_refs, refs = refs[:blocks], refs[blocks:]
    kv_ref, own_ref, other_ref, query_ref, grad_ref, expo_ref, spread_ref, stats_ref = refs[:8]
    ratio_ref, key_ref, raw, expo, dprod = refs[8:]
    size = ring_refs[0].shape[0]
    half, d_lat, d_nope = kv_ref.shape[0] // 2, kv_ref.shape[1], kv_ref.shape[2] // 2
    rows = size * blocks // half
    first_head = where_ref[0] * half
    d_rope = query_ref.shape[1] - d_lat
    keys = own_ref.shape[0]
    width = together * rows
    for k in range(blocks):
        first = pl.multiple_of(where_ref[4 + k] * size, size)
        for part in range(PACKED // 128):
            lanes = slice(part * 128, (part + 1) * 128)
            raw[part, pl.ds(first, size), :] = ring_refs[k][:, lanes].astype(F32)

    def of_head(h, part):
        return raw[part, pl.ds(h, rows, stride=half), :]

    terms = of_head(0, 2)
    lane = lax.broadcasted_iota(jnp.int32, terms.shape, 1)
    terms = jnp.where((lane >= d_rope) & (lane < d_rope + 3), terms, 0.0)
    ratio_ref[...] = jnp.broadcast_to(jnp.sum(terms, axis=1, keepdims=True), ratio_ref.shape)

    def fold(x, join):
        return join(join(x.reshape(CHUNK // 8, 8, width), axis=0), axis=0, keepdims=True)

    def group(p, carry):
        for j in range(together):
            h = p * together + j
            at = pl.ds(pl.multiple_of(h * rows, rows), rows)
            key_ref[h] = kv_ref[first_head + h, :, :d_nope]
            lat = against(of_head(h, 0).astype(BF16), key_ref[h])
            query_ref[at, :d_lat] = lat.astype(BF16)
            rope = of_head(h, 2)[:, :d_rope]
            query_ref[at, d_lat:] = rope.astype(BF16)
            lat = against(of_head(h, 1).astype(BF16), kv_ref[first_head + h, :, d_nope:])
            grad_ref[at, :] = lat.astype(BF16)
        columns = pl.ds(pl.multiple_of(p * width, width), width)
        tops, masses, dsums = [], [], []
        for c in range(2 * keys // CHUNK):
            first = c * CHUNK % keys
            ref, base = (own_ref, where_ref[1]) if c * CHUNK < keys else (other_ref, where_ref[2])
            score = against(ref[first : first + CHUNK, :], query_ref[columns, :]) * score_scale
            dp = against(ref[first : first + CHUNK, :d_lat], grad_ref[columns, :])
            key = base + first + lax.broadcasted_iota(jnp.int32, (CHUNK, 1), 0)
            score = jnp.where(key < where_ref[3], score, NEVER)
            top = jnp.maximum(fold(score, jnp.max), FLOOR)
            value = jnp.exp2(score - top)
            at = slice(c * CHUNK, (c + 1) * CHUNK)
            expo[at] = value
            dprod[at] = dp
            tops.append(top)
            masses.append(fold(value, jnp.sum))
            dsums.append(fold(value * dp, jnp.sum))
        top = functools.reduce(jnp.maximum, tops)
        factors = [jnp.exp2(t - top) for t in tops]
        mass = sum(f * m for f, m in zip(factors, masses))
        dsum = sum(f * d for f, d in zip(factors, dsums))
        centre = dsum / jnp.maximum(mass, 1e-30)
        for c, f in enumerate(factors):
            at = slice(c * CHUNK, (c + 1) * CHUNK)
            value = expo[at] * f
            expo_ref[at, columns] = value.astype(BF16)
            spread_ref[at, columns] = (value * (dprod[at] - centre)).astype(BF16)
        stats_ref[0:1, columns] = top
        stats_ref[1:2, columns] = mass
        stats_ref[2:3, columns] = dsum
        return carry

    lax.fori_loop(0, half // together, group, 0)


def attend(where, ring, kv_up, own, other, score_scale, together=TOGETHER):
    blocks, (size, packed) = len(ring), ring[0].shape
    half, d_lat = kv_up.shape[0] // 2, kv_up.shape[1]
    total = blocks * size
    rows = total // half
    keys, c_width = own.shape
    smem = pl.BlockSpec(memory_space=pltpu.SMEM)
    vmem = pl.BlockSpec(memory_space=pltpu.VMEM)
    return pl.pallas_call(
        functools.partial(attend_kernel, score_scale, blocks, together),
        out_shape=(
            jax.ShapeDtypeStruct((total, c_width), BF16),
            jax.ShapeDtypeStruct((total, d_lat), BF16),
            jax.ShapeDtypeStruct((2 * keys, total), BF16),
            jax.ShapeDtypeStruct((2 * keys, total), BF16),
            jax.ShapeDtypeStruct((3, total), F32),
            jax.ShapeDtypeStruct((rows, 128), F32),
            jax.ShapeDtypeStruct((half, d_lat, kv_up.shape[2] // 2), BF16),
        ),
        in_specs=[smem] + [vmem] * (blocks + 3),
        out_specs=[vmem] * 7,
        scratch_shapes=[
            pltpu.VMEM((packed // 128, total, 128), F32),
            pltpu.VMEM((2 * keys, together * rows), F32),
            pltpu.VMEM((2 * keys, together * rows), F32),
        ],
        compiler_params=pltpu.CompilerParams(vmem_limit_bytes=ATTEND_MIB * MIB),
        cost_estimate=pl.CostEstimate(
            flops=2 * 2 * keys * total * (c_width + d_lat),
            bytes_accessed=8 * keys * total,
            transcendentals=2 * keys * total,
        ),
    )(where, *ring, kv_up, own, other)


def project_kernel(p, own_ref, other_ref, spread_ref, expo_ref, key_ref, *out_refs):
    d_lat, d_nope = key_ref.shape[1:]
    keys = own_ref.shape[1]
    width = out_refs[0].shape[0]
    rows = spread_ref.shape[1] // key_ref.shape[0]
    columns = slice(p * width, (p + 1) * width)
    for terms_ref, out_ref in zip((spread_ref, expo_ref), out_refs):
        full = jnp.dot(own_ref[...], terms_ref[:keys, columns], preferred_element_type=F32)
        full = full + jnp.dot(
            other_ref[...], terms_ref[keys:, columns], preferred_element_type=F32
        )
        for j in range(width // rows):
            at = slice(j * rows, (j + 1) * rows)
            out_ref[at, :d_nope] = lax.dot_general(
                full[:d_lat, at].astype(BF16),
                key_ref[p * (width // rows) + j],
                (((0,), (0,)), ((), ())),
                preferred_element_type=F32,
            )
            out_ref[at, d_nope:] = full[d_lat:, at].T


def project(p, own_t, other_t, spread, expo, w_key, q_width):
    c_width, keys = own_t.shape
    width = 2 * spread.shape[1] // w_key.shape[0]
    vmem = pl.BlockSpec(memory_space=pltpu.VMEM)
    return pl.pallas_call(
        functools.partial(project_kernel, p),
        out_shape=(jax.ShapeDtypeStruct((width, q_width), F32),) * 2,
        in_specs=[vmem] * 5,
        out_specs=[vmem] * 2,
        compiler_params=pltpu.CompilerParams(vmem_limit_bytes=PROJECT_MIB * MIB),
        cost_estimate=pl.CostEstimate(
            flops=8 * keys * width * c_width, bytes_accessed=8 * keys * width, transcendentals=0
        ),
    )(own_t, other_t, spread, expo, w_key)


def row_gains(where_ref, lens_ref, ratio_ref, rows_of_core):
    rows = ratio_ref.shape[0]
    place = lax.broadcasted_iota(jnp.int32, (rows, 1), 0)
    turn = place % (2 * rows_of_core) >= rows_of_core
    swapped = jnp.where(turn, place - rows_of_core, place + rows_of_core)
    place = jnp.where(where_ref[0] == 1, swapped, place)
    ratio = ratio_ref[:, 0:1]
    segments = lens_ref.shape[0]
    members = []
    first = jnp.int32(0)
    for k in range(segments):
        last = first + lens_ref[k]
        members.append((place >= first) & (place < last))
        first = last
    sums = [jnp.sum(jnp.where(m, ratio, 0.0), axis=0, keepdims=True) for m in members]
    gains = jnp.zeros((rows, 1), F32)
    for p in range(segments // 2):
        margin = BETA * (sums[2 * p] - sums[2 * p + 1])
        weight = LOSS_SCALE * BETA / (1.0 + jnp.exp(margin))
        gains = jnp.where(members[2 * p], -weight, gains)
        gains = jnp.where(members[2 * p + 1], weight, gains)
    return gains


def weigh_kernel(scale, rows_of_core, where_ref, lens_ref, *refs):
    (joined_ref, last_ref, own_ref, ratio_ref, query_ref, grad_ref) = refs[:6]
    by_spread_refs, by_expo_refs = refs[6:-4:2], refs[7:-4:2]
    dq_keep_ref, dq_send_ref, with_spread_ref, with_expo_ref = refs[-4:]
    total = query_ref.shape[0]
    d_lat = grad_ref.shape[1]
    rows = ratio_ref.shape[0]
    half = total // rows
    gains = row_gains(where_ref, lens_ref, ratio_ref, rows_of_core)
    joined = join_stats(joined_ref[...], last_ref[...])
    centre = own_ref[2:3] / jnp.maximum(own_ref[1:2], 1e-30)
    factor = jnp.exp2(own_ref[0:1] - joined[0:1]) / joined[1:2]
    shift = joined[2:3] / joined[1:2] - centre
    sublane = lax.broadcasted_iota(jnp.int32, (8, total), 0)
    both = jnp.where(sublane == 0, factor, shift).T
    blocks, size = dq_keep_ref.shape[0], dq_keep_ref.shape[2] // 2
    second = where_ref[4 + blocks] == 1
    for h in range(half):
        at = slice(h * rows, (h + 1) * rows)
        part = slice((h % 2) * rows, (h % 2 + 1) * rows)
        factor = both[at, 0:1] * gains
        shift = both[at, 1:2]
        scaled = scale * factor
        dq = by_spread_refs[h // 2][part, :] - shift * by_expo_refs[h // 2][part, :]
        dq = scaled * dq
        if h % 2:
            for b in range(blocks):
                pieces = []
                for x in range(2):
                    first = (2 * b + x) * size
                    at_x = slice(first, first + size)
                    pieces.append(jnp.concatenate([before[at_x], dq[at_x]], axis=0))
                dq_keep_ref[b, h // 2] = jnp.where(second, pieces[1], pieces[0]).astype(BF16)
                dq_send_ref[b, h // 2] = jnp.where(second, pieces[0], pieces[1]).astype(BF16)
        before = dq
        query = scaled * query_ref[at, :].astype(F32)
        with_spread_ref[at, :] = query.astype(BF16)
        moved = shift * query
        with_expo_ref[at, :d_lat] = (
            factor * grad_ref[at, :].astype(F32) - moved[:, :d_lat]
        ).astype(BF16)
        with_expo_ref[at, d_lat:] = (-moved[:, d_lat:]).astype(BF16)


def weigh(where, lens, joined, last, stats, ratio, query, grad, projected, scale, blocks, q_dev):
    total, c_width = query.shape
    rows = ratio.shape[0]
    q_width = projected[0].shape[1]
    half = total // rows
    smem = pl.BlockSpec(memory_space=pltpu.SMEM)
    vmem = pl.BlockSpec(memory_space=pltpu.VMEM)
    dq = jax.ShapeDtypeStruct((blocks, half // 2, rows // blocks, q_width), BF16)
    weight = jax.ShapeDtypeStruct((total, c_width), BF16)
    inputs = (joined, last, stats, ratio, query, grad, *projected)
    return pl.pallas_call(
        functools.partial(weigh_kernel, scale, q_dev),
        out_shape=(dq, dq, weight, weight),
        in_specs=[smem, smem] + [vmem] * len(inputs),
        out_specs=[vmem] * 4,
        compiler_params=pltpu.CompilerParams(vmem_limit_bytes=WEIGH_MIB * MIB),
        cost_estimate=pl.CostEstimate(
            flops=10 * total * c_width, bytes_accessed=8 * total * c_width, transcendentals=0
        ),
    )(where, lens, *inputs)


def cache_kernel(part, d_lat, order_ref, spread_ref, expo_ref, with_spread_ref, with_expo_ref, *refs):
    adds, outs = refs[:-2], refs[-2:]
    keys = spread_ref.shape[3]

    def gather(ref):
        blocks = [ref[part, order_ref[i], order_ref[4 + i]] for i in range(4)]
        return jnp.concatenate(blocks, axis=0)

    out = jnp.dot(gather(spread_ref), with_spread_ref[...], preferred_element_type=F32)
    out = out + jnp.dot(gather(expo_ref), with_expo_ref[...], preferred_element_type=F32)
    rope = out.shape[1] - d_lat
    for i in range(4):
        first = (i % 2) * d_lat
        lat = slice(first, first + d_lat)
        first = 2 * d_lat + (i % 2) * rope
        tail = slice(first, first + rope)
        at = slice(i * keys, (i + 1) * keys)
        for lanes, value in ((lat, out[at, :d_lat]), (tail, out[at, d_lat:])):
            if adds:
                value = value + adds[i // 2][:, lanes].astype(F32)
            outs[i // 2][:, lanes] = value.astype(outs[i // 2].dtype)


def cache_terms(part, order, d_lat, spread, expo, with_spread, with_expo, dtypes, adds=()):
    total, c_width = with_spread.shape
    keys = spread.shape[3]
    smem = pl.BlockSpec(memory_space=pltpu.SMEM)
    vmem = pl.BlockSpec(memory_space=pltpu.VMEM)
    return pl.pallas_call(
        functools.partial(cache_kernel, part, d_lat),
        out_shape=[jax.ShapeDtypeStruct((keys, 2 * c_width), dtype) for dtype in dtypes],
        in_specs=[smem] + [vmem] * (4 + len(adds)),
        out_specs=[vmem, vmem],
        compiler_params=pltpu.CompilerParams(vmem_limit_bytes=CACHE_MIB * MIB),
        cost_estimate=pl.CostEstimate(
            flops=16 * keys * total * c_width,
            bytes_accessed=16 * keys * total,
            transcendentals=0,
        ),
    )(order, spread, expo, with_spread, with_expo, *adds)


def unfold(x, d_lat):
    rope = x.shape[1] // 2 - d_lat
    return [
        jnp.concatenate(
            [
                x[:, i * d_lat : (i + 1) * d_lat],
                x[:, 2 * d_lat + i * rope : 2 * d_lat + (i + 1) * rope],
            ],
            axis=1,
        )
        for i in range(2)
    ]


def fold_rows(x, d_lat, out_ref):
    size = x.shape[0] // 2
    rope = x.shape[1] - d_lat
    for i in range(2):
        part = x[i * size : (i + 1) * size].astype(BF16)
        out_ref[:, i * d_lat : (i + 1) * d_lat] = part[:, :d_lat]
        out_ref[:, 2 * d_lat + i * rope : 2 * d_lat + (i + 1) * rope] = part[:, d_lat:]


def forward_kernel(d_lat, keep_ref, arrived_ref, *out_refs):
    total = keep_ref[...].astype(F32) + arrived_ref[...].astype(F32)
    for block, out_ref in zip(unfold(total, d_lat), out_refs):
        fold_rows(block, d_lat, out_ref)


def turn_kernel(d_lat, own_ref, arrived_ref, send_ref, keep_ref):
    send, keep = unfold(own_ref[...] + arrived_ref[...].astype(F32), d_lat)
    fold_rows(send, d_lat, send_ref)
    keep_ref[...] = keep


def finish_kernel(d_lat, keep_ref, *refs):
    total = keep_ref[...]
    for arrived_ref in refs[:-1]:
        total = total + jnp.concatenate(unfold(arrived_ref[...].astype(F32), d_lat), axis=0)
    refs[-1][...] = total.T.astype(BF16)


def small(kernel, out_shape, *operands):
    vmem = pl.BlockSpec(memory_space=pltpu.VMEM)
    return pl.pallas_call(
        kernel,
        out_shape=out_shape,
        in_specs=[vmem] * len(operands),
        out_specs=jax.tree.map(lambda _: vmem, out_shape),
        compiler_params=pltpu.CompilerParams(vmem_limit_bytes=6 * MIB),
    )(*operands)


def per_device(queries, out_grad, kv_up, latent_cache, token_ratio, pair_lens, prompt_len):
    ctx_index = lax.axis_index("ctx")
    head_index = lax.axis_index("head")
    core = ctx_index & 1
    x_lo = (ctx_index >> 1) & 1
    z = ctx_index >> 2
    nz = lax.axis_size("ctx") // 4
    ny = lax.axis_size("head") // 2
    y = head_index & (ny - 1)
    x_hi = (head_index >= ny).astype(jnp.int32)
    other_core = lambda i: i ^ 1
    other_x_lo = lambda i: i ^ 2
    z_groups = [[4 * k + j for k in range(nz)] for j in range(4)]

    q_dev, heads, q_width = queries.shape
    p_dev, c_width = latent_cache.shape
    d_lat = kv_up.shape[1]
    d_rope = c_width - d_lat
    d_nope = q_width - d_rope
    half = heads // 2
    scale = q_width ** (-0.5)

    where = [core, ctx_index * p_dev, (ctx_index ^ 1) * p_dev, prompt_len[0]]
    where = where + [(z + k) & (nz - 1) for k in range(nz)] + [x_lo]
    where = jnp.stack(where).astype(jnp.int32)
    own_t = latent_cache.T
    other_t = permute(latent_cache, "ctx", other_core).T
    mine, theirs = pack(where, token_ratio, queries, out_grad)
    own_keys = stage(own_t)
    other_keys = stage(other_t)
    block = jnp.concatenate([mine, permute(theirs, "ctx", other_core)], 0)
    block = in_order(block, permute(block, "ctx", other_x_lo), x_lo == 1, 0)
    up = down = block
    ring = [block] + [None] * (nz - 1)
    for k in range(1, nz // 2 + 1):
        up = permute(up, "ctx", lambda i: (i + 4) % (4 * nz))
        ring[nz - k] = up
        if k < nz // 2:
            down = permute(down, "ctx", lambda i: (i - 4) % (4 * nz))
            ring[k] = down

    query, grad, expo, spread, stats, ratio, w_key = attend(
        where, ring, kv_up, own_keys, other_keys, scale * LOG2E
    )

    joined = stats
    projected = []
    pairings = [other_x_lo] + [lambda i, k=k: i ^ (4 << k) for k in range(nz.bit_length() - 1)]
    for p, pairing in enumerate(pairings):
        if p:
            joined = join(joined, last)
        last = permute(joined, "ctx", pairing)
        if p < half // 2:
            terms = project(p, own_t, other_t, spread, expo, w_key, q_width)
            last, *terms = lax.optimization_barrier((last, *terms))
            projected += terms
    dq_keep, dq_send, with_spread, with_expo = weigh(
        where, pair_lens, joined, last, stats, ratio, query, grad, projected, scale, nz, q_dev
    )
    dq_pair = permute(dq_send, "ctx", other_x_lo)
    keys = p_dev // (2 * ny)
    there, here = 1 - x_hi, x_hi
    along = [(y + k) & (ny - 1) for k in (0, 1, 2, 3)]
    orders = [
        [there, there, here, here, along[2], along[1], along[2], along[1]],
        [there, here, there, here, along[3], along[3], along[0], along[0]],
    ]
    orders = [jnp.stack(order).astype(jnp.int32) for order in orders]
    shape = (2, 2, ny, keys, spread.shape[1])
    operands = (d_lat, spread.reshape(shape), expo.reshape(shape), with_spread, with_expo)
    adds = []
    sends = cache_terms(1, orders[0], *operands, (BF16, BF16))
    later, *sends = lax.optimization_barrier((orders[1], *sends))
    adds.append([permute(x, "ctx", other_core) for x in sends])
    sends = cache_terms(1, later, *operands, (BF16, BF16))
    adds.append([permute(x, "ctx", other_core) for x in sends])
    to_x_hi = lambda x: permute(x, "head", lambda i: (i + ny) % (2 * ny))
    to_y = lambda x, k: permute(x, "head", lambda i: (i // ny) * ny + (i + k) % ny)
    send, keep = cache_terms(0, orders[0], *operands, (BF16, F32), adds[0])
    later, send = lax.optimization_barrier((orders[1], send))
    from_x_hi = to_x_hi(send)
    send, own = cache_terms(0, later, *operands, (BF16, F32), adds[1])
    dq = (dq_keep.astype(F32) + dq_pair.astype(F32)).astype(BF16)
    send, dq = lax.optimization_barrier((send, dq))
    from_y = to_y(send, 3)

    half_rows = jax.ShapeDtypeStruct((keys // 2, 2 * c_width), BF16)
    block = jax.ShapeDtypeStruct((keys, c_width), F32)
    sends = small(
        functools.partial(forward_kernel, d_lat), (half_rows, half_rows), keep, from_x_hi
    )
    arrived = [to_y(sends[0], 2), to_y(sends[1], 1)]
    send, keep = small(functools.partial(turn_kernel, d_lat), (half_rows, block), own, from_y)
    arrived.append(to_x_hi(send))
    cache_grad = small(
        functools.partial(finish_kernel, d_lat),
        jax.ShapeDtypeStruct((c_width, keys), BF16),
        keep,
        *arrived,
    ).T

    dq = lax.all_to_all(dq, "ctx", 0, 0, axis_index_groups=z_groups)
    dq = jnp.sum(dq.astype(F32), axis=0).astype(BF16).reshape(half, 2, q_dev, q_width)
    theirs = permute(dq[:, 1], "ctx", other_core)
    query_grad = jnp.transpose(in_order(dq[:, 0], theirs, core == 1, 0), (1, 0, 2))

    return (query_grad, cache_grad)


def solution(mesh):
    placed = (
        P("ctx", "head", None),
        P("ctx", "head", None),
        P("head", None, None),
        P("ctx", None),
        P("ctx"),
        P(),
        P(),
    )
    return jax.shard_map(
        per_device,
        mesh=mesh,
        in_specs=placed,
        out_specs=(P("ctx", "head", None), P(("ctx", "head"), None)),
        check_vma=False,
    )
```

```python
import functools

import jax
import jax.numpy as jnp
from jax import lax
from jax.experimental import pallas as pl
from jax.experimental.pallas import tpu as pltpu
from jax.sharding import PartitionSpec as P

BETA = 0.1
LOSS_SCALE = 2048.0
LOG2E = 1.4426950408889634
NEVER = -1e30
FLOOR = -1e29
F32 = jnp.float32
BF16 = jnp.bfloat16
CHUNK = 256
TOGETHER = 4
PACKED = 384
MIB = 1024 * 1024
ATTEND_MIB = 24
PROJECT_MIB = 8
WEIGH_MIB = 16
CACHE_MIB = 20


def permute(x, axis, to):
    return lax.ppermute(x, axis, [(i, to(i)) for i in range(lax.axis_size(axis))])


def in_order(mine, theirs, second, axis):
    return jnp.where(
        second,
        jnp.concatenate([theirs, mine], axis),
        jnp.concatenate([mine, theirs], axis),
    )


def join_stats(first, second):
    top = jnp.maximum(first[0:1], second[0:1])
    both = jnp.exp2(first[0:1] - top) * first + jnp.exp2(second[0:1] - top) * second
    return jnp.where(lax.broadcasted_iota(jnp.int32, both.shape, 0) == 0, top, both)


def join_kernel(first_ref, second_ref, out_ref):
    out_ref[...] = join_stats(first_ref[...], second_ref[...])


def join(first, second):
    vmem = pl.BlockSpec(memory_space=pltpu.VMEM)
    return pl.pallas_call(
        join_kernel,
        out_shape=jax.ShapeDtypeStruct(first.shape, F32),
        in_specs=[vmem, vmem],
        out_specs=vmem,
        compiler_params=pltpu.CompilerParams(vmem_limit_bytes=MIB),
    )(first, second)


def against(x, y):
    return lax.dot_general(x, y, (((1,), (1,)), ((), ())), preferred_element_type=F32)


def pack_kernel(where_ref, ratio_ref, queries_ref, out_grad_ref, mine_ref, theirs_ref):
    q_dev, heads, q_width = queries_ref.shape
    d_nope = out_grad_ref.shape[2]
    half = heads // 2
    d_rope = q_width - d_nope
    lane = lax.broadcasted_iota(jnp.int32, (heads, PACKED - 2 * d_nope - d_rope), 1)
    second = where_ref[0] == 1
    mine, theirs = [], []
    for j in range(q_dev):
        query = queries_ref[j].astype(F32)
        ratio = jnp.full(lane.shape, ratio_ref[j], F32)
        high = ratio.astype(BF16).astype(F32)
        middle = (ratio - high).astype(BF16).astype(F32)
        terms = jnp.where(lane == 0, high, jnp.where(lane == 1, middle, ratio - high - middle))
        terms = jnp.where(lane < 3, terms, 0.0)
        row = [query[:, :d_nope], out_grad_ref[j].astype(F32), query[:, d_nope:], terms]
        row = jnp.concatenate(row, axis=1)
        mine.append(jnp.where(second, row[half:], row[:half]))
        theirs.append(jnp.where(second, row[:half], row[half:]))
    mine_ref[...] = jnp.concatenate(mine, axis=0).astype(BF16)
    theirs_ref[...] = jnp.concatenate(theirs, axis=0).astype(BF16)


def pack(where, token_ratio, queries, out_grad):
    q_dev, heads = queries.shape[:2]
    smem = pl.BlockSpec(memory_space=pltpu.SMEM)
    vmem = pl.BlockSpec(memory_space=pltpu.VMEM)
    packed = jax.ShapeDtypeStruct((q_dev * heads // 2, PACKED), BF16)
    return pl.pallas_call(
        pack_kernel,
        out_shape=(packed, packed),
        in_specs=[smem, smem, vmem, vmem],
        out_specs=[vmem, vmem],
        compiler_params=pltpu.CompilerParams(vmem_limit_bytes=2 * MIB),
        cost_estimate=pl.CostEstimate(flops=0, bytes_accessed=32 * MIB, transcendentals=0),
    )(where, token_ratio, queries, out_grad)


def stage_kernel(cache_ref, out_ref):
    out_ref[...] = cache_ref[...].T


def stage(cache_t):
    c_width, keys = cache_t.shape
    vmem = pl.BlockSpec(memory_space=pltpu.VMEM)
    return pl.pallas_call(
        stage_kernel,
        out_shape=jax.ShapeDtypeStruct((keys, c_width), BF16),
        in_specs=[vmem],
        out_specs=vmem,
        compiler_params=pltpu.CompilerParams(vmem_limit_bytes=6 * MIB),
        cost_estimate=pl.CostEstimate(
            flops=keys * c_width, bytes_accessed=4 * keys * c_width, transcendentals=0
        ),
    )(cache_t)


def attend_kernel(score_scale, blocks, together, where_ref, *refs):
    ring_refs, refs = refs[:blocks], refs[blocks:]
    kv_ref, own_ref, other_ref, query_ref, grad_ref, expo_ref, spread_ref, stats_ref = refs[:8]
    ratio_ref, key_ref, raw, expo, dprod = refs[8:]
    size = ring_refs[0].shape[0]
    half, d_lat, d_nope = kv_ref.shape[0] // 2, kv_ref.shape[1], kv_ref.shape[2] // 2
    rows = size * blocks // half
    first_head = where_ref[0] * half
    d_rope = query_ref.shape[1] - d_lat
    keys = own_ref.shape[0]
    width = together * rows
    for k in range(blocks):
        first = pl.multiple_of(where_ref[4 + k] * size, size)
        for part in range(PACKED // 128):
            lanes = slice(part * 128, (part + 1) * 128)
            raw[part, pl.ds(first, size), :] = ring_refs[k][:, lanes].astype(F32)

    def of_head(h, part):
        return raw[part, pl.ds(h, rows, stride=half), :]

    terms = of_head(0, 2)
    lane = lax.broadcasted_iota(jnp.int32, terms.shape, 1)
    terms = jnp.where((lane >= d_rope) & (lane < d_rope + 3), terms, 0.0)
    ratio_ref[...] = jnp.broadcast_to(jnp.sum(terms, axis=1, keepdims=True), ratio_ref.shape)

    def fold(x, join):
        return join(join(x.reshape(CHUNK // 8, 8, width), axis=0), axis=0, keepdims=True)

    def group(p, carry):
        for j in range(together):
            h = p * together + j
            at = pl.ds(pl.multiple_of(h * rows, rows), rows)
            key_ref[h] = kv_ref[first_head + h, :, :d_nope]
            lat = against(of_head(h, 0).astype(BF16), key_ref[h])
            query_ref[at, :d_lat] = lat.astype(BF16)
            rope = of_head(h, 2)[:, :d_rope]
            query_ref[at, d_lat:] = rope.astype(BF16)
            lat = against(of_head(h, 1).astype(BF16), kv_ref[first_head + h, :, d_nope:])
            grad_ref[at, :] = lat.astype(BF16)
        columns = pl.ds(pl.multiple_of(p * width, width), width)
        tops, masses, dsums = [], [], []
        for c in range(2 * keys // CHUNK):
            first = c * CHUNK % keys
            ref, base = (own_ref, where_ref[1]) if c * CHUNK < keys else (other_ref, where_ref[2])
            score = against(ref[first : first + CHUNK, :], query_ref[columns, :]) * score_scale
            dp = against(ref[first : first + CHUNK, :d_lat], grad_ref[columns, :])
            key = base + first + lax.broadcasted_iota(jnp.int32, (CHUNK, 1), 0)
            score = jnp.where(key < where_ref[3], score, NEVER)
            top = jnp.maximum(fold(score, jnp.max), FLOOR)
            value = jnp.exp2(score - top)
            at = slice(c * CHUNK, (c + 1) * CHUNK)
            expo[at] = value
            dprod[at] = dp
            tops.append(top)
            masses.append(fold(value, jnp.sum))
            dsums.append(fold(value * dp, jnp.sum))
        top = functools.reduce(jnp.maximum, tops)
        factors = [jnp.exp2(t - top) for t in tops]
        mass = sum(f * m for f, m in zip(factors, masses))
        dsum = sum(f * d for f, d in zip(factors, dsums))
        centre = dsum / jnp.maximum(mass, 1e-30)
        for c, f in enumerate(factors):
            at = slice(c * CHUNK, (c + 1) * CHUNK)
            value = expo[at] * f
            expo_ref[at, columns] = value.astype(BF16)
            spread_ref[at, columns] = (value * (dprod[at] - centre)).astype(BF16)
        stats_ref[0:1, columns] = top
        stats_ref[1:2, columns] = mass
        stats_ref[2:3, columns] = dsum
        return carry

    lax.fori_loop(0, half // together, group, 0)


def attend(where, ring, kv_up, own, other, score_scale, together=TOGETHER):
    blocks, (size, packed) = len(ring), ring[0].shape
    half, d_lat = kv_up.shape[0] // 2, kv_up.shape[1]
    total = blocks * size
    rows = total // half
    keys, c_width = own.shape
    smem = pl.BlockSpec(memory_space=pltpu.SMEM)
    vmem = pl.BlockSpec(memory_space=pltpu.VMEM)
    return pl.pallas_call(
        functools.partial(attend_kernel, score_scale, blocks, together),
        out_shape=(
            jax.ShapeDtypeStruct((total, c_width), BF16),
            jax.ShapeDtypeStruct((total, d_lat), BF16),
            jax.ShapeDtypeStruct((2 * keys, total), BF16),
            jax.ShapeDtypeStruct((2 * keys, total), BF16),
            jax.ShapeDtypeStruct((3, total), F32),
            jax.ShapeDtypeStruct((rows, 128), F32),
            jax.ShapeDtypeStruct((half, d_lat, kv_up.shape[2] // 2), BF16),
        ),
        in_specs=[smem] + [vmem] * (blocks + 3),
        out_specs=[vmem] * 7,
        scratch_shapes=[
            pltpu.VMEM((packed // 128, total, 128), F32),
            pltpu.VMEM((2 * keys, together * rows), F32),
            pltpu.VMEM((2 * keys, together * rows), F32),
        ],
        compiler_params=pltpu.CompilerParams(vmem_limit_bytes=ATTEND_MIB * MIB),
        cost_estimate=pl.CostEstimate(
            flops=2 * 2 * keys * total * (c_width + d_lat),
            bytes_accessed=8 * keys * total,
            transcendentals=2 * keys * total,
        ),
    )(where, *ring, kv_up, own, other)


def project_kernel(p, own_ref, other_ref, spread_ref, expo_ref, key_ref, *out_refs):
    d_lat, d_nope = key_ref.shape[1:]
    keys = own_ref.shape[1]
    width = out_refs[0].shape[0]
    rows = spread_ref.shape[1] // key_ref.shape[0]
    columns = slice(p * width, (p + 1) * width)
    for terms_ref, out_ref in zip((spread_ref, expo_ref), out_refs):
        full = jnp.dot(own_ref[...], terms_ref[:keys, columns], preferred_element_type=F32)
        full = full + jnp.dot(
            other_ref[...], terms_ref[keys:, columns], preferred_element_type=F32
        )
        for j in range(width // rows):
            at = slice(j * rows, (j + 1) * rows)
            out_ref[at, :d_nope] = lax.dot_general(
                full[:d_lat, at].astype(BF16),
                key_ref[p * (width // rows) + j],
                (((0,), (0,)), ((), ())),
                preferred_element_type=F32,
            )
            out_ref[at, d_nope:] = full[d_lat:, at].T


def project(p, own_t, other_t, spread, expo, w_key, q_width):
    c_width, keys = own_t.shape
    width = 2 * spread.shape[1] // w_key.shape[0]
    vmem = pl.BlockSpec(memory_space=pltpu.VMEM)
    return pl.pallas_call(
        functools.partial(project_kernel, p),
        out_shape=(jax.ShapeDtypeStruct((width, q_width), F32),) * 2,
        in_specs=[vmem] * 5,
        out_specs=[vmem] * 2,
        compiler_params=pltpu.CompilerParams(vmem_limit_bytes=PROJECT_MIB * MIB),
        cost_estimate=pl.CostEstimate(
            flops=8 * keys * width * c_width, bytes_accessed=8 * keys * width, transcendentals=0
        ),
    )(own_t, other_t, spread, expo, w_key)


def row_gains(where_ref, lens_ref, ratio_ref, rows_of_core):
    rows = ratio_ref.shape[0]
    place = lax.broadcasted_iota(jnp.int32, (rows, 1), 0)
    turn = place % (2 * rows_of_core) >= rows_of_core
    swapped = jnp.where(turn, place - rows_of_core, place + rows_of_core)
    place = jnp.where(where_ref[0] == 1, swapped, place)
    ratio = ratio_ref[:, 0:1]
    segments = lens_ref.shape[0]
    members = []
    first = jnp.int32(0)
    for k in range(segments):
        last = first + lens_ref[k]
        members.append((place >= first) & (place < last))
        first = last
    sums = [jnp.sum(jnp.where(m, ratio, 0.0), axis=0, keepdims=True) for m in members]
    gains = jnp.zeros((rows, 1), F32)
    for p in range(segments // 2):
        margin = BETA * (sums[2 * p] - sums[2 * p + 1])
        weight = LOSS_SCALE * BETA / (1.0 + jnp.exp(margin))
        gains = jnp.where(members[2 * p], -weight, gains)
        gains = jnp.where(members[2 * p + 1], weight, gains)
    return gains


def weigh_kernel(scale, rows_of_core, where_ref, lens_ref, *refs):
    (joined_ref, last_ref, own_ref, ratio_ref, query_ref, grad_ref) = refs[:6]
    by_spread_refs, by_expo_refs = refs[6:-4:2], refs[7:-4:2]
    dq_keep_ref, dq_send_ref, with_spread_ref, with_expo_ref = refs[-4:]
    total = query_ref.shape[0]
    d_lat = grad_ref.shape[1]
    rows = ratio_ref.shape[0]
    half = total // rows
    gains = row_gains(where_ref, lens_ref, ratio_ref, rows_of_core)
    joined = join_stats(joined_ref[...], last_ref[...])
    centre = own_ref[2:3] / jnp.maximum(own_ref[1:2], 1e-30)
    factor = jnp.exp2(own_ref[0:1] - joined[0:1]) / joined[1:2]
    shift = joined[2:3] / joined[1:2] - centre
    sublane = lax.broadcasted_iota(jnp.int32, (8, total), 0)
    both = jnp.where(sublane == 0, factor, shift).T
    blocks, size = dq_keep_ref.shape[0], dq_keep_ref.shape[2] // 2
    second = where_ref[4 + blocks] == 1
    for h in range(half):
        at = slice(h * rows, (h + 1) * rows)
        part = slice((h % 2) * rows, (h % 2 + 1) * rows)
        factor = both[at, 0:1] * gains
        shift = both[at, 1:2]
        scaled = scale * factor
        dq = by_spread_refs[h // 2][part, :] - shift * by_expo_refs[h // 2][part, :]
        dq = scaled * dq
        if h % 2:
            for b in range(blocks):
                pieces = []
                for x in range(2):
                    first = (2 * b + x) * size
                    at_x = slice(first, first + size)
                    pieces.append(jnp.concatenate([before[at_x], dq[at_x]], axis=0))
                dq_keep_ref[b, h // 2] = jnp.where(second, pieces[1], pieces[0]).astype(BF16)
                dq_send_ref[b, h // 2] = jnp.where(second, pieces[0], pieces[1]).astype(BF16)
        before = dq
        query = scaled * query_ref[at, :].astype(F32)
        with_spread_ref[at, :] = query.astype(BF16)
        moved = shift * query
        with_expo_ref[at, :d_lat] = (
            factor * grad_ref[at, :].astype(F32) - moved[:, :d_lat]
        ).astype(BF16)
        with_expo_ref[at, d_lat:] = (-moved[:, d_lat:]).astype(BF16)


def weigh(where, lens, joined, last, stats, ratio, query, grad, projected, scale, blocks, q_dev):
    total, c_width = query.shape
    rows = ratio.shape[0]
    q_width = projected[0].shape[1]
    half = total // rows
    smem = pl.BlockSpec(memory_space=pltpu.SMEM)
    vmem = pl.BlockSpec(memory_space=pltpu.VMEM)
    dq = jax.ShapeDtypeStruct((blocks, half // 2, rows // blocks, q_width), BF16)
    weight = jax.ShapeDtypeStruct((total, c_width), BF16)
    inputs = (joined, last, stats, ratio, query, grad, *projected)
    return pl.pallas_call(
        functools.partial(weigh_kernel, scale, q_dev),
        out_shape=(dq, dq, weight, weight),
        in_specs=[smem, smem] + [vmem] * len(inputs),
        out_specs=[vmem] * 4,
        compiler_params=pltpu.CompilerParams(vmem_limit_bytes=WEIGH_MIB * MIB),
        cost_estimate=pl.CostEstimate(
            flops=10 * total * c_width, bytes_accessed=8 * total * c_width, transcendentals=0
        ),
    )(where, lens, *inputs)


def cache_kernel(part, d_lat, order_ref, spread_ref, expo_ref, with_spread_ref, with_expo_ref, *refs):
    adds, outs = refs[:-2], refs[-2:]
    keys = spread_ref.shape[3]

    def gather(ref):
        blocks = [ref[part, order_ref[i], order_ref[4 + i]] for i in range(4)]
        return jnp.concatenate(blocks, axis=0)

    out = jnp.dot(gather(spread_ref), with_spread_ref[...], preferred_element_type=F32)
    out = out + jnp.dot(gather(expo_ref), with_expo_ref[...], preferred_element_type=F32)
    rope = out.shape[1] - d_lat
    for i in range(4):
        first = (i % 2) * d_lat
        lat = slice(first, first + d_lat)
        first = 2 * d_lat + (i % 2) * rope
        tail = slice(first, first + rope)
        at = slice(i * keys, (i + 1) * keys)
        for lanes, value in ((lat, out[at, :d_lat]), (tail, out[at, d_lat:])):
            if adds:
                value = value + adds[i // 2][:, lanes].astype(F32)
            outs[i // 2][:, lanes] = value.astype(outs[i // 2].dtype)


def cache_terms(part, order, d_lat, spread, expo, with_spread, with_expo, dtypes, adds=()):
    total, c_width = with_spread.shape
    keys = spread.shape[3]
    smem = pl.BlockSpec(memory_space=pltpu.SMEM)
    vmem = pl.BlockSpec(memory_space=pltpu.VMEM)
    return pl.pallas_call(
        functools.partial(cache_kernel, part, d_lat),
        out_shape=[jax.ShapeDtypeStruct((keys, 2 * c_width), dtype) for dtype in dtypes],
        in_specs=[smem] + [vmem] * (4 + len(adds)),
        out_specs=[vmem, vmem],
        compiler_params=pltpu.CompilerParams(vmem_limit_bytes=CACHE_MIB * MIB),
        cost_estimate=pl.CostEstimate(
            flops=16 * keys * total * c_width,
            bytes_accessed=16 * keys * total,
            transcendentals=0,
        ),
    )(order, spread, expo, with_spread, with_expo, *adds)


def unfold(x, d_lat):
    rope = x.shape[1] // 2 - d_lat
    return [
        jnp.concatenate(
            [
                x[:, i * d_lat : (i + 1) * d_lat],
                x[:, 2 * d_lat + i * rope : 2 * d_lat + (i + 1) * rope],
            ],
            axis=1,
        )
        for i in range(2)
    ]


def fold_rows(x, d_lat, out_ref):
    size = x.shape[0] // 2
    rope = x.shape[1] - d_lat
    for i in range(2):
        part = x[i * size : (i + 1) * size].astype(BF16)
        out_ref[:, i * d_lat : (i + 1) * d_lat] = part[:, :d_lat]
        out_ref[:, 2 * d_lat + i * rope : 2 * d_lat + (i + 1) * rope] = part[:, d_lat:]


def forward_kernel(d_lat, keep_ref, arrived_ref, *out_refs):
    total = keep_ref[...].astype(F32) + arrived_ref[...].astype(F32)
    for block, out_ref in zip(unfold(total, d_lat), out_refs):
        fold_rows(block, d_lat, out_ref)


def turn_kernel(d_lat, own_ref, arrived_ref, send_ref, keep_ref):
    send, keep = unfold(own_ref[...] + arrived_ref[...].astype(F32), d_lat)
    fold_rows(send, d_lat, send_ref)
    keep_ref[...] = keep


def finish_kernel(d_lat, keep_ref, *refs):
    total = keep_ref[...]
    for arrived_ref in refs[:-1]:
        total = total + jnp.concatenate(unfold(arrived_ref[...].astype(F32), d_lat), axis=0)
    refs[-1][...] = total.T.astype(BF16)


def small(kernel, out_shape, *operands):
    vmem = pl.BlockSpec(memory_space=pltpu.VMEM)
    return pl.pallas_call(
        kernel,
        out_shape=out_shape,
        in_specs=[vmem] * len(operands),
        out_specs=jax.tree.map(lambda _: vmem, out_shape),
        compiler_params=pltpu.CompilerParams(vmem_limit_bytes=6 * MIB),
    )(*operands)


def per_device(queries, out_grad, kv_up, latent_cache, token_ratio, pair_lens, prompt_len):
    ctx_index = lax.axis_index("ctx")
    head_index = lax.axis_index("head")
    core = ctx_index & 1
    x_lo = (ctx_index >> 1) & 1
    z = ctx_index >> 2
    nz = lax.axis_size("ctx") // 4
    ny = lax.axis_size("head") // 2
    y = head_index & (ny - 1)
    x_hi = (head_index >= ny).astype(jnp.int32)
    other_core = lambda i: i ^ 1
    other_x_lo = lambda i: i ^ 2
    z_groups = [[4 * k + j for k in range(nz)] for j in range(4)]

    q_dev, heads, q_width = queries.shape
    p_dev, c_width = latent_cache.shape
    d_lat = kv_up.shape[1]
    d_rope = c_width - d_lat
    d_nope = q_width - d_rope
    half = heads // 2
    scale = q_width ** (-0.5)

    where = [core, ctx_index * p_dev, (ctx_index ^ 1) * p_dev, prompt_len[0]]
    where = where + [(z + k) & (nz - 1) for k in range(nz)] + [x_lo]
    where = jnp.stack(where).astype(jnp.int32)
    mine, theirs = pack(where, token_ratio, queries, out_grad)
    block = jnp.concatenate([mine, permute(theirs, "ctx", other_core)], 0)
    block = in_order(block, permute(block, "ctx", other_x_lo), x_lo == 1, 0)
    block, latent_cache = lax.optimization_barrier((block, latent_cache))
    own_t = latent_cache.T
    other_t = permute(latent_cache, "ctx", other_core).T
    own_keys = stage(own_t)
    other_keys = stage(other_t)
    up = down = block
    ring = [block] + [None] * (nz - 1)
    for k in range(1, nz // 2 + 1):
        up = permute(up, "ctx", lambda i: (i + 4) % (4 * nz))
        ring[nz - k] = up
        if k < nz // 2:
            down = permute(down, "ctx", lambda i: (i - 4) % (4 * nz))
            ring[k] = down

    query, grad, expo, spread, stats, ratio, w_key = attend(
        where, ring, kv_up, own_keys, other_keys, scale * LOG2E
    )

    joined = stats
    projected = []
    pairings = [other_x_lo] + [lambda i, k=k: i ^ (4 << k) for k in range(nz.bit_length() - 1)]
    for p, pairing in enumerate(pairings):
        if p:
            joined = join(joined, last)
        last = permute(joined, "ctx", pairing)
        if p < half // 2:
            terms = project(p, own_t, other_t, spread, expo, w_key, q_width)
            last, *terms = lax.optimization_barrier((last, *terms))
            projected += terms
    dq_keep, dq_send, with_spread, with_expo = weigh(
        where, pair_lens, joined, last, stats, ratio, query, grad, projected, scale, nz, q_dev
    )
    dq_pair = permute(dq_send, "ctx", other_x_lo)
    keys = p_dev // (2 * ny)
    there, here = 1 - x_hi, x_hi
    along = [(y + k) & (ny - 1) for k in (0, 1, 2, 3)]
    orders = [
        [there, there, here, here, along[2], along[1], along[2], along[1]],
        [there, here, there, here, along[3], along[3], along[0], along[0]],
    ]
    orders = [jnp.stack(order).astype(jnp.int32) for order in orders]
    shape = (2, 2, ny, keys, spread.shape[1])
    operands = (d_lat, spread.reshape(shape), expo.reshape(shape), with_spread, with_expo)
    adds = []
    sends = cache_terms(1, orders[0], *operands, (BF16, BF16))
    later, *sends = lax.optimization_barrier((orders[1], *sends))
    adds.append([permute(x, "ctx", other_core) for x in sends])
    sends = cache_terms(1, later, *operands, (BF16, BF16))
    adds.append([permute(x, "ctx", other_core) for x in sends])
    to_x_hi = lambda x: permute(x, "head", lambda i: (i + ny) % (2 * ny))
    to_y = lambda x, k: permute(x, "head", lambda i: (i // ny) * ny + (i + k) % ny)
    send, keep = cache_terms(0, orders[0], *operands, (BF16, F32), adds[0])
    later, send = lax.optimization_barrier((orders[1], send))
    from_x_hi = to_x_hi(send)
    send, own = cache_terms(0, later, *operands, (BF16, F32), adds[1])
    dq = (dq_keep.astype(F32) + dq_pair.astype(F32)).astype(BF16)
    send, dq = lax.optimization_barrier((send, dq))
    from_y = to_y(send, 3)

    half_rows = jax.ShapeDtypeStruct((keys // 2, 2 * c_width), BF16)
    block = jax.ShapeDtypeStruct((keys, c_width), F32)
    sends = small(
        functools.partial(forward_kernel, d_lat), (half_rows, half_rows), keep, from_x_hi
    )
    arrived = [to_y(sends[0], 2), to_y(sends[1], 1)]
    send, keep = small(functools.partial(turn_kernel, d_lat), (half_rows, block), own, from_y)
    arrived.append(to_x_hi(send))
    cache_grad = small(
        functools.partial(finish_kernel, d_lat),
        jax.ShapeDtypeStruct((c_width, keys), BF16),
        keep,
        *arrived,
    ).T

    dq = lax.all_to_all(dq, "ctx", 0, 0, axis_index_groups=z_groups)
    dq = jnp.sum(dq.astype(F32), axis=0).astype(BF16).reshape(half, 2, q_dev, q_width)
    theirs = permute(dq[:, 1], "ctx", other_core)
    query_grad = jnp.transpose(in_order(dq[:, 0], theirs, core == 1, 0), (1, 0, 2))

    return (query_grad, cache_grad)


def solution(mesh):
    placed = (
        P("ctx", "head", None),
        P("ctx", "head", None),
        P("head", None, None),
        P("ctx", None),
        P("ctx"),
        P(),
        P(),
    )
    return jax.shard_map(
        per_device,
        mesh=mesh,
        in_specs=placed,
        out_specs=(P("ctx", "head", None), P(("ctx", "head"), None)),
        check_vma=False,
    )
```

```python
import functools

import jax
import jax.numpy as jnp
from jax import lax
from jax.experimental import pallas as pl
from jax.experimental.pallas import tpu as pltpu
from jax.sharding import PartitionSpec as P

BETA = 0.1
LOSS_SCALE = 2048.0
LOG2E = 1.4426950408889634
NEVER = -1e30
FLOOR = -1e29
F32 = jnp.float32
BF16 = jnp.bfloat16
CHUNK = 256
TOGETHER = 4
PACKED = 384
MIB = 1024 * 1024
ATTEND_MIB = 24
PROJECT_MIB = 10
WEIGH_MIB = 16
CACHE_MIB = 20


def permute(x, axis, to):
    return lax.ppermute(x, axis, [(i, to(i)) for i in range(lax.axis_size(axis))])


def in_order(mine, theirs, second, axis):
    return jnp.where(
        second,
        jnp.concatenate([theirs, mine], axis),
        jnp.concatenate([mine, theirs], axis),
    )


def join_stats(first, second):
    top = jnp.maximum(first[0:1], second[0:1])
    both = jnp.exp2(first[0:1] - top) * first + jnp.exp2(second[0:1] - top) * second
    return jnp.where(lax.broadcasted_iota(jnp.int32, both.shape, 0) == 0, top, both)


def join_kernel(*refs):
    refs[-1][...] = functools.reduce(join_stats, [ref[...] for ref in refs[:-1]])


def join(*parts):
    vmem = pl.BlockSpec(memory_space=pltpu.VMEM)
    return pl.pallas_call(
        join_kernel,
        out_shape=jax.ShapeDtypeStruct(parts[0].shape, F32),
        in_specs=[vmem] * len(parts),
        out_specs=vmem,
        compiler_params=pltpu.CompilerParams(vmem_limit_bytes=MIB),
    )(*parts)


def against(x, y):
    return lax.dot_general(x, y, (((1,), (1,)), ((), ())), preferred_element_type=F32)


def pack_kernel(where_ref, ratio_ref, queries_ref, out_grad_ref, mine_ref, theirs_ref):
    q_dev, heads, q_width = queries_ref.shape
    d_nope = out_grad_ref.shape[2]
    half = heads // 2
    d_rope = q_width - d_nope
    lane = lax.broadcasted_iota(jnp.int32, (heads, PACKED - 2 * d_nope - d_rope), 1)
    second = where_ref[0] == 1
    mine, theirs = [], []
    for j in range(q_dev):
        query = queries_ref[j].astype(F32)
        ratio = jnp.full(lane.shape, ratio_ref[j], F32)
        high = ratio.astype(BF16).astype(F32)
        middle = (ratio - high).astype(BF16).astype(F32)
        terms = jnp.where(lane == 0, high, jnp.where(lane == 1, middle, ratio - high - middle))
        terms = jnp.where(lane < 3, terms, 0.0)
        row = [query[:, :d_nope], out_grad_ref[j].astype(F32), query[:, d_nope:], terms]
        row = jnp.concatenate(row, axis=1)
        mine.append(jnp.where(second, row[half:], row[:half]))
        theirs.append(jnp.where(second, row[:half], row[half:]))
    mine_ref[...] = jnp.concatenate(mine, axis=0).astype(BF16)
    theirs_ref[...] = jnp.concatenate(theirs, axis=0).astype(BF16)


def pack(where, token_ratio, queries, out_grad):
    q_dev, heads = queries.shape[:2]
    smem = pl.BlockSpec(memory_space=pltpu.SMEM)
    vmem = pl.BlockSpec(memory_space=pltpu.VMEM)
    packed = jax.ShapeDtypeStruct((q_dev * heads // 2, PACKED), BF16)
    return pl.pallas_call(
        pack_kernel,
        out_shape=(packed, packed),
        in_specs=[smem, smem, vmem, vmem],
        out_specs=[vmem, vmem],
        compiler_params=pltpu.CompilerParams(vmem_limit_bytes=2 * MIB),
        cost_estimate=pl.CostEstimate(flops=0, bytes_accessed=32 * MIB, transcendentals=0),
    )(where, token_ratio, queries, out_grad)


def stage_kernel(cache_ref, *refs):
    refs[-1][...] = cache_ref[...].T
    if len(refs) == 3:
        own_ref, both_ref = refs[:2]
        keys = own_ref.shape[1]
        both_ref[:, :keys] = own_ref[...]
        both_ref[:, keys:] = cache_ref[...]


def stage(cache_t, own_t=None):
    c_width, keys = cache_t.shape
    vmem = pl.BlockSpec(memory_space=pltpu.VMEM)
    turned = jax.ShapeDtypeStruct((keys, c_width), BF16)
    both = jax.ShapeDtypeStruct((c_width, 2 * keys), BF16)
    operands, outs = ((cache_t,), (turned,)) if own_t is None else ((cache_t, own_t), (both, turned))
    return pl.pallas_call(
        stage_kernel,
        out_shape=outs,
        in_specs=[vmem] * len(operands),
        out_specs=[vmem] * len(outs),
        compiler_params=pltpu.CompilerParams(vmem_limit_bytes=10 * MIB),
        cost_estimate=pl.CostEstimate(
            flops=keys * c_width, bytes_accessed=4 * keys * c_width, transcendentals=0
        ),
    )(*operands)


def attend_kernel(score_scale, blocks, together, where_ref, *refs):
    ring_refs, refs = refs[:blocks], refs[blocks:]
    kv_ref, own_ref, other_ref, query_ref, grad_ref, expo_ref, spread_ref, stats_ref = refs[:8]
    ratio_ref, key_ref, raw, expo, dprod = refs[8:]
    size = ring_refs[0].shape[0]
    half, d_lat, d_nope = kv_ref.shape[0] // 2, kv_ref.shape[1], kv_ref.shape[2] // 2
    rows = size * blocks // half
    first_head = where_ref[0] * half
    d_rope = query_ref.shape[1] - d_lat
    keys = own_ref.shape[0]
    width = together * rows
    for k in range(blocks):
        first = pl.multiple_of(where_ref[4 + k] * size, size)
        for part in range(PACKED // 128):
            lanes = slice(part * 128, (part + 1) * 128)
            raw[part, pl.ds(first, size), :] = ring_refs[k][:, lanes].astype(F32)

    def of_head(h, part):
        return raw[part, pl.ds(h, rows, stride=half), :]

    terms = of_head(0, 2)
    lane = lax.broadcasted_iota(jnp.int32, terms.shape, 1)
    terms = jnp.where((lane >= d_rope) & (lane < d_rope + 3), terms, 0.0)
    ratio_ref[...] = jnp.broadcast_to(jnp.sum(terms, axis=1, keepdims=True), ratio_ref.shape)

    def fold(x, join):
        return join(join(x.reshape(CHUNK // 8, 8, width), axis=0), axis=0, keepdims=True)

    def group(p, carry):
        for j in range(together):
            h = p * together + j
            at = pl.ds(pl.multiple_of(h * rows, rows), rows)
            key_ref[h] = kv_ref[first_head + h, :, :d_nope]
            lat = against(of_head(h, 0).astype(BF16), key_ref[h])
            query_ref[at, :d_lat] = lat.astype(BF16)
            rope = of_head(h, 2)[:, :d_rope]
            query_ref[at, d_lat:] = rope.astype(BF16)
            lat = against(of_head(h, 1).astype(BF16), kv_ref[first_head + h, :, d_nope:])
            grad_ref[at, :] = lat.astype(BF16)
        columns = pl.ds(pl.multiple_of(p * width, width), width)
        tops, masses, dsums = [], [], []
        for c in range(2 * keys // CHUNK):
            first = c * CHUNK % keys
            ref, base = (own_ref, where_ref[1]) if c * CHUNK < keys else (other_ref, where_ref[2])
            score = against(ref[first : first + CHUNK, :], query_ref[columns, :]) * score_scale
            dp = against(ref[first : first + CHUNK, :d_lat], grad_ref[columns, :])
            key = base + first + lax.broadcasted_iota(jnp.int32, (CHUNK, 1), 0)
            score = jnp.where(key < where_ref[3], score, NEVER)
            top = jnp.maximum(fold(score, jnp.max), FLOOR)
            value = jnp.exp2(score - top)
            at = slice(c * CHUNK, (c + 1) * CHUNK)
            expo[at] = value
            dprod[at] = dp
            tops.append(top)
            masses.append(fold(value, jnp.sum))
            dsums.append(fold(value * dp, jnp.sum))
        top = functools.reduce(jnp.maximum, tops)
        factors = [jnp.exp2(t - top) for t in tops]
        mass = sum(f * m for f, m in zip(factors, masses))
        dsum = sum(f * d for f, d in zip(factors, dsums))
        centre = dsum / jnp.maximum(mass, 1e-30)
        for c, f in enumerate(factors):
            at = slice(c * CHUNK, (c + 1) * CHUNK)
            value = expo[at] * f
            expo_ref[at, columns] = value.astype(BF16)
            spread_ref[at, columns] = (value * (dprod[at] - centre)).astype(BF16)
        stats_ref[0:1, columns] = top
        stats_ref[1:2, columns] = mass
        stats_ref[2:3, columns] = dsum
        return carry

    lax.fori_loop(0, half // together, group, 0)


def attend(where, ring, kv_up, own, other, score_scale, together=TOGETHER):
    blocks, (size, packed) = len(ring), ring[0].shape
    half, d_lat = kv_up.shape[0] // 2, kv_up.shape[1]
    total = blocks * size
    rows = total // half
    keys, c_width = own.shape
    smem = pl.BlockSpec(memory_space=pltpu.SMEM)
    vmem = pl.BlockSpec(memory_space=pltpu.VMEM)
    return pl.pallas_call(
        functools.partial(attend_kernel, score_scale, blocks, together),
        out_shape=(
            jax.ShapeDtypeStruct((total, c_width), BF16),
            jax.ShapeDtypeStruct((total, d_lat), BF16),
            jax.ShapeDtypeStruct((2 * keys, total), BF16),
            jax.ShapeDtypeStruct((2 * keys, total), BF16),
            jax.ShapeDtypeStruct((3, total), F32),
            jax.ShapeDtypeStruct((rows, 128), F32),
            jax.ShapeDtypeStruct((half, d_lat, kv_up.shape[2] // 2), BF16),
        ),
        in_specs=[smem] + [vmem] * (blocks + 3),
        out_specs=[vmem] * 7,
        scratch_shapes=[
            pltpu.VMEM((packed // 128, total, 128), F32),
            pltpu.VMEM((2 * keys, together * rows), F32),
            pltpu.VMEM((2 * keys, together * rows), F32),
        ],
        compiler_params=pltpu.CompilerParams(vmem_limit_bytes=ATTEND_MIB * MIB),
        cost_estimate=pl.CostEstimate(
            flops=2 * 2 * keys * total * (c_width + d_lat),
            bytes_accessed=8 * keys * total,
            transcendentals=2 * keys * total,
        ),
    )(where, *ring, kv_up, own, other)


def project_kernel(p, cache_ref, spread_ref, expo_ref, *out_refs):
    width = out_refs[0].shape[1]
    columns = slice(p * width, (p + 1) * width)
    for terms_ref, out_ref in zip((spread_ref, expo_ref), out_refs):
        out_ref[...] = jnp.dot(
            cache_ref[...], terms_ref[:, columns], preferred_element_type=F32
        )


def project(p, parts, cache_t, spread, expo):
    c_width, keys = cache_t.shape
    width = spread.shape[1] // parts
    vmem = pl.BlockSpec(memory_space=pltpu.VMEM)
    return pl.pallas_call(
        functools.partial(project_kernel, p),
        out_shape=(jax.ShapeDtypeStruct((c_width, width), F32),) * 2,
        in_specs=[vmem] * 3,
        out_specs=[vmem] * 2,
        compiler_params=pltpu.CompilerParams(vmem_limit_bytes=PROJECT_MIB * MIB),
        cost_estimate=pl.CostEstimate(
            flops=4 * keys * width * c_width, bytes_accessed=4 * keys * width, transcendentals=0
        ),
    )(cache_t, spread, expo)


def row_gains(where_ref, lens_ref, ratio_ref, rows_of_core):
    rows = ratio_ref.shape[0]
    place = lax.broadcasted_iota(jnp.int32, (rows, 1), 0)
    turn = place % (2 * rows_of_core) >= rows_of_core
    swapped = jnp.where(turn, place - rows_of_core, place + rows_of_core)
    place = jnp.where(where_ref[0] == 1, swapped, place)
    ratio = ratio_ref[:, 0:1]
    segments = lens_ref.shape[0]
    members = []
    first = jnp.int32(0)
    for k in range(segments):
        last = first + lens_ref[k]
        members.append((place >= first) & (place < last))
        first = last
    sums = [jnp.sum(jnp.where(m, ratio, 0.0), axis=0, keepdims=True) for m in members]
    gains = jnp.zeros((rows, 1), F32)
    for p in range(segments // 2):
        margin = BETA * (sums[2 * p] - sums[2 * p + 1])
        weight = LOSS_SCALE * BETA / (1.0 + jnp.exp(margin))
        gains = jnp.where(members[2 * p], -weight, gains)
        gains = jnp.where(members[2 * p + 1], weight, gains)
    return gains


def row_factors(joined_refs, own_ref):
    joined = functools.reduce(join_stats, [ref[...] for ref in joined_refs])
    centre = own_ref[2:3] / jnp.maximum(own_ref[1:2], 1e-30)
    factor = jnp.exp2(own_ref[0:1] - joined[0:1]) / joined[1:2]
    return factor, joined[2:3] / joined[1:2] - centre


def weigh_kernel(scale, rows_of_core, where_ref, lens_ref, *refs):
    joined_refs, (own_ref, ratio_ref, query_ref, grad_ref) = refs[:4], refs[4:8]
    with_spread_ref, with_expo_ref, factors_ref = refs[8:]
    total = query_ref.shape[0]
    d_lat = grad_ref.shape[1]
    rows = ratio_ref.shape[0]
    gains = row_gains(where_ref, lens_ref, ratio_ref, rows_of_core)
    factor, shift = row_factors(joined_refs, own_ref)
    gains_row = jnp.broadcast_to(gains, (rows, 128)).T[0:1]
    gains_row = jnp.concatenate([gains_row] * (total // rows), axis=1)
    factors_ref[0:1] = scale * gains_row * factor
    factors_ref[1:2] = shift
    sublane = lax.broadcasted_iota(jnp.int32, (8, total), 0)
    both = jnp.where(sublane == 0, factor, shift).T
    for h in range(total // rows):
        at = slice(h * rows, (h + 1) * rows)
        factor = both[at, 0:1] * gains
        query = scale * factor * query_ref[at, :].astype(F32)
        with_spread_ref[at, :] = query.astype(BF16)
        moved = both[at, 1:2] * query
        with_expo_ref[at, :d_lat] = (
            factor * grad_ref[at, :].astype(F32) - moved[:, :d_lat]
        ).astype(BF16)
        with_expo_ref[at, d_lat:] = (-moved[:, d_lat:]).astype(BF16)


def weigh(where, lens, joined, stats, ratio, query, grad, scale, q_dev):
    total, c_width = query.shape
    smem = pl.BlockSpec(memory_space=pltpu.SMEM)
    vmem = pl.BlockSpec(memory_space=pltpu.VMEM)
    weight = jax.ShapeDtypeStruct((total, c_width), BF16)
    inputs = (*joined, stats, ratio, query, grad)
    return pl.pallas_call(
        functools.partial(weigh_kernel, scale, q_dev),
        out_shape=(weight, weight, jax.ShapeDtypeStruct((2, total), F32)),
        in_specs=[smem, smem] + [vmem] * len(inputs),
        out_specs=[vmem] * 3,
        compiler_params=pltpu.CompilerParams(vmem_limit_bytes=WEIGH_MIB * MIB),
        cost_estimate=pl.CostEstimate(
            flops=10 * total * c_width, bytes_accessed=8 * total * c_width, transcendentals=0
        ),
    )(where, lens, *inputs)


def query_kernel(where_ref, factors_ref, key_ref, *refs):
    by_spread_refs, by_expo_refs = refs[:-2:2], refs[1:-2:2]
    keep_ref, send_ref = refs[-2:]
    half, d_lat = key_ref.shape[:2]
    blocks, size = keep_ref.shape[0], keep_ref.shape[2] // 2
    rows = 2 * size * blocks
    second = where_ref[4 + blocks] == 1
    together = half // len(by_spread_refs)
    for p in range(half // 2):
        part = 2 * p // together
        columns = slice(p * 2 * rows, (p + 1) * 2 * rows)
        first = (2 * p % together) * rows
        inside = slice(first, first + 2 * rows)
        full = factors_ref[1:2, columns] * by_expo_refs[part][:, inside]
        full = factors_ref[0:1, columns] * (by_spread_refs[part][:, inside] - full)
        heads = []
        for j in range(2):
            at = slice(j * rows, (j + 1) * rows)
            nope = lax.dot_general(
                full[:d_lat, at].astype(BF16),
                key_ref[2 * p + j],
                (((0,), (0,)), ((), ())),
                preferred_element_type=F32,
            )
            heads.append(jnp.concatenate([nope, full[d_lat:, at].T], axis=1))
        for b in range(blocks):
            pieces = []
            for x in range(2):
                first = (2 * b + x) * size
                pieces.append(jnp.concatenate([y[first : first + size] for y in heads], axis=0))
            keep_ref[b, p] = jnp.where(second, pieces[1], pieces[0]).astype(BF16)
            send_ref[b, p] = jnp.where(second, pieces[0], pieces[1]).astype(BF16)


def query_terms(where, factors, w_key, projected, blocks, q_width):
    half = w_key.shape[0]
    rows = factors.shape[1] // half
    smem = pl.BlockSpec(memory_space=pltpu.SMEM)
    vmem = pl.BlockSpec(memory_space=pltpu.VMEM)
    dq = jax.ShapeDtypeStruct((blocks, half // 2, rows // blocks, q_width), BF16)
    return pl.pallas_call(
        query_kernel,
        out_shape=(dq, dq),
        in_specs=[smem] + [vmem] * (2 + len(projected)),
        out_specs=[vmem] * 2,
        compiler_params=pltpu.CompilerParams(vmem_limit_bytes=WEIGH_MIB * MIB),
        cost_estimate=pl.CostEstimate(
            flops=4 * w_key.size * rows, bytes_accessed=8 * w_key.size, transcendentals=0
        ),
    )(where, factors, w_key, *projected)


def cache_kernel(part, d_lat, order_ref, spread_ref, expo_ref, with_spread_ref, with_expo_ref, *refs):
    adds, outs = refs[:-2], refs[-2:]
    keys = spread_ref.shape[3]

    def gather(ref):
        blocks = [ref[part, order_ref[i], order_ref[4 + i]] for i in range(4)]
        return jnp.concatenate(blocks, axis=0)

    out = jnp.dot(gather(spread_ref), with_spread_ref[...], preferred_element_type=F32)
    out = out + jnp.dot(gather(expo_ref), with_expo_ref[...], preferred_element_type=F32)
    rope = out.shape[1] - d_lat
    for i in range(4):
        first = (i % 2) * d_lat
        lat = slice(first, first + d_lat)
        first = 2 * d_lat + (i % 2) * rope
        tail = slice(first, first + rope)
        at = slice(i * keys, (i + 1) * keys)
        for lanes, value in ((lat, out[at, :d_lat]), (tail, out[at, d_lat:])):
            if adds:
                value = value + adds[i // 2][:, lanes].astype(F32)
            outs[i // 2][:, lanes] = value.astype(outs[i // 2].dtype)


def cache_terms(part, order, d_lat, spread, expo, with_spread, with_expo, dtypes, adds=()):
    total, c_width = with_spread.shape
    keys = spread.shape[3]
    smem = pl.BlockSpec(memory_space=pltpu.SMEM)
    vmem = pl.BlockSpec(memory_space=pltpu.VMEM)
    return pl.pallas_call(
        functools.partial(cache_kernel, part, d_lat),
        out_shape=[jax.ShapeDtypeStruct((keys, 2 * c_width), dtype) for dtype in dtypes],
        in_specs=[smem] + [vmem] * (4 + len(adds)),
        out_specs=[vmem, vmem],
        compiler_params=pltpu.CompilerParams(vmem_limit_bytes=CACHE_MIB * MIB),
        cost_estimate=pl.CostEstimate(
            flops=16 * keys * total * c_width,
            bytes_accessed=16 * keys * total,
            transcendentals=0,
        ),
    )(order, spread, expo, with_spread, with_expo, *adds)


def unfold(x, d_lat):
    rope = x.shape[1] // 2 - d_lat
    return [
        jnp.concatenate(
            [
                x[:, i * d_lat : (i + 1) * d_lat],
                x[:, 2 * d_lat + i * rope : 2 * d_lat + (i + 1) * rope],
            ],
            axis=1,
        )
        for i in range(2)
    ]


def fold_rows(x, d_lat, out_ref):
    size = x.shape[0] // 2
    rope = x.shape[1] - d_lat
    for i in range(2):
        part = x[i * size : (i + 1) * size].astype(BF16)
        out_ref[:, i * d_lat : (i + 1) * d_lat] = part[:, :d_lat]
        out_ref[:, 2 * d_lat + i * rope : 2 * d_lat + (i + 1) * rope] = part[:, d_lat:]


def forward_kernel(d_lat, keep_ref, arrived_ref, *out_refs):
    total = keep_ref[...].astype(F32) + arrived_ref[...].astype(F32)
    for block, out_ref in zip(unfold(total, d_lat), out_refs):
        fold_rows(block, d_lat, out_ref)


def turn_kernel(d_lat, own_ref, arrived_ref, send_ref, keep_ref):
    send, keep = unfold(own_ref[...] + arrived_ref[...].astype(F32), d_lat)
    fold_rows(send, d_lat, send_ref)
    keep_ref[...] = keep


def finish_kernel(d_lat, keep_ref, *refs):
    total = keep_ref[...]
    for arrived_ref in refs[:-1]:
        total = total + jnp.concatenate(unfold(arrived_ref[...].astype(F32), d_lat), axis=0)
    refs[-1][...] = total.T.astype(BF16)


def small(kernel, out_shape, *operands):
    vmem = pl.BlockSpec(memory_space=pltpu.VMEM)
    return pl.pallas_call(
        kernel,
        out_shape=out_shape,
        in_specs=[vmem] * len(operands),
        out_specs=jax.tree.map(lambda _: vmem, out_shape),
        compiler_params=pltpu.CompilerParams(vmem_limit_bytes=6 * MIB),
    )(*operands)


def per_device(queries, out_grad, kv_up, latent_cache, token_ratio, pair_lens, prompt_len):
    ctx_index = lax.axis_index("ctx")
    head_index = lax.axis_index("head")
    core = ctx_index & 1
    x_lo = (ctx_index >> 1) & 1
    z = ctx_index >> 2
    nz = lax.axis_size("ctx") // 4
    ny = lax.axis_size("head") // 2
    y = head_index & (ny - 1)
    x_hi = (head_index >= ny).astype(jnp.int32)
    other_core = lambda i: i ^ 1
    other_x_lo = lambda i: i ^ 2
    z_groups = [[4 * k + j for k in range(nz)] for j in range(4)]

    q_dev, heads, q_width = queries.shape
    p_dev, c_width = latent_cache.shape
    d_lat = kv_up.shape[1]
    d_rope = c_width - d_lat
    d_nope = q_width - d_rope
    half = heads // 2
    scale = q_width ** (-0.5)

    where = [core, ctx_index * p_dev, (ctx_index ^ 1) * p_dev, prompt_len[0]]
    where = where + [(z + k) & (nz - 1) for k in range(nz)] + [x_lo]
    where = jnp.stack(where).astype(jnp.int32)
    mine, theirs = pack(where, token_ratio, queries, out_grad)
    block = jnp.concatenate([mine, permute(theirs, "ctx", other_core)], 0)
    block = in_order(block, permute(block, "ctx", other_x_lo), x_lo == 1, 0)
    block, latent_cache = lax.optimization_barrier((block, latent_cache))
    own_t = latent_cache.T
    other_t = permute(latent_cache, "ctx", other_core).T
    (own_keys,) = stage(own_t)
    cache_t, other_keys = stage(other_t, own_t)
    along_z = lambda x, k: permute(x, "ctx", lambda i: (i + 4 * k) % (4 * nz))
    ring = [block] + [None] * (nz - 1)
    ring[nz - 2], ring[2] = along_z(block, 2), along_z(block, -2)
    ring[nz - 1], ring[1] = along_z(block, 1), along_z(block, -1)
    ring[nz - 4] = along_z(ring[nz - 2], 2)
    ring[nz - 3], ring[3] = along_z(ring[nz - 2], 1), along_z(ring[2], -1)

    query, grad, expo, spread, stats, ratio, w_key = attend(
        where, ring, kv_up, own_keys, other_keys, scale * LOG2E
    )

    joined = [stats]
    projected = []
    parts = 2
    for group, partners in enumerate(((2, 4, 6), (8, 16, 24))):
        mine = joined[0] if group == 0 else join(*joined)
        joined = [permute(mine, "ctx", lambda i, k=k: i ^ k) for k in partners]
        terms = project(group, parts, cache_t, spread, expo)
        joined = lax.optimization_barrier((*joined, *terms))
        projected += joined[len(partners) :]
        joined = (mine, *joined[: len(partners)])
    with_spread, with_expo, factors = weigh(
        where, pair_lens, joined, stats, ratio, query, grad, scale, q_dev
    )
    dq_keep, dq_send = query_terms(where, factors, w_key, projected, nz, q_width)
    dq_pair = permute(dq_send, "ctx", other_x_lo)
    keys = p_dev // (2 * ny)
    there, here = 1 - x_hi, x_hi
    along = [(y + k) & (ny - 1) for k in (0, 1, 2, 3)]
    orders = [
        [there, there, here, here, along[2], along[1], along[2], along[1]],
        [there, here, there, here, along[3], along[3], along[0], along[0]],
    ]
    orders = [jnp.stack(order).astype(jnp.int32) for order in orders]
    shape = (2, 2, ny, keys, spread.shape[1])
    operands = (d_lat, spread.reshape(shape), expo.reshape(shape), with_spread, with_expo)
    adds = []
    sends = cache_terms(1, orders[0], *operands, (BF16, BF16))
    later, *sends = lax.optimization_barrier((orders[1], *sends))
    adds.append([permute(x, "ctx", other_core) for x in sends])
    sends = cache_terms(1, later, *operands, (BF16, BF16))
    adds.append([permute(x, "ctx", other_core) for x in sends])
    to_x_hi = lambda x: permute(x, "head", lambda i: (i + ny) % (2 * ny))
    to_y = lambda x, k: permute(x, "head", lambda i: (i // ny) * ny + (i + k) % ny)
    send, keep = cache_terms(0, orders[0], *operands, (BF16, F32), adds[0])
    later, send = lax.optimization_barrier((orders[1], send))
    from_x_hi = to_x_hi(send)
    send, own = cache_terms(0, later, *operands, (BF16, F32), adds[1])
    dq = (dq_keep.astype(F32) + dq_pair.astype(F32)).astype(BF16)
    send, dq = lax.optimization_barrier((send, dq))
    from_y = to_y(send, 3)

    half_rows = jax.ShapeDtypeStruct((keys // 2, 2 * c_width), BF16)
    block = jax.ShapeDtypeStruct((keys, c_width), F32)
    sends = small(
        functools.partial(forward_kernel, d_lat), (half_rows, half_rows), keep, from_x_hi
    )
    arrived = [to_y(sends[0], 2), to_y(sends[1], 1)]
    send, keep = small(functools.partial(turn_kernel, d_lat), (half_rows, block), own, from_y)
    arrived.append(to_x_hi(send))
    cache_grad = small(
        functools.partial(finish_kernel, d_lat),
        jax.ShapeDtypeStruct((c_width, keys), BF16),
        keep,
        *arrived,
    ).T

    dq = lax.all_to_all(dq, "ctx", 0, 0, axis_index_groups=z_groups)
    dq = jnp.sum(dq.astype(F32), axis=0).astype(BF16).reshape(half, 2, q_dev, q_width)
    theirs = permute(dq[:, 1], "ctx", other_core)
    query_grad = jnp.transpose(in_order(dq[:, 0], theirs, core == 1, 0), (1, 0, 2))

    return (query_grad, cache_grad)


def solution(mesh):
    placed = (
        P("ctx", "head", None),
        P("ctx", "head", None),
        P("head", None, None),
        P("ctx", None),
        P("ctx"),
        P(),
        P(),
    )
    return jax.shard_map(
        per_device,
        mesh=mesh,
        in_specs=placed,
        out_specs=(P("ctx", "head", None), P(("ctx", "head"), None)),
        check_vma=False,
    )
```

```python
import functools

import jax
import jax.numpy as jnp
from jax import lax
from jax.experimental import pallas as pl
from jax.experimental.pallas import tpu as pltpu
from jax.sharding import PartitionSpec as P

BETA = 0.1
LOSS_SCALE = 2048.0
LOG2E = 1.4426950408889634
NEVER = -1e30
FLOOR = -1e29
F32 = jnp.float32
BF16 = jnp.bfloat16
CHUNK = 1024
TOGETHER = 4
PACKED = 384
MIB = 1024 * 1024
ATTEND_MIB = 24
PROJECT_MIB = 10
WEIGH_MIB = 16
CACHE_MIB = 20


def permute(x, axis, to):
    return lax.ppermute(x, axis, [(i, to(i)) for i in range(lax.axis_size(axis))])


def in_order(mine, theirs, second, axis):
    return jnp.where(
        second,
        jnp.concatenate([theirs, mine], axis),
        jnp.concatenate([mine, theirs], axis),
    )


def join_stats(first, second):
    top = jnp.maximum(first[0:1], second[0:1])
    both = jnp.exp2(first[0:1] - top) * first + jnp.exp2(second[0:1] - top) * second
    return jnp.where(lax.broadcasted_iota(jnp.int32, both.shape, 0) == 0, top, both)


def join_kernel(*refs):
    refs[-1][...] = functools.reduce(join_stats, [ref[...] for ref in refs[:-1]])


def join(*parts):
    vmem = pl.BlockSpec(memory_space=pltpu.VMEM)
    return pl.pallas_call(
        join_kernel,
        out_shape=jax.ShapeDtypeStruct(parts[0].shape, F32),
        in_specs=[vmem] * len(parts),
        out_specs=vmem,
        compiler_params=pltpu.CompilerParams(vmem_limit_bytes=MIB),
    )(*parts)


def against(x, y):
    return lax.dot_general(x, y, (((1,), (1,)), ((), ())), preferred_element_type=F32)


def pack_kernel(where_ref, ratio_ref, queries_ref, out_grad_ref, mine_ref, theirs_ref):
    q_dev, heads, q_width = queries_ref.shape
    d_nope = out_grad_ref.shape[2]
    half = heads // 2
    d_rope = q_width - d_nope
    lane = lax.broadcasted_iota(jnp.int32, (heads, PACKED - 2 * d_nope - d_rope), 1)
    second = where_ref[0] == 1
    mine, theirs = [], []
    for j in range(q_dev):
        query = queries_ref[j].astype(F32)
        ratio = jnp.full(lane.shape, ratio_ref[j], F32)
        high = ratio.astype(BF16).astype(F32)
        middle = (ratio - high).astype(BF16).astype(F32)
        terms = jnp.where(lane == 0, high, jnp.where(lane == 1, middle, ratio - high - middle))
        terms = jnp.where(lane < 3, terms, 0.0)
        row = [query[:, :d_nope], out_grad_ref[j].astype(F32), query[:, d_nope:], terms]
        row = jnp.concatenate(row, axis=1)
        mine.append(jnp.where(second, row[half:], row[:half]))
        theirs.append(jnp.where(second, row[:half], row[half:]))
    mine_ref[...] = jnp.concatenate(mine, axis=0).astype(BF16)
    theirs_ref[...] = jnp.concatenate(theirs, axis=0).astype(BF16)


def pack(where, token_ratio, queries, out_grad):
    q_dev, heads = queries.shape[:2]
    smem = pl.BlockSpec(memory_space=pltpu.SMEM)
    vmem = pl.BlockSpec(memory_space=pltpu.VMEM)
    packed = jax.ShapeDtypeStruct((q_dev * heads // 2, PACKED), BF16)
    return pl.pallas_call(
        pack_kernel,
        out_shape=(packed, packed),
        in_specs=[smem, smem, vmem, vmem],
        out_specs=[vmem, vmem],
        compiler_params=pltpu.CompilerParams(vmem_limit_bytes=2 * MIB),
        cost_estimate=pl.CostEstimate(flops=0, bytes_accessed=32 * MIB, transcendentals=0),
    )(where, token_ratio, queries, out_grad)


def stage_kernel(cache_ref, *refs):
    refs[-1][...] = cache_ref[...].T
    if len(refs) == 3:
        own_ref, both_ref = refs[:2]
        keys = own_ref.shape[1]
        both_ref[:, :keys] = own_ref[...]
        both_ref[:, keys:] = cache_ref[...]


def stage(cache_t, own_t=None):
    c_width, keys = cache_t.shape
    vmem = pl.BlockSpec(memory_space=pltpu.VMEM)
    turned = jax.ShapeDtypeStruct((keys, c_width), BF16)
    both = jax.ShapeDtypeStruct((c_width, 2 * keys), BF16)
    operands, outs = ((cache_t,), (turned,)) if own_t is None else ((cache_t, own_t), (both, turned))
    return pl.pallas_call(
        stage_kernel,
        out_shape=outs,
        in_specs=[vmem] * len(operands),
        out_specs=[vmem] * len(outs),
        compiler_params=pltpu.CompilerParams(vmem_limit_bytes=10 * MIB),
        cost_estimate=pl.CostEstimate(
            flops=keys * c_width, bytes_accessed=4 * keys * c_width, transcendentals=0
        ),
    )(*operands)


def attend_kernel(score_scale, blocks, together, where_ref, *refs):
    ring_refs, refs = refs[:blocks], refs[blocks:]
    kv_ref, own_ref, other_ref, query_ref, grad_ref, expo_ref, spread_ref, stats_ref = refs[:8]
    ratio_ref, key_ref, raw, expo, dprod = refs[8:]
    size = ring_refs[0].shape[0]
    half, d_lat, d_nope = kv_ref.shape[0] // 2, kv_ref.shape[1], kv_ref.shape[2] // 2
    rows = size * blocks // half
    first_head = where_ref[0] * half
    d_rope = query_ref.shape[1] - d_lat
    keys = own_ref.shape[0]
    width = together * rows
    for k in range(blocks):
        first = pl.multiple_of(where_ref[4 + k] * size, size)
        for part in range(PACKED // 128):
            lanes = slice(part * 128, (part + 1) * 128)
            raw[part, pl.ds(first, size), :] = ring_refs[k][:, lanes].astype(F32)

    def of_head(h, part):
        return raw[part, pl.ds(h, rows, stride=half), :]

    terms = of_head(0, 2)
    lane = lax.broadcasted_iota(jnp.int32, terms.shape, 1)
    terms = jnp.where((lane >= d_rope) & (lane < d_rope + 3), terms, 0.0)
    ratio_ref[...] = jnp.broadcast_to(jnp.sum(terms, axis=1, keepdims=True), ratio_ref.shape)

    def fold(x, join):
        return join(join(x.reshape(CHUNK // 8, 8, width), axis=0), axis=0, keepdims=True)

    def group(p, carry):
        for j in range(together):
            h = p * together + j
            at = pl.ds(pl.multiple_of(h * rows, rows), rows)
            key_ref[h] = kv_ref[first_head + h, :, :d_nope]
            lat = against(of_head(h, 0).astype(BF16), key_ref[h])
            query_ref[at, :d_lat] = lat.astype(BF16)
            rope = of_head(h, 2)[:, :d_rope]
            query_ref[at, d_lat:] = rope.astype(BF16)
            lat = against(of_head(h, 1).astype(BF16), kv_ref[first_head + h, :, d_nope:])
            grad_ref[at, :] = lat.astype(BF16)
        columns = pl.ds(pl.multiple_of(p * width, width), width)
        tops, masses, dsums = [], [], []
        for c in range(2 * keys // CHUNK):
            first = c * CHUNK % keys
            ref, base = (own_ref, where_ref[1]) if c * CHUNK < keys else (other_ref, where_ref[2])
            score = against(ref[first : first + CHUNK, :], query_ref[columns, :]) * score_scale
            dp = against(ref[first : first + CHUNK, :d_lat], grad_ref[columns, :])
            key = base + first + lax.broadcasted_iota(jnp.int32, (CHUNK, 1), 0)
            score = jnp.where(key < where_ref[3], score, NEVER)
            top = jnp.maximum(fold(score, jnp.max), FLOOR)
            value = jnp.exp2(score - top)
            at = slice(c * CHUNK, (c + 1) * CHUNK)
            expo[at] = value
            dprod[at] = dp
            tops.append(top)
            masses.append(fold(value, jnp.sum))
            dsums.append(fold(value * dp, jnp.sum))
        top = functools.reduce(jnp.maximum, tops)
        factors = [jnp.exp2(t - top) for t in tops]
        mass = sum(f * m for f, m in zip(factors, masses))
        dsum = sum(f * d for f, d in zip(factors, dsums))
        centre = dsum / jnp.maximum(mass, 1e-30)
        for c, f in enumerate(factors):
            at = slice(c * CHUNK, (c + 1) * CHUNK)
            value = expo[at] * f
            expo_ref[at, columns] = value.astype(BF16)
            spread_ref[at, columns] = (value * (dprod[at] - centre)).astype(BF16)
        stats_ref[0:1, columns] = top
        stats_ref[1:2, columns] = mass
        stats_ref[2:3, columns] = dsum
        return carry

    lax.fori_loop(0, half // together, group, 0)


def attend(where, ring, kv_up, own, other, score_scale, together=TOGETHER):
    blocks, (size, packed) = len(ring), ring[0].shape
    half, d_lat = kv_up.shape[0] // 2, kv_up.shape[1]
    total = blocks * size
    rows = total // half
    keys, c_width = own.shape
    smem = pl.BlockSpec(memory_space=pltpu.SMEM)
    vmem = pl.BlockSpec(memory_space=pltpu.VMEM)
    return pl.pallas_call(
        functools.partial(attend_kernel, score_scale, blocks, together),
        out_shape=(
            jax.ShapeDtypeStruct((total, c_width), BF16),
            jax.ShapeDtypeStruct((total, d_lat), BF16),
            jax.ShapeDtypeStruct((2 * keys, total), BF16),
            jax.ShapeDtypeStruct((2 * keys, total), BF16),
            jax.ShapeDtypeStruct((3, total), F32),
            jax.ShapeDtypeStruct((rows, 128), F32),
            jax.ShapeDtypeStruct((half, d_lat, kv_up.shape[2] // 2), BF16),
        ),
        in_specs=[smem] + [vmem] * (blocks + 3),
        out_specs=[vmem] * 7,
        scratch_shapes=[
            pltpu.VMEM((packed // 128, total, 128), F32),
            pltpu.VMEM((2 * keys, together * rows), F32),
            pltpu.VMEM((2 * keys, together * rows), F32),
        ],
        compiler_params=pltpu.CompilerParams(vmem_limit_bytes=ATTEND_MIB * MIB),
        cost_estimate=pl.CostEstimate(
            flops=2 * 2 * keys * total * (c_width + d_lat),
            bytes_accessed=8 * keys * total,
            transcendentals=2 * keys * total,
        ),
    )(where, *ring, kv_up, own, other)


def project_kernel(p, cache_ref, spread_ref, expo_ref, *out_refs):
    width = out_refs[0].shape[1]
    columns = slice(p * width, (p + 1) * width)
    for terms_ref, out_ref in zip((spread_ref, expo_ref), out_refs):
        out_ref[...] = jnp.dot(
            cache_ref[...], terms_ref[:, columns], preferred_element_type=F32
        )


def project(p, parts, cache_t, spread, expo):
    c_width, keys = cache_t.shape
    width = spread.shape[1] // parts
    vmem = pl.BlockSpec(memory_space=pltpu.VMEM)
    return pl.pallas_call(
        functools.partial(project_kernel, p),
        out_shape=(jax.ShapeDtypeStruct((c_width, width), F32),) * 2,
        in_specs=[vmem] * 3,
        out_specs=[vmem] * 2,
        compiler_params=pltpu.CompilerParams(vmem_limit_bytes=PROJECT_MIB * MIB),
        cost_estimate=pl.CostEstimate(
            flops=4 * keys * width * c_width, bytes_accessed=4 * keys * width, transcendentals=0
        ),
    )(cache_t, spread, expo)


def row_gains(where_ref, lens_ref, ratio_ref, rows_of_core):
    rows = ratio_ref.shape[0]
    place = lax.broadcasted_iota(jnp.int32, (rows, 1), 0)
    turn = place % (2 * rows_of_core) >= rows_of_core
    swapped = jnp.where(turn, place - rows_of_core, place + rows_of_core)
    place = jnp.where(where_ref[0] == 1, swapped, place)
    ratio = ratio_ref[:, 0:1]
    segments = lens_ref.shape[0]
    members = []
    first = jnp.int32(0)
    for k in range(segments):
        last = first + lens_ref[k]
        members.append((place >= first) & (place < last))
        first = last
    sums = [jnp.sum(jnp.where(m, ratio, 0.0), axis=0, keepdims=True) for m in members]
    gains = jnp.zeros((rows, 1), F32)
    for p in range(segments // 2):
        margin = BETA * (sums[2 * p] - sums[2 * p + 1])
        weight = LOSS_SCALE * BETA / (1.0 + jnp.exp(margin))
        gains = jnp.where(members[2 * p], -weight, gains)
        gains = jnp.where(members[2 * p + 1], weight, gains)
    return gains


def row_factors(joined_refs, own_ref):
    joined = functools.reduce(join_stats, [ref[...] for ref in joined_refs])
    centre = own_ref[2:3] / jnp.maximum(own_ref[1:2], 1e-30)
    factor = jnp.exp2(own_ref[0:1] - joined[0:1]) / joined[1:2]
    return factor, joined[2:3] / joined[1:2] - centre


def weigh_kernel(scale, rows_of_core, where_ref, lens_ref, *refs):
    joined_refs, (own_ref, ratio_ref, query_ref, grad_ref) = refs[:4], refs[4:8]
    with_spread_ref, with_expo_ref, factors_ref = refs[8:]
    total = query_ref.shape[0]
    d_lat = grad_ref.shape[1]
    rows = ratio_ref.shape[0]
    gains = row_gains(where_ref, lens_ref, ratio_ref, rows_of_core)
    factor, shift = row_factors(joined_refs, own_ref)
    gains_row = jnp.broadcast_to(gains, (rows, 128)).T[0:1]
    gains_row = jnp.concatenate([gains_row] * (total // rows), axis=1)
    factors_ref[0:1] = scale * gains_row * factor
    factors_ref[1:2] = shift
    sublane = lax.broadcasted_iota(jnp.int32, (8, total), 0)
    both = jnp.where(sublane == 0, factor, shift).T
    for h in range(total // rows):
        at = slice(h * rows, (h + 1) * rows)
        factor = both[at, 0:1] * gains
        query = scale * factor * query_ref[at, :].astype(F32)
        with_spread_ref[at, :] = query.astype(BF16)
        moved = both[at, 1:2] * query
        with_expo_ref[at, :d_lat] = (
            factor * grad_ref[at, :].astype(F32) - moved[:, :d_lat]
        ).astype(BF16)
        with_expo_ref[at, d_lat:] = (-moved[:, d_lat:]).astype(BF16)


def weigh(where, lens, joined, stats, ratio, query, grad, scale, q_dev):
    total, c_width = query.shape
    smem = pl.BlockSpec(memory_space=pltpu.SMEM)
    vmem = pl.BlockSpec(memory_space=pltpu.VMEM)
    weight = jax.ShapeDtypeStruct((total, c_width), BF16)
    inputs = (*joined, stats, ratio, query, grad)
    return pl.pallas_call(
        functools.partial(weigh_kernel, scale, q_dev),
        out_shape=(weight, weight, jax.ShapeDtypeStruct((2, total), F32)),
        in_specs=[smem, smem] + [vmem] * len(inputs),
        out_specs=[vmem] * 3,
        compiler_params=pltpu.CompilerParams(vmem_limit_bytes=WEIGH_MIB * MIB),
        cost_estimate=pl.CostEstimate(
            flops=10 * total * c_width, bytes_accessed=8 * total * c_width, transcendentals=0
        ),
    )(where, lens, *inputs)


def query_kernel(where_ref, factors_ref, key_ref, *refs):
    by_spread_refs, by_expo_refs = refs[:-2:2], refs[1:-2:2]
    keep_ref, send_ref = refs[-2:]
    half, d_lat = key_ref.shape[:2]
    blocks, size = keep_ref.shape[0], keep_ref.shape[2] // 2
    rows = 2 * size * blocks
    second = where_ref[4 + blocks] == 1
    together = half // len(by_spread_refs)
    for p in range(half // 2):
        part = 2 * p // together
        columns = slice(p * 2 * rows, (p + 1) * 2 * rows)
        first = (2 * p % together) * rows
        inside = slice(first, first + 2 * rows)
        full = factors_ref[1:2, columns] * by_expo_refs[part][:, inside]
        full = factors_ref[0:1, columns] * (by_spread_refs[part][:, inside] - full)
        heads = []
        for j in range(2):
            at = slice(j * rows, (j + 1) * rows)
            nope = lax.dot_general(
                full[:d_lat, at].astype(BF16),
                key_ref[2 * p + j],
                (((0,), (0,)), ((), ())),
                preferred_element_type=F32,
            )
            heads.append(jnp.concatenate([nope, full[d_lat:, at].T], axis=1))
        for b in range(blocks):
            pieces = []
            for x in range(2):
                first = (2 * b + x) * size
                pieces.append(jnp.concatenate([y[first : first + size] for y in heads], axis=0))
            keep_ref[b, p] = jnp.where(second, pieces[1], pieces[0]).astype(BF16)
            send_ref[b, p] = jnp.where(second, pieces[0], pieces[1]).astype(BF16)


def query_terms(where, factors, w_key, projected, blocks, q_width):
    half = w_key.shape[0]
    rows = factors.shape[1] // half
    smem = pl.BlockSpec(memory_space=pltpu.SMEM)
    vmem = pl.BlockSpec(memory_space=pltpu.VMEM)
    dq = jax.ShapeDtypeStruct((blocks, half // 2, rows // blocks, q_width), BF16)
    return pl.pallas_call(
        query_kernel,
        out_shape=(dq, dq),
        in_specs=[smem] + [vmem] * (2 + len(projected)),
        out_specs=[vmem] * 2,
        compiler_params=pltpu.CompilerParams(vmem_limit_bytes=WEIGH_MIB * MIB),
        cost_estimate=pl.CostEstimate(
            flops=4 * w_key.size * rows, bytes_accessed=8 * w_key.size, transcendentals=0
        ),
    )(where, factors, w_key, *projected)


def cache_kernel(part, d_lat, order_ref, spread_ref, expo_ref, with_spread_ref, with_expo_ref, *refs):
    adds, outs = refs[:-2], refs[-2:]
    keys = spread_ref.shape[3]

    def gather(ref):
        blocks = [ref[part, order_ref[i], order_ref[4 + i]] for i in range(4)]
        return jnp.concatenate(blocks, axis=0)

    out = jnp.dot(gather(spread_ref), with_spread_ref[...], preferred_element_type=F32)
    out = out + jnp.dot(gather(expo_ref), with_expo_ref[...], preferred_element_type=F32)
    rope = out.shape[1] - d_lat
    for i in range(4):
        first = (i % 2) * d_lat
        lat = slice(first, first + d_lat)
        first = 2 * d_lat + (i % 2) * rope
        tail = slice(first, first + rope)
        at = slice(i * keys, (i + 1) * keys)
        for lanes, value in ((lat, out[at, :d_lat]), (tail, out[at, d_lat:])):
            if adds:
                value = value + adds[i // 2][:, lanes].astype(F32)
            outs[i // 2][:, lanes] = value.astype(outs[i // 2].dtype)


def cache_terms(part, order, d_lat, spread, expo, with_spread, with_expo, dtypes, adds=()):
    total, c_width = with_spread.shape
    keys = spread.shape[3]
    smem = pl.BlockSpec(memory_space=pltpu.SMEM)
    vmem = pl.BlockSpec(memory_space=pltpu.VMEM)
    return pl.pallas_call(
        functools.partial(cache_kernel, part, d_lat),
        out_shape=[jax.ShapeDtypeStruct((keys, 2 * c_width), dtype) for dtype in dtypes],
        in_specs=[smem] + [vmem] * (4 + len(adds)),
        out_specs=[vmem, vmem],
        compiler_params=pltpu.CompilerParams(vmem_limit_bytes=CACHE_MIB * MIB),
        cost_estimate=pl.CostEstimate(
            flops=16 * keys * total * c_width,
            bytes_accessed=16 * keys * total,
            transcendentals=0,
        ),
    )(order, spread, expo, with_spread, with_expo, *adds)


def unfold(x, d_lat):
    rope = x.shape[1] // 2 - d_lat
    return [
        jnp.concatenate(
            [
                x[:, i * d_lat : (i + 1) * d_lat],
                x[:, 2 * d_lat + i * rope : 2 * d_lat + (i + 1) * rope],
            ],
            axis=1,
        )
        for i in range(2)
    ]


def fold_rows(x, d_lat, out_ref):
    size = x.shape[0] // 2
    rope = x.shape[1] - d_lat
    for i in range(2):
        part = x[i * size : (i + 1) * size].astype(BF16)
        out_ref[:, i * d_lat : (i + 1) * d_lat] = part[:, :d_lat]
        out_ref[:, 2 * d_lat + i * rope : 2 * d_lat + (i + 1) * rope] = part[:, d_lat:]


def forward_kernel(d_lat, keep_ref, arrived_ref, *out_refs):
    total = keep_ref[...].astype(F32) + arrived_ref[...].astype(F32)
    for block, out_ref in zip(unfold(total, d_lat), out_refs):
        fold_rows(block, d_lat, out_ref)


def turn_kernel(d_lat, own_ref, arrived_ref, send_ref, keep_ref):
    send, keep = unfold(own_ref[...] + arrived_ref[...].astype(F32), d_lat)
    fold_rows(send, d_lat, send_ref)
    keep_ref[...] = keep


def finish_kernel(d_lat, keep_ref, *refs):
    total = keep_ref[...]
    for arrived_ref in refs[:-1]:
        total = total + jnp.concatenate(unfold(arrived_ref[...].astype(F32), d_lat), axis=0)
    refs[-1][...] = total.T.astype(BF16)


def small(kernel, out_shape, *operands):
    vmem = pl.BlockSpec(memory_space=pltpu.VMEM)
    return pl.pallas_call(
        kernel,
        out_shape=out_shape,
        in_specs=[vmem] * len(operands),
        out_specs=jax.tree.map(lambda _: vmem, out_shape),
        compiler_params=pltpu.CompilerParams(vmem_limit_bytes=6 * MIB),
    )(*operands)


def per_device(queries, out_grad, kv_up, latent_cache, token_ratio, pair_lens, prompt_len):
    ctx_index = lax.axis_index("ctx")
    head_index = lax.axis_index("head")
    core = ctx_index & 1
    x_lo = (ctx_index >> 1) & 1
    z = ctx_index >> 2
    nz = lax.axis_size("ctx") // 4
    ny = lax.axis_size("head") // 2
    y = head_index & (ny - 1)
    x_hi = (head_index >= ny).astype(jnp.int32)
    other_core = lambda i: i ^ 1
    other_x_lo = lambda i: i ^ 2
    z_groups = [[4 * k + j for k in range(nz)] for j in range(4)]

    q_dev, heads, q_width = queries.shape
    p_dev, c_width = latent_cache.shape
    d_lat = kv_up.shape[1]
    d_rope = c_width - d_lat
    d_nope = q_width - d_rope
    half = heads // 2
    scale = q_width ** (-0.5)

    where = [core, ctx_index * p_dev, (ctx_index ^ 1) * p_dev, prompt_len[0]]
    where = where + [(z + k) & (nz - 1) for k in range(nz)] + [x_lo]
    where = jnp.stack(where).astype(jnp.int32)
    own_t = latent_cache.T
    other_t = permute(latent_cache, "ctx", other_core).T
    mine, theirs = pack(where, token_ratio, queries, out_grad)
    block = jnp.concatenate([mine, permute(theirs, "ctx", other_core)], 0)
    block = in_order(block, permute(block, "ctx", other_x_lo), x_lo == 1, 0)
    (own_keys,) = stage(own_t)
    cache_t, other_keys = stage(other_t, own_t)
    along_z = lambda x, k: permute(x, "ctx", lambda i: (i + 4 * k) % (4 * nz))
    ring = [block] + [None] * (nz - 1)
    ring[nz - 2], ring[2] = along_z(block, 2), along_z(block, -2)
    ring[nz - 1], ring[1] = along_z(block, 1), along_z(block, -1)
    ring[nz - 4] = along_z(ring[nz - 2], 2)
    ring[nz - 3], ring[3] = along_z(ring[nz - 2], 1), along_z(ring[2], -1)

    query, grad, expo, spread, stats, ratio, w_key = attend(
        where, ring, kv_up, own_keys, other_keys, scale * LOG2E
    )

    joined = [stats]
    projected = []
    parts = 2
    for group, partners in enumerate(((2, 4, 6), (8, 16, 24))):
        mine = joined[0] if group == 0 else join(*joined)
        joined = [permute(mine, "ctx", lambda i, k=k: i ^ k) for k in partners]
        terms = project(group, parts, cache_t, spread, expo)
        joined = lax.optimization_barrier((*joined, *terms))
        projected += joined[len(partners) :]
        joined = (mine, *joined[: len(partners)])
    with_spread, with_expo, factors = weigh(
        where, pair_lens, joined, stats, ratio, query, grad, scale, q_dev
    )
    dq_keep, dq_send = query_terms(where, factors, w_key, projected, nz, q_width)
    dq_pair = permute(dq_send, "ctx", other_x_lo)
    keys = p_dev // (2 * ny)
    there, here = 1 - x_hi, x_hi
    along = [(y + k) & (ny - 1) for k in (0, 1, 2, 3)]
    orders = [
        [there, there, here, here, along[2], along[1], along[2], along[1]],
        [there, here, there, here, along[3], along[3], along[0], along[0]],
    ]
    orders = [jnp.stack(order).astype(jnp.int32) for order in orders]
    shape = (2, 2, ny, keys, spread.shape[1])
    operands = (d_lat, spread.reshape(shape), expo.reshape(shape), with_spread, with_expo)
    adds = []
    sends = cache_terms(1, orders[0], *operands, (BF16, BF16))
    later, *sends = lax.optimization_barrier((orders[1], *sends))
    adds.append([permute(x, "ctx", other_core) for x in sends])
    sends = cache_terms(1, later, *operands, (BF16, BF16))
    adds.append([permute(x, "ctx", other_core) for x in sends])
    to_x_hi = lambda x: permute(x, "head", lambda i: (i + ny) % (2 * ny))
    to_y = lambda x, k: permute(x, "head", lambda i: (i // ny) * ny + (i + k) % ny)
    send, keep = cache_terms(0, orders[0], *operands, (BF16, F32), adds[0])
    later, send = lax.optimization_barrier((orders[1], send))
    from_x_hi = to_x_hi(send)
    send, own = cache_terms(0, later, *operands, (BF16, F32), adds[1])
    dq = (dq_keep.astype(F32) + dq_pair.astype(F32)).astype(BF16)
    send, dq = lax.optimization_barrier((send, dq))
    from_y = to_y(send, 3)

    half_rows = jax.ShapeDtypeStruct((keys // 2, 2 * c_width), BF16)
    block = jax.ShapeDtypeStruct((keys, c_width), F32)
    sends = small(
        functools.partial(forward_kernel, d_lat), (half_rows, half_rows), keep, from_x_hi
    )
    arrived = [to_y(sends[0], 2), to_y(sends[1], 1)]
    send, keep = small(functools.partial(turn_kernel, d_lat), (half_rows, block), own, from_y)
    arrived.append(to_x_hi(send))
    cache_grad = small(
        functools.partial(finish_kernel, d_lat),
        jax.ShapeDtypeStruct((c_width, keys), BF16),
        keep,
        *arrived,
    ).T

    dq = lax.all_to_all(dq, "ctx", 0, 0, axis_index_groups=z_groups)
    dq = jnp.sum(dq.astype(F32), axis=0).astype(BF16).reshape(half, 2, q_dev, q_width)
    theirs = permute(dq[:, 1], "ctx", other_core)
    query_grad = jnp.transpose(in_order(dq[:, 0], theirs, core == 1, 0), (1, 0, 2))

    return (query_grad, cache_grad)


def solution(mesh):
    placed = (
        P("ctx", "head", None),
        P("ctx", "head", None),
        P("head", None, None),
        P("ctx", None),
        P("ctx"),
        P(),
        P(),
    )
    return jax.shard_map(
        per_device,
        mesh=mesh,
        in_specs=placed,
        out_specs=(P("ctx", "head", None), P(("ctx", "head"), None)),
        check_vma=False,
    )
```

```python
import functools

import jax
import jax.numpy as jnp
from jax import lax
from jax.experimental import pallas as pl
from jax.experimental.pallas import tpu as pltpu
from jax.sharding import PartitionSpec as P

BETA = 0.1
LOSS_SCALE = 2048.0
LOG2E = 1.4426950408889634
NEVER = -1e30
FLOOR = -1e29
F32 = jnp.float32
BF16 = jnp.bfloat16
CHUNK = 1024
PAIR_LANES = 640
MIB = 1024 * 1024
ATTEND_MIB = 24
PROJECT_MIB = 10
WEIGH_MIB = 16
CACHE_MIB = 20


def permute(x, axis, to):
    return lax.ppermute(x, axis, [(i, to(i)) for i in range(lax.axis_size(axis))])


def in_order(mine, theirs, second, axis):
    return jnp.where(
        second,
        jnp.concatenate([theirs, mine], axis),
        jnp.concatenate([mine, theirs], axis),
    )


def join_stats(first, second):
    top = jnp.maximum(first[0:1], second[0:1])
    both = jnp.exp2(first[0:1] - top) * first + jnp.exp2(second[0:1] - top) * second
    row = lax.broadcasted_iota(jnp.int32, both.shape, 0)
    return jnp.where(row == 0, top, jnp.where(row == 3, first + second, both))


def join_kernel(*refs):
    refs[-1][...] = functools.reduce(join_stats, [ref[...] for ref in refs[:-1]])


def join(*parts):
    vmem = pl.BlockSpec(memory_space=pltpu.VMEM)
    return pl.pallas_call(
        join_kernel,
        out_shape=jax.ShapeDtypeStruct(parts[0].shape, F32),
        in_specs=[vmem] * len(parts),
        out_specs=vmem,
        compiler_params=pltpu.CompilerParams(vmem_limit_bytes=MIB),
    )(*parts)


def against(x, y):
    return lax.dot_general(x, y, (((1,), (1,)), ((), ())), preferred_element_type=F32)


def pack_kernel(where_ref, queries_ref, out_grad_ref, mine_ref, theirs_ref, wide, rows):
    q_dev, heads, q_width = queries_ref.shape
    d_nope = out_grad_ref.shape[2]
    d_rope = q_width - d_nope
    pairs = heads // 4
    for j in range(q_dev):
        wide[j, :, :q_width] = queries_ref[j].astype(F32)
        wide[j, :, 2 * d_nope :] = out_grad_ref[j].astype(F32)
        for half in range(2):
            for second in range(2):
                first = (2 * half + second) * pairs
                of = slice(first, first + pairs)
                to = slice(j * pairs, (j + 1) * pairs)
                lane = 2 * d_nope * second
                rows[half, to, lane : lane + d_nope] = wide[j, of, :d_nope]
                rows[half, to, lane + d_nope : lane + 2 * d_nope] = wide[j, of, 2 * d_nope :]
                lane = 4 * d_nope + d_rope * second
                rows[half, to, lane : lane + d_rope] = wide[j, of, d_nope:q_width]
    other = where_ref[0] == 1
    mine_ref[...] = jnp.where(other, rows[1], rows[0]).astype(BF16)
    theirs_ref[...] = jnp.where(other, rows[0], rows[1]).astype(BF16)


def pack(where, queries, out_grad):
    q_dev, heads, d_nope = out_grad.shape
    smem = pl.BlockSpec(memory_space=pltpu.SMEM)
    vmem = pl.BlockSpec(memory_space=pltpu.VMEM)
    size = q_dev * heads // 4
    packed = jax.ShapeDtypeStruct((size, PAIR_LANES), BF16)
    return pl.pallas_call(
        pack_kernel,
        out_shape=(packed, packed),
        in_specs=[smem, vmem, vmem],
        out_specs=[vmem, vmem],
        scratch_shapes=[
            pltpu.VMEM((q_dev, heads, 3 * d_nope), F32),
            pltpu.VMEM((2, size, PAIR_LANES), F32),
        ],
        compiler_params=pltpu.CompilerParams(vmem_limit_bytes=2 * MIB),
        cost_estimate=pl.CostEstimate(flops=0, bytes_accessed=32 * MIB, transcendentals=0),
    )(where, queries, out_grad)


def stage_kernel(cache_ref, out_ref):
    out_ref[...] = cache_ref[...].T


def stage_all_kernel(where_ref, cache_ref, own_ref, kv_ref, out_ref, both_ref, key_ref):
    keys = own_ref.shape[1]
    half, _, d_nope = key_ref.shape
    out_ref[...] = cache_ref[...].T
    both_ref[:, :keys] = own_ref[...]
    both_ref[:, keys:] = cache_ref[...]
    for h in range(half):
        key_ref[h] = kv_ref[where_ref[0] * half + h, :, :d_nope]


def stage(cache_t):
    c_width, keys = cache_t.shape
    vmem = pl.BlockSpec(memory_space=pltpu.VMEM)
    return pl.pallas_call(
        stage_kernel,
        out_shape=jax.ShapeDtypeStruct((keys, c_width), BF16),
        in_specs=[vmem],
        out_specs=vmem,
        compiler_params=pltpu.CompilerParams(vmem_limit_bytes=6 * MIB),
        cost_estimate=pl.CostEstimate(
            flops=keys * c_width, bytes_accessed=4 * keys * c_width, transcendentals=0
        ),
    )(cache_t)


def stage_all(where, cache_t, own_t, kv_up):
    c_width, keys = cache_t.shape
    heads, d_lat, width = kv_up.shape
    smem = pl.BlockSpec(memory_space=pltpu.SMEM)
    vmem = pl.BlockSpec(memory_space=pltpu.VMEM)
    return pl.pallas_call(
        stage_all_kernel,
        out_shape=(
            jax.ShapeDtypeStruct((keys, c_width), BF16),
            jax.ShapeDtypeStruct((c_width, 2 * keys), BF16),
            jax.ShapeDtypeStruct((heads // 2, d_lat, width // 2), BF16),
        ),
        in_specs=[smem] + [vmem] * 3,
        out_specs=[vmem] * 3,
        compiler_params=pltpu.CompilerParams(vmem_limit_bytes=16 * MIB),
        cost_estimate=pl.CostEstimate(
            flops=keys * c_width, bytes_accessed=8 * keys * c_width, transcendentals=0
        ),
    )(where, cache_t, own_t, kv_up)


def attend_kernel(score_scale, blocks, together, where_ref, *refs):
    ring_refs, refs = refs[:blocks], refs[blocks:]
    kv_ref, key_ref, own_ref, other_ref, ratio_ref = refs[:5]
    query_ref, grad_ref, expo_ref, spread_ref, stats_ref, raw, expo, dprod = refs[5:]
    size = ring_refs[0].shape[0]
    half, d_lat, d_nope = kv_ref.shape[0] // 2, kv_ref.shape[1], kv_ref.shape[2] // 2
    pairs = half // 2
    rows = size * blocks // pairs
    first_head = where_ref[0] * half
    d_rope = query_ref.shape[1] - d_lat
    keys = own_ref.shape[0]
    width = together * rows
    for k in range(blocks):
        first = pl.multiple_of(where_ref[4 + k] * size, size)
        for part in range(PAIR_LANES // 128):
            lanes = slice(part * 128, (part + 1) * 128)
            raw[part, pl.ds(first, size), :] = ring_refs[k][:, lanes].astype(F32)
    stats_ref[3:4] = ratio_ref[...]

    def of_pair(j, part):
        return raw[part, pl.ds(j, rows, stride=pairs), :]

    def fold(x, join):
        return join(join(x.reshape(CHUNK // 8, 8, width), axis=0), axis=0, keepdims=True)

    def group(p, carry):
        for j in range(together):
            h = p * together + j
            at = pl.ds(pl.multiple_of(h * rows, rows), rows)
            lat = against(of_pair(j, 2 * p).astype(BF16), key_ref[h])
            query_ref[at, :d_lat] = lat.astype(BF16)
            rope = of_pair(j, 4)
            rope = jnp.where(p == 0, rope[:, :d_rope], rope[:, d_rope:])
            query_ref[at, d_lat:] = rope.astype(BF16)
            lat = against(of_pair(j, 2 * p + 1).astype(BF16), kv_ref[first_head + h, :, d_nope:])
            grad_ref[at, :] = lat.astype(BF16)
        columns = pl.ds(pl.multiple_of(p * width, width), width)
        tops, masses, dsums = [], [], []
        for c in range(2 * keys // CHUNK):
            first = c * CHUNK % keys
            ref, base = (own_ref, where_ref[1]) if c * CHUNK < keys else (other_ref, where_ref[2])
            score = against(ref[first : first + CHUNK, :], query_ref[columns, :]) * score_scale
            dp = against(ref[first : first + CHUNK, :d_lat], grad_ref[columns, :])
            key = base + first + lax.broadcasted_iota(jnp.int32, (CHUNK, 1), 0)
            score = jnp.where(key < where_ref[3], score, NEVER)
            top = jnp.maximum(fold(score, jnp.max), FLOOR)
            value = jnp.exp2(score - top)
            at = slice(c * CHUNK, (c + 1) * CHUNK)
            expo[at] = value
            dprod[at] = dp
            tops.append(top)
            masses.append(fold(value, jnp.sum))
            dsums.append(fold(value * dp, jnp.sum))
        top = functools.reduce(jnp.maximum, tops)
        factors = [jnp.exp2(t - top) for t in tops]
        mass = sum(f * m for f, m in zip(factors, masses))
        dsum = sum(f * d for f, d in zip(factors, dsums))
        centre = dsum / jnp.maximum(mass, 1e-30)
        for c, f in enumerate(factors):
            at = slice(c * CHUNK, (c + 1) * CHUNK)
            value = expo[at] * f
            expo_ref[at, columns] = value.astype(BF16)
            spread_ref[at, columns] = (value * (dprod[at] - centre)).astype(BF16)
        stats_ref[0:1, columns] = top
        stats_ref[1:2, columns] = mass
        stats_ref[2:3, columns] = dsum
        return carry

    lax.fori_loop(0, half // together, group, 0)


def attend(where, ring, kv_up, w_key, own, other, ratio, score_scale):
    blocks, size = len(ring), ring[0].shape[0]
    half, d_lat = kv_up.shape[0] // 2, kv_up.shape[1]
    together = half // 2
    rows = blocks * size // together
    total = half * rows
    keys, c_width = own.shape
    smem = pl.BlockSpec(memory_space=pltpu.SMEM)
    vmem = pl.BlockSpec(memory_space=pltpu.VMEM)
    return pl.pallas_call(
        functools.partial(attend_kernel, score_scale, blocks, together),
        out_shape=(
            jax.ShapeDtypeStruct((total, c_width), BF16),
            jax.ShapeDtypeStruct((total, d_lat), BF16),
            jax.ShapeDtypeStruct((2 * keys, total), BF16),
            jax.ShapeDtypeStruct((2 * keys, total), BF16),
            jax.ShapeDtypeStruct((4, total), F32),
        ),
        in_specs=[smem] + [vmem] * (blocks + 5),
        out_specs=[vmem] * 5,
        scratch_shapes=[
            pltpu.VMEM((PAIR_LANES // 128, blocks * size, 128), F32),
            pltpu.VMEM((2 * keys, together * rows), F32),
            pltpu.VMEM((2 * keys, together * rows), F32),
        ],
        compiler_params=pltpu.CompilerParams(vmem_limit_bytes=ATTEND_MIB * MIB),
        cost_estimate=pl.CostEstimate(
            flops=2 * 2 * keys * total * (c_width + d_lat),
            bytes_accessed=8 * keys * total,
            transcendentals=2 * keys * total,
        ),
    )(where, *ring, kv_up, w_key, own, other, ratio)


def project_kernel(p, cache_ref, spread_ref, expo_ref, *out_refs):
    width = out_refs[0].shape[1]
    columns = slice(p * width, (p + 1) * width)
    for terms_ref, out_ref in zip((spread_ref, expo_ref), out_refs):
        out_ref[...] = jnp.dot(
            cache_ref[...], terms_ref[:, columns], preferred_element_type=F32
        )


def project(p, parts, cache_t, spread, expo):
    c_width, keys = cache_t.shape
    width = spread.shape[1] // parts
    vmem = pl.BlockSpec(memory_space=pltpu.VMEM)
    return pl.pallas_call(
        functools.partial(project_kernel, p),
        out_shape=(jax.ShapeDtypeStruct((c_width, width), F32),) * 2,
        in_specs=[vmem] * 3,
        out_specs=[vmem] * 2,
        compiler_params=pltpu.CompilerParams(vmem_limit_bytes=PROJECT_MIB * MIB),
        cost_estimate=pl.CostEstimate(
            flops=4 * keys * width * c_width, bytes_accessed=4 * keys * width, transcendentals=0
        ),
    )(cache_t, spread, expo)


def row_gains(where_ref, lens_ref, ratio, rows_of_core):
    place = lax.broadcasted_iota(jnp.int32, ratio.shape, 1)
    turn = place % (2 * rows_of_core) >= rows_of_core
    swapped = jnp.where(turn, place - rows_of_core, place + rows_of_core)
    place = jnp.where(where_ref[0] == 1, swapped, place)
    segments = lens_ref.shape[0]
    members = []
    first = jnp.int32(0)
    for k in range(segments):
        last = first + lens_ref[k]
        members.append((place >= first) & (place < last))
        first = last
    sums = [jnp.sum(jnp.where(m, ratio, 0.0), axis=1, keepdims=True) for m in members]
    gains = jnp.zeros(ratio.shape, F32)
    for p in range(segments // 2):
        margin = BETA * (sums[2 * p] - sums[2 * p + 1])
        weight = LOSS_SCALE * BETA / (1.0 + jnp.exp(margin))
        gains = jnp.where(members[2 * p], -weight, gains)
        gains = jnp.where(members[2 * p + 1], weight, gains)
    return gains


def row_factors(joined_refs, own_ref):
    joined = functools.reduce(join_stats, [ref[...] for ref in joined_refs])
    centre = own_ref[2:3] / jnp.maximum(own_ref[1:2], 1e-30)
    factor = jnp.exp2(own_ref[0:1] - joined[0:1]) / joined[1:2]
    return joined[3:4], factor, joined[2:3] / joined[1:2] - centre


def weigh_kernel(scale, rows, rows_of_core, where_ref, lens_ref, *refs):
    joined_refs, (own_ref, query_ref, grad_ref) = refs[:4], refs[4:7]
    with_spread_ref, with_expo_ref, factors_ref = refs[7:]
    total = query_ref.shape[0]
    d_lat = grad_ref.shape[1]
    ratio, factor, shift = row_factors(joined_refs, own_ref)
    gains_row = row_gains(where_ref, lens_ref, ratio[:, :rows], rows_of_core)
    gains = jnp.broadcast_to(gains_row, (8, rows)).T[:, 0:1]
    gains_row = jnp.concatenate([gains_row] * (total // rows), axis=1)
    factors_ref[0:1] = scale * gains_row * factor
    factors_ref[1:2] = shift
    sublane = lax.broadcasted_iota(jnp.int32, (8, total), 0)
    both = jnp.where(sublane == 0, factor, shift).T
    for h in range(total // rows):
        at = slice(h * rows, (h + 1) * rows)
        factor = both[at, 0:1] * gains
        query = scale * factor * query_ref[at, :].astype(F32)
        with_spread_ref[at, :] = query.astype(BF16)
        moved = both[at, 1:2] * query
        with_expo_ref[at, :d_lat] = (
            factor * grad_ref[at, :].astype(F32) - moved[:, :d_lat]
        ).astype(BF16)
        with_expo_ref[at, d_lat:] = (-moved[:, d_lat:]).astype(BF16)


def weigh(where, lens, joined, stats, query, grad, scale, rows, q_dev):
    total, c_width = query.shape
    smem = pl.BlockSpec(memory_space=pltpu.SMEM)
    vmem = pl.BlockSpec(memory_space=pltpu.VMEM)
    weight = jax.ShapeDtypeStruct((total, c_width), BF16)
    inputs = (*joined, stats, query, grad)
    return pl.pallas_call(
        functools.partial(weigh_kernel, scale, rows, q_dev),
        out_shape=(weight, weight, jax.ShapeDtypeStruct((2, total), F32)),
        in_specs=[smem, smem] + [vmem] * len(inputs),
        out_specs=[vmem] * 3,
        compiler_params=pltpu.CompilerParams(vmem_limit_bytes=WEIGH_MIB * MIB),
        cost_estimate=pl.CostEstimate(
            flops=10 * total * c_width, bytes_accessed=8 * total * c_width, transcendentals=0
        ),
    )(where, lens, *inputs)


def query_kernel(where_ref, factors_ref, key_ref, *refs):
    by_spread_refs, by_expo_refs = refs[:-2:2], refs[1:-2:2]
    keep_ref, send_ref = refs[-2:]
    half, d_lat = key_ref.shape[:2]
    blocks, size = keep_ref.shape[0], keep_ref.shape[2] // 2
    rows = 2 * size * blocks
    second = where_ref[4 + blocks] == 1
    together = half // len(by_spread_refs)
    for p in range(half // 2):
        part = 2 * p // together
        columns = slice(p * 2 * rows, (p + 1) * 2 * rows)
        first = (2 * p % together) * rows
        inside = slice(first, first + 2 * rows)
        full = factors_ref[1:2, columns] * by_expo_refs[part][:, inside]
        full = factors_ref[0:1, columns] * (by_spread_refs[part][:, inside] - full)
        heads = []
        for j in range(2):
            at = slice(j * rows, (j + 1) * rows)
            nope = lax.dot_general(
                full[:d_lat, at].astype(BF16),
                key_ref[2 * p + j],
                (((0,), (0,)), ((), ())),
                preferred_element_type=F32,
            )
            heads.append(jnp.concatenate([nope, full[d_lat:, at].T], axis=1))
        for b in range(blocks):
            pieces = []
            for x in range(2):
                first = (2 * b + x) * size
                pieces.append(jnp.concatenate([y[first : first + size] for y in heads], axis=0))
            keep_ref[b, p] = jnp.where(second, pieces[1], pieces[0]).astype(BF16)
            send_ref[b, p] = jnp.where(second, pieces[0], pieces[1]).astype(BF16)


def query_terms(where, factors, w_key, projected, blocks, q_width):
    half = w_key.shape[0]
    rows = factors.shape[1] // half
    smem = pl.BlockSpec(memory_space=pltpu.SMEM)
    vmem = pl.BlockSpec(memory_space=pltpu.VMEM)
    dq = jax.ShapeDtypeStruct((blocks, half // 2, rows // blocks, q_width), BF16)
    return pl.pallas_call(
        query_kernel,
        out_shape=(dq, dq),
        in_specs=[smem] + [vmem] * (2 + len(projected)),
        out_specs=[vmem] * 2,
        compiler_params=pltpu.CompilerParams(vmem_limit_bytes=WEIGH_MIB * MIB),
        cost_estimate=pl.CostEstimate(
            flops=4 * w_key.size * rows, bytes_accessed=8 * w_key.size, transcendentals=0
        ),
    )(where, factors, w_key, *projected)


def cache_kernel(part, d_lat, order_ref, spread_ref, expo_ref, with_spread_ref, with_expo_ref, *refs):
    adds, outs = refs[:-2], refs[-2:]
    keys = spread_ref.shape[3]

    def gather(ref):
        blocks = [ref[part, order_ref[i], order_ref[4 + i]] for i in range(4)]
        return jnp.concatenate(blocks, axis=0)

    out = jnp.dot(gather(spread_ref), with_spread_ref[...], preferred_element_type=F32)
    out = out + jnp.dot(gather(expo_ref), with_expo_ref[...], preferred_element_type=F32)
    rope = out.shape[1] - d_lat
    for i in range(4):
        first = (i % 2) * d_lat
        lat = slice(first, first + d_lat)
        first = 2 * d_lat + (i % 2) * rope
        tail = slice(first, first + rope)
        at = slice(i * keys, (i + 1) * keys)
        for lanes, value in ((lat, out[at, :d_lat]), (tail, out[at, d_lat:])):
            if adds:
                value = value + adds[i // 2][:, lanes].astype(F32)
            outs[i // 2][:, lanes] = value.astype(outs[i // 2].dtype)


def cache_terms(part, order, d_lat, spread, expo, with_spread, with_expo, dtypes, adds=()):
    total, c_width = with_spread.shape
    keys = spread.shape[3]
    smem = pl.BlockSpec(memory_space=pltpu.SMEM)
    vmem = pl.BlockSpec(memory_space=pltpu.VMEM)
    return pl.pallas_call(
        functools.partial(cache_kernel, part, d_lat),
        out_shape=[jax.ShapeDtypeStruct((keys, 2 * c_width), dtype) for dtype in dtypes],
        in_specs=[smem] + [vmem] * (4 + len(adds)),
        out_specs=[vmem, vmem],
        compiler_params=pltpu.CompilerParams(vmem_limit_bytes=CACHE_MIB * MIB),
        cost_estimate=pl.CostEstimate(
            flops=16 * keys * total * c_width,
            bytes_accessed=16 * keys * total,
            transcendentals=0,
        ),
    )(order, spread, expo, with_spread, with_expo, *adds)


def unfold(x, d_lat):
    rope = x.shape[1] // 2 - d_lat
    return [
        jnp.concatenate(
            [
                x[:, i * d_lat : (i + 1) * d_lat],
                x[:, 2 * d_lat + i * rope : 2 * d_lat + (i + 1) * rope],
            ],
            axis=1,
        )
        for i in range(2)
    ]


def fold_rows(x, d_lat, out_ref):
    size = x.shape[0] // 2
    rope = x.shape[1] - d_lat
    for i in range(2):
        part = x[i * size : (i + 1) * size].astype(BF16)
        out_ref[:, i * d_lat : (i + 1) * d_lat] = part[:, :d_lat]
        out_ref[:, 2 * d_lat + i * rope : 2 * d_lat + (i + 1) * rope] = part[:, d_lat:]


def forward_kernel(d_lat, keep_ref, arrived_ref, *out_refs):
    total = keep_ref[...].astype(F32) + arrived_ref[...].astype(F32)
    for block, out_ref in zip(unfold(total, d_lat), out_refs):
        fold_rows(block, d_lat, out_ref)


def turn_kernel(d_lat, own_ref, arrived_ref, send_ref, keep_ref):
    send, keep = unfold(own_ref[...] + arrived_ref[...].astype(F32), d_lat)
    fold_rows(send, d_lat, send_ref)
    keep_ref[...] = keep


def finish_kernel(d_lat, keep_ref, *refs):
    total = keep_ref[...]
    for arrived_ref in refs[:-1]:
        total = total + jnp.concatenate(unfold(arrived_ref[...].astype(F32), d_lat), axis=0)
    refs[-1][...] = total.T.astype(BF16)


def small(kernel, out_shape, *operands):
    vmem = pl.BlockSpec(memory_space=pltpu.VMEM)
    return pl.pallas_call(
        kernel,
        out_shape=out_shape,
        in_specs=[vmem] * len(operands),
        out_specs=jax.tree.map(lambda _: vmem, out_shape),
        compiler_params=pltpu.CompilerParams(vmem_limit_bytes=6 * MIB),
    )(*operands)


def per_device(queries, out_grad, kv_up, latent_cache, token_ratio, pair_lens, prompt_len):
    ctx_index = lax.axis_index("ctx")
    head_index = lax.axis_index("head")
    core = ctx_index & 1
    x_lo = (ctx_index >> 1) & 1
    z = ctx_index >> 2
    nz = lax.axis_size("ctx") // 4
    ny = lax.axis_size("head") // 2
    y = head_index & (ny - 1)
    x_hi = (head_index >= ny).astype(jnp.int32)
    other_core = lambda i: i ^ 1
    other_x_lo = lambda i: i ^ 2
    z_groups = [[4 * k + j for k in range(nz)] for j in range(4)]

    q_dev, heads, q_width = queries.shape
    p_dev, c_width = latent_cache.shape
    d_lat = kv_up.shape[1]
    d_rope = c_width - d_lat
    d_nope = q_width - d_rope
    half = heads // 2
    scale = q_width ** (-0.5)

    where = [core, ctx_index * p_dev, (ctx_index ^ 1) * p_dev, prompt_len[0]]
    where = where + [(z + k) & (nz - 1) for k in range(nz)] + [x_lo]
    where = jnp.stack(where).astype(jnp.int32)
    own_t = latent_cache.T
    other_t = permute(latent_cache, "ctx", other_core).T
    rows = 4 * nz * q_dev
    ratio = jnp.concatenate([token_ratio, permute(token_ratio, "ctx", other_core)])
    chip = jnp.arange(half * rows, dtype=jnp.int32)[None, :] // (2 * q_dev) == ctx_index // 2
    ratio = jnp.where(chip, jnp.tile(ratio, half * rows // (2 * q_dev))[None, :], 0.0)
    mine, theirs = pack(where, queries, out_grad)
    block = jnp.concatenate([mine, permute(theirs, "ctx", other_core)], 0)
    block = in_order(block, permute(block, "ctx", other_x_lo), x_lo == 1, 0)
    own_keys = stage(own_t)
    other_keys, cache_t, w_key = stage_all(where, other_t, own_t, kv_up)
    along_z = lambda x, k: permute(x, "ctx", lambda i: (i + 4 * k) % (4 * nz))
    ring = [block] + [None] * (nz - 1)
    ring[nz - 2], ring[2] = along_z(block, 2), along_z(block, -2)
    ring[nz - 1], ring[1] = along_z(block, 1), along_z(block, -1)
    ring[nz - 4] = along_z(ring[nz - 2], 2)
    ring[nz - 3], ring[3] = along_z(ring[nz - 2], 1), along_z(ring[2], -1)

    query, grad, expo, spread, stats = attend(
        where, ring, kv_up, w_key, own_keys, other_keys, ratio, scale * LOG2E
    )

    joined = [stats]
    projected = []
    parts = 2
    for group, partners in enumerate(((2, 4, 6), (8, 16, 24))):
        mine = joined[0] if group == 0 else join(*joined)
        joined = [permute(mine, "ctx", lambda i, k=k: i ^ k) for k in partners]
        terms = project(group, parts, cache_t, spread, expo)
        joined = lax.optimization_barrier((*joined, *terms))
        projected += joined[len(partners) :]
        joined = (mine, *joined[: len(partners)])
    with_spread, with_expo, factors = weigh(
        where, pair_lens, joined, stats, query, grad, scale, rows, q_dev
    )
    dq_keep, dq_send = query_terms(where, factors, w_key, projected, nz, q_width)
    dq_pair = permute(dq_send, "ctx", other_x_lo)
    keys = p_dev // (2 * ny)
    there, here = 1 - x_hi, x_hi
    along = [(y + k) & (ny - 1) for k in (0, 1, 2, 3)]
    orders = [
        [there, there, here, here, along[2], along[1], along[2], along[1]],
        [there, here, there, here, along[3], along[3], along[0], along[0]],
    ]
    orders = [jnp.stack(order).astype(jnp.int32) for order in orders]
    shape = (2, 2, ny, keys, spread.shape[1])
    operands = (d_lat, spread.reshape(shape), expo.reshape(shape), with_spread, with_expo)
    adds = []
    sends = cache_terms(1, orders[0], *operands, (BF16, BF16))
    later, *sends = lax.optimization_barrier((orders[1], *sends))
    adds.append([permute(x, "ctx", other_core) for x in sends])
    sends = cache_terms(1, later, *operands, (BF16, BF16))
    adds.append([permute(x, "ctx", other_core) for x in sends])
    to_x_hi = lambda x: permute(x, "head", lambda i: (i + ny) % (2 * ny))
    to_y = lambda x, k: permute(x, "head", lambda i: (i // ny) * ny + (i + k) % ny)
    send, keep = cache_terms(0, orders[0], *operands, (BF16, F32), adds[0])
    later, send = lax.optimization_barrier((orders[1], send))
    from_x_hi = to_x_hi(send)
    send, own = cache_terms(0, later, *operands, (BF16, F32), adds[1])
    dq = (dq_keep.astype(F32) + dq_pair.astype(F32)).astype(BF16)
    send, dq = lax.optimization_barrier((send, dq))
    from_y = to_y(send, 3)

    half_rows = jax.ShapeDtypeStruct((keys // 2, 2 * c_width), BF16)
    block = jax.ShapeDtypeStruct((keys, c_width), F32)
    sends = small(
        functools.partial(forward_kernel, d_lat), (half_rows, half_rows), keep, from_x_hi
    )
    arrived = [to_y(sends[0], 2), to_y(sends[1], 1)]
    send, keep = small(functools.partial(turn_kernel, d_lat), (half_rows, block), own, from_y)
    arrived.append(to_x_hi(send))
    cache_grad = small(
        functools.partial(finish_kernel, d_lat),
        jax.ShapeDtypeStruct((c_width, keys), BF16),
        keep,
        *arrived,
    ).T

    dq = lax.all_to_all(dq, "ctx", 0, 0, axis_index_groups=z_groups)
    dq = jnp.sum(dq.astype(F32), axis=0).astype(BF16).reshape(half, 2, q_dev, q_width)
    theirs = permute(dq[:, 1], "ctx", other_core)
    query_grad = jnp.transpose(in_order(dq[:, 0], theirs, core == 1, 0), (1, 0, 2))

    return (query_grad, cache_grad)


def solution(mesh):
    placed = (
        P("ctx", "head", None),
        P("ctx", "head", None),
        P("head", None, None),
        P("ctx", None),
        P("ctx"),
        P(),
        P(),
    )
    return jax.shard_map(
        per_device,
        mesh=mesh,
        in_specs=placed,
        out_specs=(P("ctx", "head", None), P(("ctx", "head"), None)),
        check_vma=False,
    )
```

```python
import functools

import jax
import jax.numpy as jnp
from jax import lax
from jax.experimental import pallas as pl
from jax.experimental.pallas import tpu as pltpu
from jax.sharding import PartitionSpec as P

BETA = 0.1
LOSS_SCALE = 2048.0
LOG2E = 1.4426950408889634
NEVER = -1e30
FLOOR = -1e29
F32 = jnp.float32
BF16 = jnp.bfloat16
CHUNK = 1024
PAIR_LANES = 640
MIB = 1024 * 1024
ATTEND_MIB = 24
PROJECT_MIB = 10
WEIGH_MIB = 16
CACHE_MIB = 20


def permute(x, axis, to):
    return lax.ppermute(x, axis, [(i, to(i)) for i in range(lax.axis_size(axis))])


def in_order(mine, theirs, second, axis):
    return jnp.where(
        second,
        jnp.concatenate([theirs, mine], axis),
        jnp.concatenate([mine, theirs], axis),
    )


def join_stats(first, second):
    top = jnp.maximum(first[0:1], second[0:1])
    both = jnp.exp2(first[0:1] - top) * first + jnp.exp2(second[0:1] - top) * second
    row = lax.broadcasted_iota(jnp.int32, both.shape, 0)
    return jnp.where(row == 0, top, jnp.where(row == 3, first + second, both))


def join_kernel(*refs):
    refs[-1][...] = functools.reduce(join_stats, [ref[...] for ref in refs[:-1]])


def join(*parts):
    vmem = pl.BlockSpec(memory_space=pltpu.VMEM)
    return pl.pallas_call(
        join_kernel,
        out_shape=jax.ShapeDtypeStruct(parts[0].shape, F32),
        in_specs=[vmem] * len(parts),
        out_specs=vmem,
        compiler_params=pltpu.CompilerParams(vmem_limit_bytes=MIB),
    )(*parts)


def against(x, y):
    return lax.dot_general(x, y, (((1,), (1,)), ((), ())), preferred_element_type=F32)


def pack_kernel(where_ref, queries_ref, out_grad_ref, mine_ref, theirs_ref, wide, rows):
    q_dev, heads, q_width = queries_ref.shape
    d_nope = out_grad_ref.shape[2]
    d_rope = q_width - d_nope
    pairs = heads // 4
    for j in range(q_dev):
        wide[j, :, :q_width] = queries_ref[j].astype(F32)
        wide[j, :, 2 * d_nope :] = out_grad_ref[j].astype(F32)
        for half in range(2):
            for second in range(2):
                first = (2 * half + second) * pairs
                of = slice(first, first + pairs)
                to = slice(j * pairs, (j + 1) * pairs)
                lane = 2 * d_nope * second
                rows[half, to, lane : lane + d_nope] = wide[j, of, :d_nope]
                rows[half, to, lane + d_nope : lane + 2 * d_nope] = wide[j, of, 2 * d_nope :]
                lane = 4 * d_nope + d_rope * second
                rows[half, to, lane : lane + d_rope] = wide[j, of, d_nope:q_width]
    other = where_ref[0] == 1
    mine_ref[...] = jnp.where(other, rows[1], rows[0]).astype(BF16)
    theirs_ref[...] = jnp.where(other, rows[0], rows[1]).astype(BF16)


def pack(where, queries, out_grad):
    q_dev, heads, d_nope = out_grad.shape
    smem = pl.BlockSpec(memory_space=pltpu.SMEM)
    vmem = pl.BlockSpec(memory_space=pltpu.VMEM)
    size = q_dev * heads // 4
    packed = jax.ShapeDtypeStruct((size, PAIR_LANES), BF16)
    return pl.pallas_call(
        pack_kernel,
        out_shape=(packed, packed),
        in_specs=[smem, vmem, vmem],
        out_specs=[vmem, vmem],
        scratch_shapes=[
            pltpu.VMEM((q_dev, heads, 3 * d_nope), F32),
            pltpu.VMEM((2, size, PAIR_LANES), F32),
        ],
        compiler_params=pltpu.CompilerParams(vmem_limit_bytes=2 * MIB),
        cost_estimate=pl.CostEstimate(flops=0, bytes_accessed=MIB, transcendentals=0),
    )(where, queries, out_grad)


def stage_own_kernel(where_ref, cache_ref, kv_ref, out_ref, key_ref, value_ref):
    half, _, d_nope = key_ref.shape
    out_ref[...] = cache_ref[...].T
    for h in range(half):
        key_ref[h] = kv_ref[where_ref[0] * half + h, :, :d_nope]
        value_ref[h] = kv_ref[where_ref[0] * half + h, :, d_nope:]


def stage_own(where, cache_t, kv_up):
    c_width, keys = cache_t.shape
    heads, d_lat, width = kv_up.shape
    smem = pl.BlockSpec(memory_space=pltpu.SMEM)
    vmem = pl.BlockSpec(memory_space=pltpu.VMEM)
    weight = jax.ShapeDtypeStruct((heads // 2, d_lat, width // 2), BF16)
    return pl.pallas_call(
        stage_own_kernel,
        out_shape=(jax.ShapeDtypeStruct((keys, c_width), BF16), weight, weight),
        in_specs=[smem, vmem, vmem],
        out_specs=[vmem] * 3,
        compiler_params=pltpu.CompilerParams(vmem_limit_bytes=16 * MIB),
        cost_estimate=pl.CostEstimate(
            flops=keys * c_width, bytes_accessed=8 * keys * c_width, transcendentals=0
        ),
    )(where, cache_t, kv_up)


def stage_other_kernel(cache_ref, own_ref, out_ref, both_ref):
    keys = own_ref.shape[1]
    out_ref[...] = cache_ref[...].T
    both_ref[:, :keys] = own_ref[...]
    both_ref[:, keys:] = cache_ref[...]


def stage_other(cache_t, own_t):
    c_width, keys = cache_t.shape
    vmem = pl.BlockSpec(memory_space=pltpu.VMEM)
    return pl.pallas_call(
        stage_other_kernel,
        out_shape=(
            jax.ShapeDtypeStruct((keys, c_width), BF16),
            jax.ShapeDtypeStruct((c_width, 2 * keys), BF16),
        ),
        in_specs=[vmem] * 2,
        out_specs=[vmem] * 2,
        compiler_params=pltpu.CompilerParams(vmem_limit_bytes=10 * MIB),
        cost_estimate=pl.CostEstimate(
            flops=keys * c_width, bytes_accessed=4 * keys * c_width, transcendentals=0
        ),
    )(cache_t, own_t)


def attend_kernel(score_scale, blocks, together, where_ref, *refs):
    ring_refs, refs = refs[:blocks], refs[blocks:]
    key_ref, value_ref, own_ref, other_ref, mine_ref, theirs_ref = refs[:6]
    query_ref, grad_ref, expo_ref, spread_ref, stats_ref, raw, expo, dprod = refs[6:]
    size = ring_refs[0].shape[0]
    half, d_lat = key_ref.shape[:2]
    pairs = half // 2
    rows = size * blocks // pairs
    d_rope = query_ref.shape[1] - d_lat
    keys = own_ref.shape[0]
    width = together * rows
    for k in range(blocks):
        first = pl.multiple_of(where_ref[4 + k] * size, size)
        for part in range(PAIR_LANES // 128):
            lanes = slice(part * 128, (part + 1) * 128)
            raw[part, pl.ds(first, size), :] = ring_refs[k][:, lanes].astype(F32)
    q_dev = mine_ref.shape[0]
    lane = lax.broadcasted_iota(jnp.int32, (1, stats_ref.shape[1]), 1)
    lane = lane - where_ref[5 + blocks] * (2 * q_dev)
    ratio = jnp.zeros(lane.shape, F32)
    for j in range(q_dev):
        ratio = jnp.where(lane == j, mine_ref[j], ratio)
        ratio = jnp.where(lane == q_dev + j, theirs_ref[j], ratio)
    stats_ref[3:4] = ratio

    def of_pair(j, part):
        return raw[part, pl.ds(j, rows, stride=pairs), :]

    def fold(x, join):
        return join(join(x.reshape(CHUNK // 8, 8, width), axis=0), axis=0, keepdims=True)

    def group(p, carry):
        for j in range(together):
            h = p * together + j
            at = pl.ds(pl.multiple_of(h * rows, rows), rows)
            lat = against(of_pair(j, 2 * p).astype(BF16), key_ref[h])
            query_ref[at, :d_lat] = lat.astype(BF16)
            rope = of_pair(j, 4)
            rope = jnp.where(p == 0, rope[:, :d_rope], rope[:, d_rope:])
            query_ref[at, d_lat:] = rope.astype(BF16)
            lat = against(of_pair(j, 2 * p + 1).astype(BF16), value_ref[h])
            grad_ref[at, :] = lat.astype(BF16)
        columns = pl.ds(pl.multiple_of(p * width, width), width)
        tops, masses, dsums = [], [], []
        for c in range(2 * keys // CHUNK):
            first = c * CHUNK % keys
            ref, base = (own_ref, where_ref[1]) if c * CHUNK < keys else (other_ref, where_ref[2])
            score = against(ref[first : first + CHUNK, :], query_ref[columns, :]) * score_scale
            dp = against(ref[first : first + CHUNK, :d_lat], grad_ref[columns, :])
            key = base + first + lax.broadcasted_iota(jnp.int32, (CHUNK, 1), 0)
            score = jnp.where(key < where_ref[3], score, NEVER)
            top = jnp.maximum(fold(score, jnp.max), FLOOR)
            value = jnp.exp2(score - top)
            at = slice(c * CHUNK, (c + 1) * CHUNK)
            expo[at] = value
            dprod[at] = dp
            tops.append(top)
            masses.append(fold(value, jnp.sum))
            dsums.append(fold(value * dp, jnp.sum))
        top = functools.reduce(jnp.maximum, tops)
        factors = [jnp.exp2(t - top) for t in tops]
        mass = sum(f * m for f, m in zip(factors, masses))
        dsum = sum(f * d for f, d in zip(factors, dsums))
        centre = dsum / jnp.maximum(mass, 1e-30)
        for c, f in enumerate(factors):
            at = slice(c * CHUNK, (c + 1) * CHUNK)
            value = expo[at] * f
            expo_ref[at, columns] = value.astype(BF16)
            spread_ref[at, columns] = (value * (dprod[at] - centre)).astype(BF16)
        stats_ref[0:1, columns] = top
        stats_ref[1:2, columns] = mass
        stats_ref[2:3, columns] = dsum
        return carry

    lax.fori_loop(0, half // together, group, 0)


def attend(where, ring, w_key, w_val, own, other, ratios, score_scale):
    blocks, size = len(ring), ring[0].shape[0]
    half, d_lat = w_key.shape[:2]
    together = half // 2
    rows = blocks * size // together
    total = half * rows
    keys, c_width = own.shape
    smem = pl.BlockSpec(memory_space=pltpu.SMEM)
    vmem = pl.BlockSpec(memory_space=pltpu.VMEM)
    return pl.pallas_call(
        functools.partial(attend_kernel, score_scale, blocks, together),
        out_shape=(
            jax.ShapeDtypeStruct((total, c_width), BF16),
            jax.ShapeDtypeStruct((total, d_lat), BF16),
            jax.ShapeDtypeStruct((2 * keys, total), BF16),
            jax.ShapeDtypeStruct((2 * keys, total), BF16),
            jax.ShapeDtypeStruct((4, total), F32),
        ),
        in_specs=[smem] + [vmem] * (blocks + 4) + [smem] * 2,
        out_specs=[vmem] * 5,
        scratch_shapes=[
            pltpu.VMEM((PAIR_LANES // 128, blocks * size, 128), F32),
            pltpu.VMEM((2 * keys, together * rows), F32),
            pltpu.VMEM((2 * keys, together * rows), F32),
        ],
        compiler_params=pltpu.CompilerParams(vmem_limit_bytes=ATTEND_MIB * MIB),
        cost_estimate=pl.CostEstimate(
            flops=2 * 2 * keys * total * (c_width + d_lat),
            bytes_accessed=8 * keys * total,
            transcendentals=2 * keys * total,
        ),
    )(where, *ring, w_key, w_val, own, other, *ratios)


def project_kernel(p, cache_ref, spread_ref, expo_ref, *out_refs):
    width = out_refs[0].shape[1]
    columns = slice(p * width, (p + 1) * width)
    for terms_ref, out_ref in zip((spread_ref, expo_ref), out_refs):
        out_ref[...] = jnp.dot(
            cache_ref[...], terms_ref[:, columns], preferred_element_type=F32
        )


def project(p, parts, cache_t, spread, expo):
    c_width, keys = cache_t.shape
    width = spread.shape[1] // parts
    vmem = pl.BlockSpec(memory_space=pltpu.VMEM)
    return pl.pallas_call(
        functools.partial(project_kernel, p),
        out_shape=(jax.ShapeDtypeStruct((c_width, width), F32),) * 2,
        in_specs=[vmem] * 3,
        out_specs=[vmem] * 2,
        compiler_params=pltpu.CompilerParams(vmem_limit_bytes=PROJECT_MIB * MIB),
        cost_estimate=pl.CostEstimate(
            flops=4 * keys * width * c_width, bytes_accessed=4 * keys * width, transcendentals=0
        ),
    )(cache_t, spread, expo)


def row_gains(where_ref, lens_ref, ratio, rows_of_core):
    place = lax.broadcasted_iota(jnp.int32, ratio.shape, 1)
    turn = place % (2 * rows_of_core) >= rows_of_core
    swapped = jnp.where(turn, place - rows_of_core, place + rows_of_core)
    place = jnp.where(where_ref[0] == 1, swapped, place)
    segments = lens_ref.shape[0]
    members = []
    first = jnp.int32(0)
    for k in range(segments):
        last = first + lens_ref[k]
        members.append((place >= first) & (place < last))
        first = last
    sums = [jnp.sum(jnp.where(m, ratio, 0.0), axis=1, keepdims=True) for m in members]
    gains = jnp.zeros(ratio.shape, F32)
    for p in range(segments // 2):
        margin = BETA * (sums[2 * p] - sums[2 * p + 1])
        weight = LOSS_SCALE * BETA / (1.0 + jnp.exp(margin))
        gains = jnp.where(members[2 * p], -weight, gains)
        gains = jnp.where(members[2 * p + 1], weight, gains)
    return gains


def row_factors(joined_refs, own_ref):
    joined = functools.reduce(join_stats, [ref[...] for ref in joined_refs])
    centre = own_ref[2:3] / jnp.maximum(own_ref[1:2], 1e-30)
    factor = jnp.exp2(own_ref[0:1] - joined[0:1]) / joined[1:2]
    return joined[3:4], factor, joined[2:3] / joined[1:2] - centre


def weigh_kernel(scale, rows, rows_of_core, where_ref, lens_ref, *refs):
    joined_refs, (own_ref, query_ref, grad_ref) = refs[:4], refs[4:7]
    with_spread_ref, with_expo_ref, factors_ref = refs[7:]
    total = query_ref.shape[0]
    d_lat = grad_ref.shape[1]
    ratio, factor, shift = row_factors(joined_refs, own_ref)
    gains_row = row_gains(where_ref, lens_ref, ratio[:, :rows], rows_of_core)
    gains = jnp.broadcast_to(gains_row, (8, rows)).T[:, 0:1]
    gains_row = jnp.concatenate([gains_row] * (total // rows), axis=1)
    factors_ref[0:1] = scale * gains_row * factor
    factors_ref[1:2] = shift
    sublane = lax.broadcasted_iota(jnp.int32, (8, total), 0)
    both = jnp.where(sublane == 0, factor, shift).T
    for h in range(total // rows):
        at = slice(h * rows, (h + 1) * rows)
        factor = both[at, 0:1] * gains
        query = scale * factor * query_ref[at, :].astype(F32)
        with_spread_ref[at, :] = query.astype(BF16)
        moved = both[at, 1:2] * query
        with_expo_ref[at, :d_lat] = (
            factor * grad_ref[at, :].astype(F32) - moved[:, :d_lat]
        ).astype(BF16)
        with_expo_ref[at, d_lat:] = (-moved[:, d_lat:]).astype(BF16)


def weigh(where, lens, joined, stats, query, grad, scale, rows, q_dev):
    total, c_width = query.shape
    smem = pl.BlockSpec(memory_space=pltpu.SMEM)
    vmem = pl.BlockSpec(memory_space=pltpu.VMEM)
    weight = jax.ShapeDtypeStruct((total, c_width), BF16)
    inputs = (*joined, stats, query, grad)
    return pl.pallas_call(
        functools.partial(weigh_kernel, scale, rows, q_dev),
        out_shape=(weight, weight, jax.ShapeDtypeStruct((2, total), F32)),
        in_specs=[smem, smem] + [vmem] * len(inputs),
        out_specs=[vmem] * 3,
        compiler_params=pltpu.CompilerParams(vmem_limit_bytes=WEIGH_MIB * MIB),
        cost_estimate=pl.CostEstimate(
            flops=10 * total * c_width, bytes_accessed=8 * total * c_width, transcendentals=0
        ),
    )(where, lens, *inputs)


def query_kernel(where_ref, factors_ref, key_ref, *refs):
    by_spread_refs, by_expo_refs = refs[:-2:2], refs[1:-2:2]
    keep_ref, send_ref = refs[-2:]
    half, d_lat = key_ref.shape[:2]
    blocks, size = keep_ref.shape[0], keep_ref.shape[2] // 2
    rows = 2 * size * blocks
    second = where_ref[4 + blocks] == 1
    together = half // len(by_spread_refs)
    for p in range(half // 2):
        part = 2 * p // together
        columns = slice(p * 2 * rows, (p + 1) * 2 * rows)
        first = (2 * p % together) * rows
        inside = slice(first, first + 2 * rows)
        full = factors_ref[1:2, columns] * by_expo_refs[part][:, inside]
        full = factors_ref[0:1, columns] * (by_spread_refs[part][:, inside] - full)
        heads = []
        for j in range(2):
            at = slice(j * rows, (j + 1) * rows)
            nope = lax.dot_general(
                full[:d_lat, at].astype(BF16),
                key_ref[2 * p + j],
                (((0,), (0,)), ((), ())),
                preferred_element_type=F32,
            )
            heads.append(jnp.concatenate([nope, full[d_lat:, at].T], axis=1))
        for b in range(blocks):
            pieces = []
            for x in range(2):
                first = (2 * b + x) * size
                pieces.append(jnp.concatenate([y[first : first + size] for y in heads], axis=0))
            keep_ref[b, p] = jnp.where(second, pieces[1], pieces[0]).astype(BF16)
            send_ref[b, p] = jnp.where(second, pieces[0], pieces[1]).astype(BF16)


def query_terms(where, factors, w_key, projected, blocks, q_width):
    half = w_key.shape[0]
    rows = factors.shape[1] // half
    smem = pl.BlockSpec(memory_space=pltpu.SMEM)
    vmem = pl.BlockSpec(memory_space=pltpu.VMEM)
    dq = jax.ShapeDtypeStruct((blocks, half // 2, rows // blocks, q_width), BF16)
    return pl.pallas_call(
        query_kernel,
        out_shape=(dq, dq),
        in_specs=[smem] + [vmem] * (2 + len(projected)),
        out_specs=[vmem] * 2,
        compiler_params=pltpu.CompilerParams(vmem_limit_bytes=WEIGH_MIB * MIB),
        cost_estimate=pl.CostEstimate(
            flops=4 * w_key.size * rows, bytes_accessed=8 * w_key.size, transcendentals=0
        ),
    )(where, factors, w_key, *projected)


def cache_kernel(
    part, turn, d_lat, where_ref, spread_ref, expo_ref, with_spread_ref, with_expo_ref, *refs
):
    adds, outs = refs[:-2], refs[-2:]
    keys = spread_ref.shape[3]

    ny = spread_ref.shape[2]
    y, here = where_ref[where_ref.shape[0] - 2], where_ref[where_ref.shape[0] - 1]
    there = 1 - here
    if turn == 0:
        places = [(there, 2), (there, 1), (here, 2), (here, 1)]
    else:
        places = [(there, 3), (here, 3), (there, 0), (here, 0)]

    def gather(ref):
        blocks = [ref[part, x, (y + k) & (ny - 1)] for x, k in places]
        return jnp.concatenate(blocks, axis=0)

    out = jnp.dot(gather(spread_ref), with_spread_ref[...], preferred_element_type=F32)
    out = out + jnp.dot(gather(expo_ref), with_expo_ref[...], preferred_element_type=F32)
    rope = out.shape[1] - d_lat
    for i in range(4):
        first = (i % 2) * d_lat
        lat = slice(first, first + d_lat)
        first = 2 * d_lat + (i % 2) * rope
        tail = slice(first, first + rope)
        at = slice(i * keys, (i + 1) * keys)
        for lanes, value in ((lat, out[at, :d_lat]), (tail, out[at, d_lat:])):
            if adds:
                value = value + adds[i // 2][:, lanes].astype(F32)
            outs[i // 2][:, lanes] = value.astype(outs[i // 2].dtype)


def cache_terms(part, turn, where, d_lat, spread, expo, with_spread, with_expo, dtypes, adds=()):
    total, c_width = with_spread.shape
    keys = spread.shape[3]
    smem = pl.BlockSpec(memory_space=pltpu.SMEM)
    vmem = pl.BlockSpec(memory_space=pltpu.VMEM)
    return pl.pallas_call(
        functools.partial(cache_kernel, part, turn, d_lat),
        out_shape=[jax.ShapeDtypeStruct((keys, 2 * c_width), dtype) for dtype in dtypes],
        in_specs=[smem] + [vmem] * (4 + len(adds)),
        out_specs=[vmem, vmem],
        compiler_params=pltpu.CompilerParams(vmem_limit_bytes=CACHE_MIB * MIB),
        cost_estimate=pl.CostEstimate(
            flops=16 * keys * total * c_width,
            bytes_accessed=16 * keys * total,
            transcendentals=0,
        ),
    )(where, spread, expo, with_spread, with_expo, *adds)


def unfold(x, d_lat):
    rope = x.shape[1] // 2 - d_lat
    return [
        jnp.concatenate(
            [
                x[:, i * d_lat : (i + 1) * d_lat],
                x[:, 2 * d_lat + i * rope : 2 * d_lat + (i + 1) * rope],
            ],
            axis=1,
        )
        for i in range(2)
    ]


def fold_rows(x, d_lat, out_ref):
    size = x.shape[0] // 2
    rope = x.shape[1] - d_lat
    for i in range(2):
        part = x[i * size : (i + 1) * size].astype(BF16)
        out_ref[:, i * d_lat : (i + 1) * d_lat] = part[:, :d_lat]
        out_ref[:, 2 * d_lat + i * rope : 2 * d_lat + (i + 1) * rope] = part[:, d_lat:]


def forward_kernel(d_lat, keep_ref, arrived_ref, *out_refs):
    total = keep_ref[...].astype(F32) + arrived_ref[...].astype(F32)
    for block, out_ref in zip(unfold(total, d_lat), out_refs):
        fold_rows(block, d_lat, out_ref)


def turn_kernel(d_lat, own_ref, arrived_ref, send_ref, keep_ref):
    send, keep = unfold(own_ref[...] + arrived_ref[...].astype(F32), d_lat)
    fold_rows(send, d_lat, send_ref)
    keep_ref[...] = keep


def finish_kernel(d_lat, keep_ref, *refs):
    total = keep_ref[...]
    for arrived_ref in refs[:-1]:
        total = total + jnp.concatenate(unfold(arrived_ref[...].astype(F32), d_lat), axis=0)
    refs[-1][...] = total.T.astype(BF16)


def small(kernel, out_shape, *operands):
    vmem = pl.BlockSpec(memory_space=pltpu.VMEM)
    return pl.pallas_call(
        kernel,
        out_shape=out_shape,
        in_specs=[vmem] * len(operands),
        out_specs=jax.tree.map(lambda _: vmem, out_shape),
        compiler_params=pltpu.CompilerParams(vmem_limit_bytes=6 * MIB),
    )(*operands)


def per_device(queries, out_grad, kv_up, latent_cache, token_ratio, pair_lens, prompt_len):
    ctx_index = lax.axis_index("ctx")
    head_index = lax.axis_index("head")
    core = ctx_index & 1
    x_lo = (ctx_index >> 1) & 1
    z = ctx_index >> 2
    nz = lax.axis_size("ctx") // 4
    ny = lax.axis_size("head") // 2
    y = head_index & (ny - 1)
    x_hi = (head_index >= ny).astype(jnp.int32)
    other_core = lambda i: i ^ 1
    other_x_lo = lambda i: i ^ 2
    z_groups = [[4 * k + j for k in range(nz)] for j in range(4)]

    q_dev, heads, q_width = queries.shape
    p_dev, c_width = latent_cache.shape
    d_lat = kv_up.shape[1]
    d_rope = c_width - d_lat
    d_nope = q_width - d_rope
    half = heads // 2
    scale = q_width ** (-0.5)
    rows = 4 * nz * q_dev

    where = [core, ctx_index * p_dev, (ctx_index ^ 1) * p_dev, prompt_len[0]]
    where = where + [(z + k) & (nz - 1) for k in range(nz)]
    where = where + [x_lo, ctx_index >> 1, y, x_hi]
    where = jnp.stack(where).astype(jnp.int32)
    own_t = latent_cache.T
    other_t = permute(latent_cache, "ctx", other_core).T
    other_ratio = permute(token_ratio, "ctx", other_core)
    mine, theirs = pack(where, queries, out_grad)
    block = jnp.concatenate([mine, permute(theirs, "ctx", other_core)], 0)
    own_keys, w_key, w_val = stage_own(where, own_t, kv_up)
    from_x_lo = permute(block, "ctx", other_x_lo)
    from_x_lo, own_keys, w_key, w_val, other_ratio = lax.optimization_barrier(
        (from_x_lo, own_keys, w_key, w_val, other_ratio)
    )
    block = in_order(block, from_x_lo, x_lo == 1, 0)
    other_keys, cache_t = stage_other(other_t, own_t)
    along_z = lambda x, k: permute(x, "ctx", lambda i: (i + 4 * k) % (4 * nz))
    ring = [block] + [None] * (nz - 1)
    ring[nz - 2], ring[2] = along_z(block, 2), along_z(block, -2)
    ring[nz - 1], ring[1] = along_z(block, 1), along_z(block, -1)
    ring[nz - 4] = along_z(ring[nz - 2], 2)
    ring[nz - 3], ring[3] = along_z(ring[nz - 2], 1), along_z(ring[2], -1)

    query, grad, expo, spread, stats = attend(
        where, ring, w_key, w_val, own_keys, other_keys, (token_ratio, other_ratio), scale * LOG2E
    )

    joined = [stats]
    projected = []
    parts = 2
    for group, partners in enumerate(((2, 4, 6), (8, 16, 24))):
        mine = joined[0] if group == 0 else join(*joined)
        joined = [permute(mine, "ctx", lambda i, k=k: i ^ k) for k in partners]
        terms = project(group, parts, cache_t, spread, expo)
        joined = lax.optimization_barrier((*joined, *terms))
        projected += joined[len(partners) :]
        joined = (mine, *joined[: len(partners)])
    with_spread, with_expo, factors = weigh(
        where, pair_lens, joined, stats, query, grad, scale, rows, q_dev
    )
    dq_keep, dq_send = query_terms(where, factors, w_key, projected, nz, q_width)
    dq_pair = permute(dq_send, "ctx", other_x_lo)
    keys = p_dev // (2 * ny)
    shape = (2, 2, ny, keys, spread.shape[1])
    operands = (d_lat, spread.reshape(shape), expo.reshape(shape), with_spread, with_expo)
    adds = []
    sends = cache_terms(1, 0, where, *operands, (BF16, BF16))
    later, *sends = lax.optimization_barrier((where, *sends))
    adds.append([permute(x, "ctx", other_core) for x in sends])
    sends = cache_terms(1, 1, later, *operands, (BF16, BF16))
    adds.append([permute(x, "ctx", other_core) for x in sends])
    to_x_hi = lambda x: permute(x, "head", lambda i: (i + ny) % (2 * ny))
    to_y = lambda x, k: permute(x, "head", lambda i: (i // ny) * ny + (i + k) % ny)
    send, keep = cache_terms(0, 0, where, *operands, (BF16, F32), adds[0])
    later, send = lax.optimization_barrier((where, send))
    from_x_hi = to_x_hi(send)
    send, own = cache_terms(0, 1, later, *operands, (BF16, F32), adds[1])
    dq = (dq_keep.astype(F32) + dq_pair.astype(F32)).astype(BF16)
    send, dq = lax.optimization_barrier((send, dq))
    from_y = to_y(send, 3)

    half_rows = jax.ShapeDtypeStruct((keys // 2, 2 * c_width), BF16)
    block = jax.ShapeDtypeStruct((keys, c_width), F32)
    sends = small(
        functools.partial(forward_kernel, d_lat), (half_rows, half_rows), keep, from_x_hi
    )
    arrived = [to_y(sends[0], 2), to_y(sends[1], 1)]
    send, keep = small(functools.partial(turn_kernel, d_lat), (half_rows, block), own, from_y)
    arrived.append(to_x_hi(send))
    cache_grad = small(
        functools.partial(finish_kernel, d_lat),
        jax.ShapeDtypeStruct((c_width, keys), BF16),
        keep,
        *arrived,
    ).T

    dq = lax.all_to_all(dq, "ctx", 0, 0, axis_index_groups=z_groups)
    dq = jnp.sum(dq.astype(F32), axis=0).astype(BF16).reshape(half, 2, q_dev, q_width)
    theirs = permute(dq[:, 1], "ctx", other_core)
    query_grad = jnp.transpose(in_order(dq[:, 0], theirs, core == 1, 0), (1, 0, 2))

    return (query_grad, cache_grad)


def solution(mesh):
    placed = (
        P("ctx", "head", None),
        P("ctx", "head", None),
        P("head", None, None),
        P("ctx", None),
        P("ctx"),
        P(),
        P(),
    )
    return jax.shard_map(
        per_device,
        mesh=mesh,
        in_specs=placed,
        out_specs=(P("ctx", "head", None), P(("ctx", "head"), None)),
        check_vma=False,
    )
```

```python
import functools

import jax
import jax.numpy as jnp
from jax import lax
from jax.experimental import pallas as pl
from jax.experimental.pallas import tpu as pltpu
from jax.sharding import PartitionSpec as P

BETA = 0.1
LOSS_SCALE = 2048.0
LOG2E = 1.4426950408889634
NEVER = -1e30
FLOOR = -1e29
F32 = jnp.float32
BF16 = jnp.bfloat16
CHUNK = 1024
PAIR_LANES = 640
MIB = 1024 * 1024
ATTEND_MIB = 24
PROJECT_MIB = 10
WEIGH_MIB = 16
CACHE_MIB = 20


def permute(x, axis, to):
    return lax.ppermute(x, axis, [(i, to(i)) for i in range(lax.axis_size(axis))])


def in_order(mine, theirs, second, axis):
    return jnp.where(
        second,
        jnp.concatenate([theirs, mine], axis),
        jnp.concatenate([mine, theirs], axis),
    )


def join_stats(first, second):
    top = jnp.maximum(first[0:1], second[0:1])
    both = jnp.exp2(first[0:1] - top) * first + jnp.exp2(second[0:1] - top) * second
    row = lax.broadcasted_iota(jnp.int32, both.shape, 0)
    return jnp.where(row == 0, top, jnp.where(row == 3, first + second, both))


def join_kernel(*refs):
    refs[-1][...] = functools.reduce(join_stats, [ref[...] for ref in refs[:-1]])


def join(*parts):
    vmem = pl.BlockSpec(memory_space=pltpu.VMEM)
    return pl.pallas_call(
        join_kernel,
        out_shape=jax.ShapeDtypeStruct(parts[0].shape, F32),
        in_specs=[vmem] * len(parts),
        out_specs=vmem,
        compiler_params=pltpu.CompilerParams(vmem_limit_bytes=MIB),
    )(*parts)


def against(x, y):
    return lax.dot_general(x, y, (((1,), (1,)), ((), ())), preferred_element_type=F32)


def pack_kernel(where_ref, queries_ref, out_grad_ref, mine_ref, theirs_ref, wide, rows):
    q_dev, heads, q_width = queries_ref.shape
    d_nope = out_grad_ref.shape[2]
    d_rope = q_width - d_nope
    pairs = heads // 4
    for j in range(q_dev):
        wide[j, :, :q_width] = queries_ref[j].astype(F32)
        wide[j, :, 2 * d_nope :] = out_grad_ref[j].astype(F32)
        for half in range(2):
            for second in range(2):
                first = (2 * half + second) * pairs
                of = slice(first, first + pairs)
                to = slice(j * pairs, (j + 1) * pairs)
                lane = 2 * d_nope * second
                rows[half, to, lane : lane + d_nope] = wide[j, of, :d_nope]
                rows[half, to, lane + d_nope : lane + 2 * d_nope] = wide[j, of, 2 * d_nope :]
                lane = 4 * d_nope + d_rope * second
                rows[half, to, lane : lane + d_rope] = wide[j, of, d_nope:q_width]
    other = where_ref[0] == 1
    mine_ref[...] = jnp.where(other, rows[1], rows[0]).astype(BF16)
    theirs_ref[...] = jnp.where(other, rows[0], rows[1]).astype(BF16)


def pack(where, queries, out_grad):
    q_dev, heads, d_nope = out_grad.shape
    smem = pl.BlockSpec(memory_space=pltpu.SMEM)
    vmem = pl.BlockSpec(memory_space=pltpu.VMEM)
    size = q_dev * heads // 4
    packed = jax.ShapeDtypeStruct((size, PAIR_LANES), BF16)
    return pl.pallas_call(
        pack_kernel,
        out_shape=(packed, packed),
        in_specs=[smem, vmem, vmem],
        out_specs=[vmem, vmem],
        scratch_shapes=[
            pltpu.VMEM((q_dev, heads, 3 * d_nope), F32),
            pltpu.VMEM((2, size, PAIR_LANES), F32),
        ],
        compiler_params=pltpu.CompilerParams(vmem_limit_bytes=2 * MIB),
        cost_estimate=pl.CostEstimate(flops=0, bytes_accessed=MIB, transcendentals=0),
    )(where, queries, out_grad)


def stage_own_kernel(cache_ref, out_ref):
    out_ref[...] = cache_ref[...].T


def stage_own(cache_t):
    c_width, keys = cache_t.shape
    vmem = pl.BlockSpec(memory_space=pltpu.VMEM)
    return pl.pallas_call(
        stage_own_kernel,
        out_shape=jax.ShapeDtypeStruct((keys, c_width), BF16),
        in_specs=[vmem],
        out_specs=vmem,
        compiler_params=pltpu.CompilerParams(vmem_limit_bytes=6 * MIB),
        cost_estimate=pl.CostEstimate(
            flops=keys * c_width, bytes_accessed=4 * keys * c_width, transcendentals=0
        ),
    )(cache_t)


def stage_other_kernel(
    where_ref, cache_ref, own_ref, kv_ref, out_ref, both_ref, key_ref, value_ref
):
    keys = own_ref.shape[1]
    half, _, d_nope = key_ref.shape
    out_ref[...] = cache_ref[...].T
    both_ref[:, :keys] = own_ref[...]
    both_ref[:, keys:] = cache_ref[...]
    for h in range(half):
        key_ref[h] = kv_ref[where_ref[0] * half + h, :, :d_nope]
        value_ref[h] = kv_ref[where_ref[0] * half + h, :, d_nope:]


def stage_other(where, cache_t, own_t, kv_up):
    c_width, keys = cache_t.shape
    heads, d_lat, width = kv_up.shape
    smem = pl.BlockSpec(memory_space=pltpu.SMEM)
    vmem = pl.BlockSpec(memory_space=pltpu.VMEM)
    weight = jax.ShapeDtypeStruct((heads // 2, d_lat, width // 2), BF16)
    return pl.pallas_call(
        stage_other_kernel,
        out_shape=(
            jax.ShapeDtypeStruct((keys, c_width), BF16),
            jax.ShapeDtypeStruct((c_width, 2 * keys), BF16),
            weight,
            weight,
        ),
        in_specs=[smem] + [vmem] * 3,
        out_specs=[vmem] * 4,
        compiler_params=pltpu.CompilerParams(vmem_limit_bytes=18 * MIB),
        cost_estimate=pl.CostEstimate(
            flops=keys * c_width, bytes_accessed=8 * keys * c_width, transcendentals=0
        ),
    )(where, cache_t, own_t, kv_up)


def attend_kernel(score_scale, blocks, together, where_ref, *refs):
    ring_refs, refs = refs[:blocks], refs[blocks:]
    key_ref, value_ref, own_ref, other_ref, mine_ref, theirs_ref = refs[:6]
    query_ref, grad_ref, expo_ref, spread_ref, stats_ref, raw, expo, dprod = refs[6:]
    size = ring_refs[0].shape[0]
    half, d_lat = key_ref.shape[:2]
    pairs = half // 2
    rows = size * blocks // pairs
    d_rope = query_ref.shape[1] - d_lat
    keys = own_ref.shape[0]
    width = together * rows
    for k in range(blocks):
        first = pl.multiple_of(where_ref[4 + k] * size, size)
        for part in range(PAIR_LANES // 128):
            lanes = slice(part * 128, (part + 1) * 128)
            raw[part, pl.ds(first, size), :] = ring_refs[k][:, lanes].astype(F32)
    q_dev = mine_ref.shape[0]
    lane = lax.broadcasted_iota(jnp.int32, (1, stats_ref.shape[1]), 1)
    lane = lane - where_ref[5 + blocks] * (2 * q_dev)
    ratio = jnp.zeros(lane.shape, F32)
    for j in range(q_dev):
        ratio = jnp.where(lane == j, mine_ref[j], ratio)
        ratio = jnp.where(lane == q_dev + j, theirs_ref[j], ratio)
    stats_ref[3:4] = ratio

    def of_pair(j, part):
        return raw[part, pl.ds(j, rows, stride=pairs), :]

    def fold(x, join):
        return join(join(x.reshape(CHUNK // 8, 8, width), axis=0), axis=0, keepdims=True)

    def group(p, carry):
        for j in range(together):
            h = p * together + j
            at = pl.ds(pl.multiple_of(h * rows, rows), rows)
            lat = against(of_pair(j, 2 * p).astype(BF16), key_ref[h])
            query_ref[at, :d_lat] = lat.astype(BF16)
            rope = of_pair(j, 4)
            rope = jnp.where(p == 0, rope[:, :d_rope], rope[:, d_rope:])
            query_ref[at, d_lat:] = rope.astype(BF16)
            lat = against(of_pair(j, 2 * p + 1).astype(BF16), value_ref[h])
            grad_ref[at, :] = lat.astype(BF16)
        columns = pl.ds(pl.multiple_of(p * width, width), width)
        tops, masses, dsums = [], [], []
        for c in range(2 * keys // CHUNK):
            first = c * CHUNK % keys
            ref, base = (own_ref, where_ref[1]) if c * CHUNK < keys else (other_ref, where_ref[2])
            score = against(ref[first : first + CHUNK, :], query_ref[columns, :]) * score_scale
            dp = against(ref[first : first + CHUNK, :d_lat], grad_ref[columns, :])
            key = base + first + lax.broadcasted_iota(jnp.int32, (CHUNK, 1), 0)
            score = jnp.where(key < where_ref[3], score, NEVER)
            top = jnp.maximum(fold(score, jnp.max), FLOOR)
            value = jnp.exp2(score - top)
            at = slice(c * CHUNK, (c + 1) * CHUNK)
            expo[at] = value
            dprod[at] = dp
            tops.append(top)
            masses.append(fold(value, jnp.sum))
            dsums.append(fold(value * dp, jnp.sum))
        top = functools.reduce(jnp.maximum, tops)
        factors = [jnp.exp2(t - top) for t in tops]
        mass = sum(f * m for f, m in zip(factors, masses))
        dsum = sum(f * d for f, d in zip(factors, dsums))
        centre = dsum / jnp.maximum(mass, 1e-30)
        for c, f in enumerate(factors):
            at = slice(c * CHUNK, (c + 1) * CHUNK)
            value = expo[at] * f
            expo_ref[at, columns] = value.astype(BF16)
            spread_ref[at, columns] = (value * (dprod[at] - centre)).astype(BF16)
        stats_ref[0:1, columns] = top
        stats_ref[1:2, columns] = mass
        stats_ref[2:3, columns] = dsum
        return carry

    lax.fori_loop(0, half // together, group, 0)


def attend(where, ring, w_key, w_val, own, other, ratios, score_scale):
    blocks, size = len(ring), ring[0].shape[0]
    half, d_lat = w_key.shape[:2]
    together = half // 2
    rows = blocks * size // together
    total = half * rows
    keys, c_width = own.shape
    smem = pl.BlockSpec(memory_space=pltpu.SMEM)
    vmem = pl.BlockSpec(memory_space=pltpu.VMEM)
    return pl.pallas_call(
        functools.partial(attend_kernel, score_scale, blocks, together),
        out_shape=(
            jax.ShapeDtypeStruct((total, c_width), BF16),
            jax.ShapeDtypeStruct((total, d_lat), BF16),
            jax.ShapeDtypeStruct((2 * keys, total), BF16),
            jax.ShapeDtypeStruct((2 * keys, total), BF16),
            jax.ShapeDtypeStruct((4, total), F32),
        ),
        in_specs=[smem] + [vmem] * (blocks + 4) + [smem] * 2,
        out_specs=[vmem] * 5,
        scratch_shapes=[
            pltpu.VMEM((PAIR_LANES // 128, blocks * size, 128), F32),
            pltpu.VMEM((2 * keys, together * rows), F32),
            pltpu.VMEM((2 * keys, together * rows), F32),
        ],
        compiler_params=pltpu.CompilerParams(vmem_limit_bytes=ATTEND_MIB * MIB),
        cost_estimate=pl.CostEstimate(
            flops=2 * 2 * keys * total * (c_width + d_lat),
            bytes_accessed=8 * keys * total,
            transcendentals=2 * keys * total,
        ),
    )(where, *ring, w_key, w_val, own, other, *ratios)


def project_kernel(p, cache_ref, spread_ref, expo_ref, *out_refs):
    width = out_refs[0].shape[1]
    columns = slice(p * width, (p + 1) * width)
    for terms_ref, out_ref in zip((spread_ref, expo_ref), out_refs):
        out_ref[...] = jnp.dot(
            cache_ref[...], terms_ref[:, columns], preferred_element_type=F32
        )


def project(p, parts, cache_t, spread, expo):
    c_width, keys = cache_t.shape
    width = spread.shape[1] // parts
    vmem = pl.BlockSpec(memory_space=pltpu.VMEM)
    return pl.pallas_call(
        functools.partial(project_kernel, p),
        out_shape=(jax.ShapeDtypeStruct((c_width, width), F32),) * 2,
        in_specs=[vmem] * 3,
        out_specs=[vmem] * 2,
        compiler_params=pltpu.CompilerParams(vmem_limit_bytes=PROJECT_MIB * MIB),
        cost_estimate=pl.CostEstimate(
            flops=4 * keys * width * c_width, bytes_accessed=4 * keys * width, transcendentals=0
        ),
    )(cache_t, spread, expo)


def row_gains(where_ref, lens_ref, ratio, rows_of_core):
    place = lax.broadcasted_iota(jnp.int32, ratio.shape, 1)
    turn = place % (2 * rows_of_core) >= rows_of_core
    swapped = jnp.where(turn, place - rows_of_core, place + rows_of_core)
    place = jnp.where(where_ref[0] == 1, swapped, place)
    segments = lens_ref.shape[0]
    members = []
    first = jnp.int32(0)
    for k in range(segments):
        last = first + lens_ref[k]
        members.append((place >= first) & (place < last))
        first = last
    sums = [jnp.sum(jnp.where(m, ratio, 0.0), axis=1, keepdims=True) for m in members]
    gains = jnp.zeros(ratio.shape, F32)
    for p in range(segments // 2):
        margin = BETA * (sums[2 * p] - sums[2 * p + 1])
        weight = LOSS_SCALE * BETA / (1.0 + jnp.exp(margin))
        gains = jnp.where(members[2 * p], -weight, gains)
        gains = jnp.where(members[2 * p + 1], weight, gains)
    return gains


def row_factors(joined_refs, own_ref):
    joined = functools.reduce(join_stats, [ref[...] for ref in joined_refs])
    centre = own_ref[2:3] / jnp.maximum(own_ref[1:2], 1e-30)
    factor = jnp.exp2(own_ref[0:1] - joined[0:1]) / joined[1:2]
    return joined[3:4], factor, joined[2:3] / joined[1:2] - centre


def weigh_kernel(scale, rows, rows_of_core, where_ref, lens_ref, *refs):
    joined_refs, (own_ref, query_ref, grad_ref) = refs[:4], refs[4:7]
    with_spread_ref, with_expo_ref, factors_ref = refs[7:]
    total = query_ref.shape[0]
    d_lat = grad_ref.shape[1]
    ratio, factor, shift = row_factors(joined_refs, own_ref)
    gains_row = row_gains(where_ref, lens_ref, ratio[:, :rows], rows_of_core)
    gains = jnp.broadcast_to(gains_row, (8, rows)).T[:, 0:1]
    gains_row = jnp.concatenate([gains_row] * (total // rows), axis=1)
    factors_ref[0:1] = scale * gains_row * factor
    factors_ref[1:2] = shift
    sublane = lax.broadcasted_iota(jnp.int32, (8, total), 0)
    both = jnp.where(sublane == 0, factor, shift).T
    for h in range(total // rows):
        at = slice(h * rows, (h + 1) * rows)
        factor = both[at, 0:1] * gains
        query = scale * factor * query_ref[at, :].astype(F32)
        with_spread_ref[at, :] = query.astype(BF16)
        moved = both[at, 1:2] * query
        with_expo_ref[at, :d_lat] = (
            factor * grad_ref[at, :].astype(F32) - moved[:, :d_lat]
        ).astype(BF16)
        with_expo_ref[at, d_lat:] = (-moved[:, d_lat:]).astype(BF16)


def weigh(where, lens, joined, stats, query, grad, scale, rows, q_dev):
    total, c_width = query.shape
    smem = pl.BlockSpec(memory_space=pltpu.SMEM)
    vmem = pl.BlockSpec(memory_space=pltpu.VMEM)
    weight = jax.ShapeDtypeStruct((total, c_width), BF16)
    inputs = (*joined, stats, query, grad)
    return pl.pallas_call(
        functools.partial(weigh_kernel, scale, rows, q_dev),
        out_shape=(weight, weight, jax.ShapeDtypeStruct((2, total), F32)),
        in_specs=[smem, smem] + [vmem] * len(inputs),
        out_specs=[vmem] * 3,
        compiler_params=pltpu.CompilerParams(vmem_limit_bytes=WEIGH_MIB * MIB),
        cost_estimate=pl.CostEstimate(
            flops=10 * total * c_width, bytes_accessed=8 * total * c_width, transcendentals=0
        ),
    )(where, lens, *inputs)


def query_kernel(where_ref, factors_ref, key_ref, *refs):
    by_spread_refs, by_expo_refs = refs[:-2:2], refs[1:-2:2]
    keep_ref, send_ref = refs[-2:]
    half, d_lat = key_ref.shape[:2]
    blocks, size = keep_ref.shape[0], keep_ref.shape[2] // 2
    rows = 2 * size * blocks
    second = where_ref[4 + blocks] == 1
    together = half // len(by_spread_refs)
    for p in range(half // 2):
        part = 2 * p // together
        columns = slice(p * 2 * rows, (p + 1) * 2 * rows)
        first = (2 * p % together) * rows
        inside = slice(first, first + 2 * rows)
        full = factors_ref[1:2, columns] * by_expo_refs[part][:, inside]
        full = factors_ref[0:1, columns] * (by_spread_refs[part][:, inside] - full)
        heads = []
        for j in range(2):
            at = slice(j * rows, (j + 1) * rows)
            nope = lax.dot_general(
                full[:d_lat, at].astype(BF16),
                key_ref[2 * p + j],
                (((0,), (0,)), ((), ())),
                preferred_element_type=F32,
            )
            heads.append(jnp.concatenate([nope, full[d_lat:, at].T], axis=1))
        for b in range(blocks):
            pieces = []
            for x in range(2):
                first = (2 * b + x) * size
                pieces.append(jnp.concatenate([y[first : first + size] for y in heads], axis=0))
            keep_ref[b, p] = jnp.where(second, pieces[1], pieces[0]).astype(BF16)
            send_ref[b, p] = jnp.where(second, pieces[0], pieces[1]).astype(BF16)


def query_terms(where, factors, w_key, projected, blocks, q_width):
    half = w_key.shape[0]
    rows = factors.shape[1] // half
    smem = pl.BlockSpec(memory_space=pltpu.SMEM)
    vmem = pl.BlockSpec(memory_space=pltpu.VMEM)
    dq = jax.ShapeDtypeStruct((blocks, half // 2, rows // blocks, q_width), BF16)
    return pl.pallas_call(
        query_kernel,
        out_shape=(dq, dq),
        in_specs=[smem] + [vmem] * (2 + len(projected)),
        out_specs=[vmem] * 2,
        compiler_params=pltpu.CompilerParams(vmem_limit_bytes=WEIGH_MIB * MIB),
        cost_estimate=pl.CostEstimate(
            flops=4 * w_key.size * rows, bytes_accessed=8 * w_key.size, transcendentals=0
        ),
    )(where, factors, w_key, *projected)


def cache_kernel(
    part, turn, d_lat, where_ref, spread_ref, expo_ref, with_spread_ref, with_expo_ref, *refs
):
    adds, outs = refs[:-2], refs[-2:]
    keys = spread_ref.shape[3]

    ny = spread_ref.shape[2]
    y, here = where_ref[where_ref.shape[0] - 2], where_ref[where_ref.shape[0] - 1]
    there = 1 - here
    if turn == 0:
        places = [(there, 2), (there, 1), (here, 2), (here, 1)]
    else:
        places = [(there, 3), (here, 3), (there, 0), (here, 0)]

    def gather(ref):
        blocks = [ref[part, x, (y + k) & (ny - 1)] for x, k in places]
        return jnp.concatenate(blocks, axis=0)

    out = jnp.dot(gather(spread_ref), with_spread_ref[...], preferred_element_type=F32)
    out = out + jnp.dot(gather(expo_ref), with_expo_ref[...], preferred_element_type=F32)
    rope = out.shape[1] - d_lat
    for i in range(4):
        first = (i % 2) * d_lat
        lat = slice(first, first + d_lat)
        first = 2 * d_lat + (i % 2) * rope
        tail = slice(first, first + rope)
        at = slice(i * keys, (i + 1) * keys)
        for lanes, value in ((lat, out[at, :d_lat]), (tail, out[at, d_lat:])):
            if adds:
                value = value + adds[i // 2][:, lanes].astype(F32)
            outs[i // 2][:, lanes] = value.astype(outs[i // 2].dtype)


def cache_terms(part, turn, where, d_lat, spread, expo, with_spread, with_expo, dtypes, adds=()):
    total, c_width = with_spread.shape
    keys = spread.shape[3]
    smem = pl.BlockSpec(memory_space=pltpu.SMEM)
    vmem = pl.BlockSpec(memory_space=pltpu.VMEM)
    return pl.pallas_call(
        functools.partial(cache_kernel, part, turn, d_lat),
        out_shape=[jax.ShapeDtypeStruct((keys, 2 * c_width), dtype) for dtype in dtypes],
        in_specs=[smem] + [vmem] * (4 + len(adds)),
        out_specs=[vmem, vmem],
        compiler_params=pltpu.CompilerParams(vmem_limit_bytes=CACHE_MIB * MIB),
        cost_estimate=pl.CostEstimate(
            flops=16 * keys * total * c_width,
            bytes_accessed=16 * keys * total,
            transcendentals=0,
        ),
    )(where, spread, expo, with_spread, with_expo, *adds)


def unfold(x, d_lat):
    rope = x.shape[1] // 2 - d_lat
    return [
        jnp.concatenate(
            [
                x[:, i * d_lat : (i + 1) * d_lat],
                x[:, 2 * d_lat + i * rope : 2 * d_lat + (i + 1) * rope],
            ],
            axis=1,
        )
        for i in range(2)
    ]


def fold_rows(x, d_lat, out_ref):
    size = x.shape[0] // 2
    rope = x.shape[1] - d_lat
    for i in range(2):
        part = x[i * size : (i + 1) * size].astype(BF16)
        out_ref[:, i * d_lat : (i + 1) * d_lat] = part[:, :d_lat]
        out_ref[:, 2 * d_lat + i * rope : 2 * d_lat + (i + 1) * rope] = part[:, d_lat:]


def forward_kernel(d_lat, keep_ref, arrived_ref, *out_refs):
    total = keep_ref[...].astype(F32) + arrived_ref[...].astype(F32)
    for block, out_ref in zip(unfold(total, d_lat), out_refs):
        fold_rows(block, d_lat, out_ref)


def turn_kernel(d_lat, own_ref, arrived_ref, send_ref, keep_ref):
    send, keep = unfold(own_ref[...] + arrived_ref[...].astype(F32), d_lat)
    fold_rows(send, d_lat, send_ref)
    keep_ref[...] = keep


def finish_kernel(d_lat, keep_ref, *refs):
    total = keep_ref[...]
    for arrived_ref in refs[:-1]:
        total = total + jnp.concatenate(unfold(arrived_ref[...].astype(F32), d_lat), axis=0)
    refs[-1][...] = total.T.astype(BF16)


def small(kernel, out_shape, *operands):
    vmem = pl.BlockSpec(memory_space=pltpu.VMEM)
    return pl.pallas_call(
        kernel,
        out_shape=out_shape,
        in_specs=[vmem] * len(operands),
        out_specs=jax.tree.map(lambda _: vmem, out_shape),
        compiler_params=pltpu.CompilerParams(vmem_limit_bytes=6 * MIB),
    )(*operands)


def per_device(queries, out_grad, kv_up, latent_cache, token_ratio, pair_lens, prompt_len):
    ctx_index = lax.axis_index("ctx")
    head_index = lax.axis_index("head")
    core = ctx_index & 1
    x_lo = (ctx_index >> 1) & 1
    z = ctx_index >> 2
    nz = lax.axis_size("ctx") // 4
    ny = lax.axis_size("head") // 2
    y = head_index & (ny - 1)
    x_hi = (head_index >= ny).astype(jnp.int32)
    other_core = lambda i: i ^ 1
    other_x_lo = lambda i: i ^ 2
    z_groups = [[4 * k + j for k in range(nz)] for j in range(4)]

    q_dev, heads, q_width = queries.shape
    p_dev, c_width = latent_cache.shape
    d_lat = kv_up.shape[1]
    d_rope = c_width - d_lat
    d_nope = q_width - d_rope
    half = heads // 2
    scale = q_width ** (-0.5)
    rows = 4 * nz * q_dev

    where = [core, ctx_index * p_dev, (ctx_index ^ 1) * p_dev, prompt_len[0]]
    where = where + [(z + k) & (nz - 1) for k in range(nz)]
    where = where + [x_lo, ctx_index >> 1, y, x_hi]
    where = jnp.stack(where).astype(jnp.int32)
    own_t = latent_cache.T
    other_t = permute(latent_cache, "ctx", other_core).T
    other_ratio = permute(token_ratio, "ctx", other_core)
    mine, theirs = pack(where, queries, out_grad)
    block = jnp.concatenate([mine, permute(theirs, "ctx", other_core)], 0)
    own_keys = stage_own(own_t)
    from_x_lo = permute(block, "ctx", other_x_lo)
    from_x_lo, own_keys, other_ratio = lax.optimization_barrier(
        (from_x_lo, own_keys, other_ratio)
    )
    block = in_order(block, from_x_lo, x_lo == 1, 0)
    other_keys, cache_t, w_key, w_val = stage_other(where, other_t, own_t, kv_up)
    along_z = lambda x, k: permute(x, "ctx", lambda i: (i + 4 * k) % (4 * nz))
    ring = [block] + [None] * (nz - 1)
    ring[nz - 2], ring[2] = along_z(block, 2), along_z(block, -2)
    ring[nz - 1], ring[1] = along_z(block, 1), along_z(block, -1)
    ring[nz - 4] = along_z(ring[nz - 2], 2)
    ring[nz - 3], ring[3] = along_z(ring[nz - 2], 1), along_z(ring[2], -1)

    query, grad, expo, spread, stats = attend(
        where, ring, w_key, w_val, own_keys, other_keys, (token_ratio, other_ratio), scale * LOG2E
    )

    joined = [stats]
    projected = []
    parts = 2
    for group, partners in enumerate(((2, 4, 6), (8, 16, 24))):
        mine = joined[0] if group == 0 else join(*joined)
        joined = [permute(mine, "ctx", lambda i, k=k: i ^ k) for k in partners]
        terms = project(group, parts, cache_t, spread, expo)
        joined = lax.optimization_barrier((*joined, *terms))
        projected += joined[len(partners) :]
        joined = (mine, *joined[: len(partners)])
    with_spread, with_expo, factors = weigh(
        where, pair_lens, joined, stats, query, grad, scale, rows, q_dev
    )
    dq_keep, dq_send = query_terms(where, factors, w_key, projected, nz, q_width)
    dq_pair = permute(dq_send, "ctx", other_x_lo)
    keys = p_dev // (2 * ny)
    shape = (2, 2, ny, keys, spread.shape[1])
    operands = (d_lat, spread.reshape(shape), expo.reshape(shape), with_spread, with_expo)
    adds = []
    sends = cache_terms(1, 0, where, *operands, (BF16, BF16))
    later, *sends = lax.optimization_barrier((where, *sends))
    adds.append([permute(x, "ctx", other_core) for x in sends])
    sends = cache_terms(1, 1, later, *operands, (BF16, BF16))
    adds.append([permute(x, "ctx", other_core) for x in sends])
    to_x_hi = lambda x: permute(x, "head", lambda i: (i + ny) % (2 * ny))
    to_y = lambda x, k: permute(x, "head", lambda i: (i // ny) * ny + (i + k) % ny)
    send, keep = cache_terms(0, 0, where, *operands, (BF16, F32), adds[0])
    later, send = lax.optimization_barrier((where, send))
    from_x_hi = to_x_hi(send)
    send, own = cache_terms(0, 1, later, *operands, (BF16, F32), adds[1])
    dq = (dq_keep.astype(F32) + dq_pair.astype(F32)).astype(BF16)
    send, dq = lax.optimization_barrier((send, dq))
    from_y = to_y(send, 3)

    half_rows = jax.ShapeDtypeStruct((keys // 2, 2 * c_width), BF16)
    block = jax.ShapeDtypeStruct((keys, c_width), F32)
    sends = small(
        functools.partial(forward_kernel, d_lat), (half_rows, half_rows), keep, from_x_hi
    )
    arrived = [to_y(sends[0], 2), to_y(sends[1], 1)]
    send, keep = small(functools.partial(turn_kernel, d_lat), (half_rows, block), own, from_y)
    arrived.append(to_x_hi(send))
    cache_grad = small(
        functools.partial(finish_kernel, d_lat),
        jax.ShapeDtypeStruct((c_width, keys), BF16),
        keep,
        *arrived,
    ).T

    dq = lax.all_to_all(dq, "ctx", 0, 0, axis_index_groups=z_groups)
    dq = jnp.sum(dq.astype(F32), axis=0).astype(BF16).reshape(half, 2, q_dev, q_width)
    theirs = permute(dq[:, 1], "ctx", other_core)
    query_grad = jnp.transpose(in_order(dq[:, 0], theirs, core == 1, 0), (1, 0, 2))

    return (query_grad, cache_grad)


def solution(mesh):
    placed = (
        P("ctx", "head", None),
        P("ctx", "head", None),
        P("head", None, None),
        P("ctx", None),
        P("ctx"),
        P(),
        P(),
    )
    return jax.shard_map(
        per_device,
        mesh=mesh,
        in_specs=placed,
        out_specs=(P("ctx", "head", None), P(("ctx", "head"), None)),
        check_vma=False,
    )
```
